32 devices in a mesh: head: 4 (over z), batch: 4 (over y, core), dp: 2 (over x).
Axes of the slice: x: 2, y: 2, z: 4, core: 2. Of those that a mesh axis runs over, the one named last changes fastest.
Arguments:
- layer_input: bfloat16 [8, 4096, 1024], P(('batch', 'dp'), 'head'), may hold values from -6 to 6
- lengths: int32 [8, 3], P(('batch', 'dp')), may hold values from 1024 to 2048, as said below
- norm1_gain: float32 [1024], replicated, may hold values from 0.5 to 1.5
- qkv_weight: bfloat16 [3, 1024, 1024], P(None, None, 'head'), may hold values from -0.1875 to 0.1875
- kernels: float32 [3, 3, 1024], P(None, None, 'head'), may hold values from -1 to 1
- out_weight: bfloat16 [1024, 1024], P('head'), may hold values from -1.5 to 1.5
- out_bias: float32 [1024], replicated, may hold values from -4 to 4
- norm2_gain: float32 [1024], replicated, may hold values from 0.5 to 1.5
- up_weight: bfloat16 [1024, 4096], P(None, 'head'), may hold values from -0.1875 to 0.1875
- up_bias: float32 [4096], P('head'), may hold values from -6 to 6
- down_weight: bfloat16 [4096, 1024], P('head'), may hold values from -0.09375 to 0.09375
- down_bias: float32 [1024], replicated, may hold values from -6 to 6
- out_grad: bfloat16 [8, 4096, 1024], P(('batch', 'dp'), 'head'), may hold values from -6 to 6
Outputs:
- layer_output: bfloat16 [8, 4096, 1024], P(('batch', 'dp'), 'head')
- layer_input_grad: bfloat16 [8, 4096, 1024], P(('batch', 'dp'), 'head')
- norm1_gain_grad: float32 [1024], replicated
- qkv_weight_grad: float32 [3, 1024, 1024], P(None, None, 'head')
- kernels_grad: float32 [3, 3, 1024], P(None, None, 'head')
- out_weight_grad: float32 [1024, 1024], P('head')
- out_bias_grad: float32 [1024], replicated
- norm2_gain_grad: float32 [1024], replicated
- up_weight_grad: float32 [1024, 4096], P(None, 'head')
- up_bias_grad: float32 [4096], P('head')
- down_weight_grad: float32 [4096, 1024], P('head')
- down_bias_grad: float32 [1024], replicated
The draws below stay inside these ranges and needn't reach their ends.
Inputs may be any that keep to these rules, and one draw needn't show every extreme that they name: Each group's three lengths are two of 1024 and one of 2048, in an order drawn for each group.
All inputs are finite; a program needn't handle non-finite values.
Results may differ from the reference program's by a relative error of at most 0.02.
Values may be sent and summed in bfloat16 or wider, within the bound.
A program may use at most 256 MiB of HBM per device.

```python
import math
import jax
import jax.numpy as jnp
from jax import lax

D = 1024
HEADS = 16
HS = 64
FF = 4096
LONG = 2048
SHORT = 1024
GROUPS = 8


def draw_lengths(key, part):
    key = jax.random.fold_in(key, 11)
    long_slot = jax.random.randint(key, (GROUPS, 1), 0, 3)
    columns = jnp.arange(3, dtype=jnp.int32)[None, :]
    return jnp.where(columns == long_slot, LONG, SHORT).astype(jnp.int32)


def levels(key, extent, pieces, smallest, high):
    def one(axis_at, shards_of):
        draws = jax.random.uniform(jax.random.fold_in(jax.random.fold_in(key, 6), axis_at), (shards_of,), jnp.float32, smallest / len(pieces), high / len(pieces))
        return jnp.repeat(jnp.exp(draws), extent[axis_at] // shards_of).reshape((-1,) + (1,) * (len(extent) - axis_at - 1))

    level = one(*pieces[0])
    for cut in pieces[1:]:
        level = level * one(*cut)
    return level


def normal_values(key, extent, spread, most, pieces=(), kind=jnp.bfloat16):
    drawn = jax.random.normal(key, extent, jnp.float32) * spread
    if len(pieces) > 0:
        drawn = levels(key, extent, pieces, -0.22, 0.18) * drawn
    return jnp.clip(drawn, min=-most, max=most).astype(kind)


def setup_inputs(seed: int = 0) -> dict:
    streams_of = jax.random.split(jax.random.key(seed), 14)
    return {
        "layer_input": normal_values(streams_of[0], (GROUPS, 2 * LONG, D), 1.0, 6.0, ((0, 8), (1, 4))),
        "lengths": draw_lengths(jax.random.fold_in(streams_of[13], 71), 0),
        "norm1_gain": jnp.clip(jax.random.uniform(streams_of[2], (D,), jnp.float32, 0.5, 1.5), 0.5, 1.5),
        "qkv_weight": normal_values(streams_of[3], (3, D, D), D ** -0.5, 0.1875, ((2, 4),)),
        "kernels": jnp.clip(jax.random.uniform(streams_of[4], (3, 3, D), jnp.float32, -1.0, 1.0) * levels(streams_of[4], (3, 3, D), ((2, 4),), -0.4, 0.0), -1.0, 1.0),
        "out_weight": normal_values(streams_of[5], (D, D), (D // 64) ** -0.5, 1.5, ((0, 4),)),
        "out_bias": normal_values(streams_of[6], (D,), 0.3, 4.0, (), jnp.float32),
        "norm2_gain": jnp.clip(jax.random.uniform(streams_of[7], (D,), jnp.float32, 0.5, 1.5), 0.5, 1.5),
        "up_weight": normal_values(streams_of[8], (D, FF), D ** -0.5, 0.1875, ((1, 4),)),
        "up_bias": normal_values(streams_of[9], (FF,), 0.5, 6.0, ((0, 4),), jnp.float32),
        "down_weight": normal_values(streams_of[10], (FF, D), FF ** -0.5, 0.09375, ((0, 4),)),
        "down_bias": normal_values(streams_of[11], (D,), 0.5, 6.0, (), jnp.float32),
        "out_grad": normal_values(streams_of[12], (GROUPS, 2 * LONG, D), 1.0, 6.0, ((0, 8), (1, 4))),
    }


@jax.custom_vjp
def low(v):
    return lax.optimization_barrier(v.astype(jnp.bfloat16)).astype(jnp.float32)

@jax.custom_vjp
def low_back(v):
    return v

def low_keep(v):
    return (low(v), None)

def low_pass(kept, grad):
    return (grad,)

def back_keep(v):
    return (v, None)

def back_low(kept, grad):
    return (low(grad),)
low.defvjp(low_keep, low_pass)
low_back.defvjp(back_keep, back_low)
EPSILON = 1e-06
HIGHEST = lax.Precision.HIGHEST

def matmul(left, right):
    return jnp.dot(left, right, precision=HIGHEST)

def rms_norm(values, gain_vector):
    return values * lax.rsqrt(lax.optimization_barrier(jnp.mean(values * values, axis=-1, keepdims=True)) + EPSILON) * gain_vector

def shifted(values, offset):
    return jnp.concatenate([jnp.zeros((offset, values.shape[1]), values.dtype), values[:-offset]], axis=0)

def depthwise(values, kernel, position):
    one_back = jnp.where(position[:, None] >= 1, shifted(values, 1), 0.0)
    two_back = jnp.where(position[:, None] >= 2, shifted(values, 2), 0.0)
    return kernel[0] * values + kernel[1] * one_back + kernel[2] * two_back

def sequence_layout(seq_lengths, stream_length):
    boundary = jnp.cumsum(seq_lengths).astype(jnp.int32)
    places = jnp.arange(stream_length, dtype=jnp.int32)
    past_end = places[:, None] >= boundary[None, :]
    document = lax.optimization_barrier(jnp.sum(past_end.astype(jnp.int32), axis=1)).astype(jnp.int32)
    begins = lax.optimization_barrier(jnp.max(jnp.where(past_end, boundary[None, :], 0), axis=1)).astype(jnp.int32)
    return (document, places - begins)

def attention(queries, key_rows, values, document):
    stream_length = queries.shape[0]
    block_rows = min(512, stream_length)
    places = jnp.arange(stream_length, dtype=jnp.int32)
    score_scale = 1.0 / math.sqrt(HS)

    def one_block(block_index):
        first_row = (block_index * block_rows).astype(jnp.int32)
        query_block = lax.dynamic_slice_in_dim(queries, first_row, block_rows, 0)
        row_ids = first_row + jnp.arange(block_rows, dtype=jnp.int32)
        query_docs = lax.dynamic_slice_in_dim(document, first_row, block_rows, 0)
        allowed = (places[None, :] <= row_ids[:, None]) & (document[None, :] == query_docs[:, None])
        scores = low_back(jnp.einsum('qhd,khd->hqk', query_block, key_rows, precision=HIGHEST) * score_scale)
        scores = jnp.where(allowed[None], scores, -1e+30)
        row_peak = lax.optimization_barrier(jnp.max(scores, axis=-1, keepdims=True))
        exponent = jnp.exp(scores - row_peak)
        soft_weights = exponent / lax.optimization_barrier(jnp.sum(exponent, axis=-1, keepdims=True))
        return jnp.einsum('hqk,khd->qhd', low(soft_weights), values, precision=HIGHEST)
    block_outs = lax.map(jax.checkpoint(one_block), jnp.arange(stream_length // block_rows, dtype=jnp.int32))
    return block_outs.reshape(stream_length, queries.shape[1] * queries.shape[2])

def group_forward(stream, seq_lengths, params):
    gain_one, qkv_set, kernel_set, proj_out, bias_out, gain_two, proj_up, bias_up, proj_down, bias_down = params
    stream_length = stream.shape[0]
    document, position = sequence_layout(seq_lengths, stream_length)
    normed = low(rms_norm(stream, gain_one))
    conv_outs = []
    for member in range(3):
        linear = low_back(matmul(normed, qkv_set[member]))
        conv_outs.append(low(depthwise(linear, kernel_set[member], position)).reshape(stream_length, HEADS, HS))
    attended = attention(conv_outs[0], conv_outs[1], conv_outs[2], document)
    attended = low_back(low(attended))
    hidden_state = stream + low_back(matmul(attended, proj_out) + bias_out)
    normed_two = low(rms_norm(hidden_state, gain_two))
    gate_value = low_back(matmul(normed_two, proj_up) + bias_up)
    activation = low(jnp.square(jnp.maximum(gate_value, 0.0)))
    return hidden_state + matmul(activation, proj_down) + bias_down

def reference(layer_input, lengths, norm1_gain, qkv_weight, kernels, out_weight, out_bias, norm2_gain, up_weight, up_bias, down_weight, down_bias, out_grad):
    params = tuple((tensor.astype(jnp.float32) for tensor in (norm1_gain, qkv_weight, kernels, out_weight, out_bias, norm2_gain, up_weight, up_bias, down_weight, down_bias)))

    def group_step(totals, inputs):
        stream, seq_lengths, cotangent = inputs

        def forward(values, weights):
            return group_forward(values, seq_lengths, weights)
        result, pullback = jax.vjp(forward, stream.astype(jnp.float32), params)
        stream_grad, weight_grads = pullback(cotangent.astype(jnp.float32))
        totals = jax.tree.map(jnp.add, totals, weight_grads)
        return (totals, (result.astype(jnp.bfloat16), stream_grad.astype(jnp.bfloat16)))
    zero_grads = jax.tree.map(jnp.zeros_like, params)
    totals, (outputs, input_grads) = lax.scan(group_step, zero_grads, (layer_input, lengths, out_grad))
    return (outputs, input_grads, totals[0], totals[1], totals[2], totals[3], totals[4], totals[5], totals[6], totals[7], totals[8], totals[9])
```

```python
import functools, math
import jax, jax.numpy as jnp
from jax import lax
from jax.sharding import PartitionSpec as P
from jax.experimental import pallas as pl
from jax.experimental.pallas import tpu as pltpu

HS = 64
LONG = 2048
LANES = 128
LOG2E = math.log2(math.e)
LN2 = math.log(2.0)
NT = (((1,), (1,)), ((), ()))
NN = (((1,), (0,)), ((), ()))


def dot(a, b, dims=NN):
    return lax.dot_general(a, b, dims, preferred_element_type=jnp.float32)


def spans(first, last, step):
    return [(at, min(step, last - at)) for at in range(first, last, step)]


def forward_kernel(before_ref, q_ref, k_ref, v_ref, out_ref, mass_ref, s0_ref, s1_ref, *, shards, bq, kc):
    rows = q_ref.shape[0]
    own = (shards - 1) * rows
    lane = lax.broadcasted_iota(jnp.int32, (bq, LANES), 1) < HS
    scale = 1.0 / math.sqrt(HS)

    def block(at, first):
        query = q_ref[pl.ds(at, bq), :] * jnp.bfloat16(scale)
        zero = jnp.zeros_like(query)
        queries = (jnp.where(lane, query, zero), jnp.where(lane, zero, query))
        stores = (s0_ref, s1_ref)
        peaks = [None, None]
        parts = spans(first, own + at, kc) + [(own + at, bq)]
        for start, size in parts:
            key = k_ref[pl.ds(start, size), :]
            for h in range(2):
                s = dot(queries[h], key, NT)
                if start == own + at:
                    row = lax.broadcasted_iota(jnp.int32, (bq, size), 0)
                    col = lax.broadcasted_iota(jnp.int32, (bq, size), 1)
                    s = jnp.where(col <= row, s, -1e30)
                stores[h][:, pl.ds(start, size)] = s
                top = jnp.max(s, axis=1, keepdims=True)
                peaks[h] = top if peaks[h] is None else jnp.maximum(peaks[h], top)
        sums = [None, None]
        scaled = [peak * LOG2E for peak in peaks]
        for start, size in parts:
            value = v_ref[pl.ds(start, size), :]
            wide = lax.broadcasted_iota(jnp.int32, (size, LANES), 1) < HS
            one = jnp.ones_like(value)
            values = (jnp.where(wide, value, one), jnp.where(wide, one, value))
            for h in range(2):
                p = jnp.exp2(stores[h][:, pl.ds(start, size)] * LOG2E - scaled[h]).astype(jnp.bfloat16)
                o = dot(p, values[h])
                sums[h] = o if sums[h] is None else sums[h] + o
        total = pltpu.roll(jnp.where(lane, sums[1], sums[0]), HS, 1)
        out_ref[pl.ds(at, bq), :] = (jnp.where(lane, sums[0], sums[1]) / total).astype(out_ref.dtype)
        mass = jnp.where(lane, peaks[0], peaks[1]) + jnp.log(total)
        mass = mass.T
        mass_ref[0, 0:1, pl.ds(at, bq)] = mass[0:1]
        mass_ref[0, 1:2, pl.ds(at, bq)] = mass[HS:HS + 1]

    for before in range(shards):
        @pl.when(before_ref[0] == before)
        def _():
            for at in range(0, rows, bq):
                block(at, own - before * rows)


def attention_forward(before, queries, key_rows, values):
    rows, width = queries.shape
    window = key_rows.shape[0]
    shards = window // rows
    pairs = width // LANES
    bq = min(256, rows)
    column = lambda n: pl.BlockSpec((n, LANES), lambda i, b: (0, i))
    return pl.pallas_call(
        functools.partial(forward_kernel, shards=shards, bq=bq, kc=512),
        out_shape=(jax.ShapeDtypeStruct((rows, width), jnp.bfloat16), jax.ShapeDtypeStruct((pairs, 8, rows), jnp.float32)),
        grid_spec=pltpu.PrefetchScalarGridSpec(
            num_scalar_prefetch=1, grid=(pairs,),
            in_specs=[column(rows), column(window), column(window)],
            out_specs=[column(rows), pl.BlockSpec((1, 8, rows), lambda i, b: (i, 0, 0))],
            scratch_shapes=[pltpu.VMEM((bq, window), jnp.float32)] * 2,
        ),
        compiler_params=pltpu.CompilerParams(vmem_limit_bytes=48 << 20),
    )(before, queries, key_rows, values)


def backward_kernel(before_ref, q_ref, k_ref, v_ref, g_ref, o_ref, mass_ref, dq_ref, dk_ref, dv_ref, kt_ref, *, shards, bq, kc):
    rows = q_ref.shape[0]
    window = k_ref.shape[0]
    own = window - rows
    lane = lax.broadcasted_iota(jnp.int32, (bq, LANES), 1) < HS
    scale = 1.0 / math.sqrt(HS)
    dk_ref[...] = jnp.zeros_like(dk_ref)
    dv_ref[...] = jnp.zeros_like(dv_ref)
    kt_ref[...] = k_ref[...].astype(jnp.float32).T.astype(jnp.bfloat16)

    def block(at, first):
        query = q_ref[pl.ds(at, bq), :] * jnp.bfloat16(scale)
        grad = g_ref[pl.ds(at, bq), :]
        zero = jnp.zeros_like(query)
        queries = (jnp.where(lane, query, zero), jnp.where(lane, zero, query))
        grads = (jnp.where(lane, grad, zero), jnp.where(lane, zero, grad))
        product = (grad.astype(jnp.float32) * o_ref[pl.ds(at, bq), :].astype(jnp.float32)).T
        query_grads = [jnp.zeros((HS, bq), jnp.float32)] * 2
        deltas = [jnp.sum(product[h * HS:(h + 1) * HS], axis=0, keepdims=True) for h in range(2)]
        masses = [mass_ref[0, h:h + 1, pl.ds(at, bq)] * LOG2E for h in range(2)]
        parts = spans(first, own + at, kc) + [(own + at, bq)]
        for start, size in parts:
            key = k_ref[pl.ds(start, size), :]
            value = v_ref[pl.ds(start, size), :]
            key_part = value_part = None
            for h in range(2):
                s = dot(key, queries[h], NT)
                if start == own + at:
                    row = lax.broadcasted_iota(jnp.int32, (size, bq), 1)
                    col = lax.broadcasted_iota(jnp.int32, (size, bq), 0)
                    s = jnp.where(col <= row, s, -1e30)
                p = jnp.exp2(s * LOG2E - masses[h])
                dp = dot(value, grads[h], NT)
                ds = (p * (dp - deltas[h])).astype(jnp.bfloat16)
                a = dot(p.astype(jnp.bfloat16), grads[h])
                b = dot(ds, queries[h])
                value_part = a if value_part is None else value_part + a
                key_part = b if key_part is None else key_part + b
                query_grads[h] += dot(kt_ref[h * HS:(h + 1) * HS, pl.ds(start, size)], ds)
            dk_ref[pl.ds(start, size), :] += key_part
            dv_ref[pl.ds(start, size), :] += value_part
        dq_ref[pl.ds(at, bq), :] = jnp.concatenate(query_grads, axis=0).T * scale

    for before in range(shards):
        @pl.when(before_ref[0] == before)
        def _():
            for at in range(0, rows, bq):
                block(at, own - before * rows)


def attention_backward(before, queries, key_rows, values, grads, outs, mass):
    rows, width = queries.shape
    window = key_rows.shape[0]
    shards = window // rows
    pairs = width // LANES
    bq = min(256, rows)
    column = lambda n: pl.BlockSpec((n, LANES), lambda i, b: (0, i))
    return pl.pallas_call(
        functools.partial(backward_kernel, shards=shards, bq=bq, kc=256),
        out_shape=(jax.ShapeDtypeStruct((rows, width), jnp.float32), jax.ShapeDtypeStruct((window, width), jnp.float32), jax.ShapeDtypeStruct((window, width), jnp.float32)),
        grid_spec=pltpu.PrefetchScalarGridSpec(
            num_scalar_prefetch=1, grid=(pairs,),
            in_specs=[column(rows), column(window), column(window), column(rows), column(rows), pl.BlockSpec((1, 8, rows), lambda i, b: (i, 0, 0))],
            out_specs=[column(rows), column(window), column(window)],
            scratch_shapes=[pltpu.VMEM((LANES, window), jnp.bfloat16)],
        ),
        compiler_params=pltpu.CompilerParams(vmem_limit_bytes=48 << 20),
    )(before, queries, key_rows, values, grads, outs, mass)

EPSILON = 1e-06
ALL = ("head", "batch", "dp")


def factor_of(values):
    return lax.rsqrt(jnp.mean(values * values, axis=-1, keepdims=True) + EPSILON)


def norm_backward(values, gain, upstream):
    factor = factor_of(values)
    unit = values * factor
    scaled = gain * upstream
    result = factor * (scaled - unit * jnp.mean(scaled * unit, axis=-1, keepdims=True))
    return result, upstream * unit


def back(values, offset):
    if offset == 0:
        return values
    return jnp.pad(values[:-offset], ((offset, 0), (0, 0)))


def ahead(values, offset):
    if offset == 0:
        return values
    return jnp.pad(values[offset:], ((0, offset), (0, 0)))


def nt(a, b):
    return lax.dot_general(a, b, NT, preferred_element_type=jnp.float32)


def nn(a, b):
    return lax.dot_general(a, b, NN, preferred_element_type=jnp.float32)


def tn(a, b):
    return lax.dot_general(a, b, (((0,), (0,)), ((), ())), preferred_element_type=jnp.float32)


def on_device(
    layer_input, lengths, norm1_gain, qkv_weight, kernels, out_weight, out_bias,
    norm2_gain, up_weight, up_bias, down_weight, down_bias, out_grad,
):
    rows = layer_input.shape[1]
    parts = lax.axis_size("head")
    copies = lax.axis_size("batch") * lax.axis_size("dp")
    shards = max(1, LONG // rows)
    place = lax.axis_index("head")
    mine = lax.axis_index("batch") * lax.axis_size("dp") + lax.axis_index("dp")
    width = qkv_weight.shape[1]

    first_row = place * rows
    ends = jnp.cumsum(lengths[0])
    begins = jnp.max(jnp.where(ends <= first_row, ends, 0))
    before = ((first_row - begins) // rows).astype(jnp.int32)

    def gathered(weight):
        share = weight.shape[-2] // copies
        piece = lax.dynamic_slice_in_dim(weight, mine * share, share, weight.ndim - 2)
        return lax.all_gather(piece, ALL, axis=weight.ndim - 2, tiled=True)

    def reduced(grad):
        axis = grad.ndim - 2
        piece = lax.psum_scatter(grad.astype(jnp.bfloat16), ALL, scatter_dimension=axis, tiled=True)
        return lax.all_gather(piece, ("batch", "dp"), axis=axis, tiled=True).astype(jnp.float32)

    qkv_rows = gathered(qkv_weight.transpose(0, 2, 1))
    out_rows = gathered(out_weight)
    up_rows = gathered(up_weight.T)
    down_rows = gathered(down_weight)
    kernel_all = lax.all_gather(kernels, "head", axis=2, tiled=True)
    up_bias_all = lax.all_gather(up_bias, "head", axis=0, tiled=True)

    own_float = layer_input[0].astype(jnp.float32)
    cotangent = out_grad[0]
    own_factor = factor_of(own_float)
    normed_own = (own_float * own_factor * norm1_gain).astype(jnp.bfloat16)
    pieces = [normed_own]
    for hop in range(1, shards):
        came = lax.ppermute(normed_own, "head", [(i, i + hop) for i in range(parts - hop)])
        pieces.insert(0, jnp.where(before >= hop, came, jnp.zeros_like(came)))
    window = jnp.concatenate(pieces, axis=0)
    window_rows = shards * rows
    edge = 16 if shards > 1 else 0
    late = window[window_rows - rows - edge:]

    linear = [nt(late, qkv_rows[0]).astype(jnp.bfloat16)] + [nt(window, qkv_rows[j]).astype(jnp.bfloat16) for j in (1, 2)]

    def convolve(j):
        values = linear[j].astype(jnp.float32)
        return sum(kernel_all[j, i] * back(values, i) for i in range(3)).astype(jnp.bfloat16)

    queries, key_rows, values = convolve(0)[edge:], convolve(1), convolve(2)
    attended, mass = attention_forward(before[None], queries, key_rows, values)
    hidden = own_float + nn(attended, out_rows) + out_bias
    normed_two = (hidden * factor_of(hidden) * norm2_gain).astype(jnp.bfloat16)
    gate = jnp.maximum(nt(normed_two, up_rows) + up_bias_all, 0.0)
    activation = jnp.square(gate).astype(jnp.bfloat16)
    gate_low = gate.astype(jnp.bfloat16)
    layer_output = (hidden + nn(activation, down_rows) + down_bias).astype(jnp.bfloat16)

    gate_grad = (2.0 * gate_low.astype(jnp.float32) * nt(cotangent, down_rows)).astype(jnp.bfloat16)
    down_grad = reduced(tn(activation, cotangent))
    up_grad = reduced(tn(gate_grad, normed_two)).T
    down_bias_grad = jnp.sum(cotangent.astype(jnp.float32), axis=0)
    up_bias_grad = jnp.sum(gate_grad.astype(jnp.float32), axis=0)
    normed_two_grad = nn(gate_grad, up_rows)
    back_two, gain_rows = norm_backward(hidden, norm2_gain, normed_two_grad)
    hidden_grad = cotangent.astype(jnp.float32) + back_two
    hidden_low = hidden_grad.astype(jnp.bfloat16)
    gain_two_grad = jnp.sum(gain_rows, axis=0)
    out_bias_grad = jnp.sum(hidden_low.astype(jnp.float32), axis=0)
    out_weight_grad = reduced(tn(attended, hidden_low))
    attended_grad = nt(hidden_low, out_rows).astype(jnp.bfloat16)

    conv_grad = attention_backward(before[None], queries, key_rows, values, attended_grad, attended, mass)
    conv_grad = [jnp.pad(conv_grad[0], ((edge, 0), (0, 0)))] + list(conv_grad[1:])
    kernels_grad = jnp.stack([
        jnp.stack([jnp.sum(conv_grad[j] * back(linear[j].astype(jnp.float32), i), axis=0) for i in range(3)])
        for j in range(3)
    ])
    linear_grad = [
        sum(kernel_all[j, i] * ahead(conv_grad[j], i) for i in range(3)).astype(jnp.bfloat16) for j in range(3)
    ]
    inputs = (late, window, window)
    qkv_grad = reduced(jnp.stack([tn(linear_grad[j], inputs[j]) for j in range(3)])).transpose(0, 2, 1)
    normed_grad = nn(linear_grad[1], qkv_rows[1]) + nn(linear_grad[2], qkv_rows[2])
    query_part = nn(linear_grad[0], qkv_rows[0])
    normed_grad = normed_grad + jnp.pad(query_part, ((window_rows - rows - edge, 0), (0, 0)))
    normed_own_grad = normed_grad[window_rows - rows:]
    for hop in range(1, shards):
        at = window_rows - (hop + 1) * rows
        part = normed_grad[at:at + rows].astype(jnp.bfloat16)
        part = jnp.where(before >= hop, part, jnp.zeros_like(part))
        came = lax.ppermute(part, "head", [(i + hop, i) for i in range(parts - hop)])
        normed_own_grad = normed_own_grad + came.astype(jnp.float32)
    back_one, gain_rows_one = norm_backward(own_float, norm1_gain, normed_own_grad)
    layer_grad = (hidden_grad + back_one).astype(jnp.bfloat16)
    gain_one_grad = jnp.sum(gain_rows_one, axis=0)

    gain_one_grad, gain_two_grad, out_bias_grad, down_bias_grad, up_bias_grad, kernels_grad = lax.psum(
        (gain_one_grad, gain_two_grad, out_bias_grad, down_bias_grad, up_bias_grad, kernels_grad), ALL
    )
    up_bias_grad = lax.dynamic_slice_in_dim(up_bias_grad, place * up_bias.shape[0], up_bias.shape[0], 0)
    kernels_grad = lax.dynamic_slice_in_dim(kernels_grad, place * kernels.shape[2], kernels.shape[2], 2)
    return (
        layer_output[None], layer_grad[None], gain_one_grad, qkv_grad, kernels_grad, out_weight_grad,
        out_bias_grad, gain_two_grad, up_grad, up_bias_grad, down_grad, down_bias_grad,
    )


def solution(mesh):
    rows = P(("batch", "dp"), "head", None)
    return jax.shard_map(
        on_device,
        mesh=mesh,
        in_specs=(
            rows, P(("batch", "dp"), None), P(), P(None, None, "head"), P(None, None, "head"), P("head", None), P(),
            P(), P(None, "head"), P("head"), P("head", None), P(), rows,
        ),
        out_specs=(
            rows, rows, P(), P(None, None, "head"), P(None, None, "head"), P("head", None),
            P(), P(), P(None, "head"), P("head"), P("head", None), P(),
        ),
        check_vma=False,
    )
```

```python
import functools
import math

import jax
import jax.numpy as jnp
from jax import lax
from jax.experimental import pallas as pl
from jax.experimental.pallas import tpu as pltpu
from jax.sharding import PartitionSpec as P

LONG = 2048
EPSILON = 1e-06
ALL = ("head", "batch", "dp")

HS = 64
LANES = 128
EDGE = 16
LOG2E = math.log2(math.e)
NT = (((1,), (1,)), ((), ()))
NN = (((1,), (0,)), ((), ()))
TN = (((0,), (0,)), ((), ()))


def dot(a, b, dims=NN):
    return lax.dot_general(a, b, dims, preferred_element_type=jnp.float32)


def spans(first, last, step):
    return [(at, min(step, last - at)) for at in range(first, last, step)]


def earlier(ref, start, size):
    if start == 0:
        rows = jnp.concatenate([jnp.zeros((EDGE, LANES), jnp.float32), ref[pl.ds(0, size), :].astype(jnp.float32)], axis=0)
    else:
        rows = ref[pl.ds(start - EDGE, size + EDGE), :].astype(jnp.float32)
    return [pltpu.roll(rows, i, 0)[EDGE:] if i else rows[EDGE:] for i in range(3)]


def convolve(linear_ref, kern_ref, member, target_ref, skip, step=256):
    total = linear_ref.shape[0]
    for start, size in spans(skip, total, step):
        taps = earlier(linear_ref, start, size)
        value = sum(kern_ref[3 * member + i:3 * member + i + 1, :] * taps[i] for i in range(3))
        target_ref[pl.ds(start - skip, size), :] = value.astype(jnp.bfloat16)


def convolve_back(grad_ref, linear_ref, kern_ref, member, target_ref, sums_ref, step=256):
    total = linear_ref.shape[0]
    parts = [jnp.zeros((8, LANES), jnp.float32)] * 3
    for start, size in spans(0, total, step):
        rows = grad_ref[pl.ds(start, size + 8), :]
        value = kern_ref[3 * member:3 * member + 1, :] * rows[:size]
        for i in (1, 2):
            value += kern_ref[3 * member + i:3 * member + i + 1, :] * pltpu.roll(rows, size + 8 - i, 0)[:size]
        target_ref[pl.ds(start, size), :] = value.astype(jnp.bfloat16)
        taps = earlier(linear_ref, start, size)
        for i in range(3):
            parts[i] += jnp.sum((rows[:size] * taps[i]).reshape(size // 8, 8, LANES), axis=0)
    for i in range(3):
        sums_ref[3 * member + i:3 * member + i + 1, :] = jnp.sum(parts[i], axis=0, keepdims=True)


def forward_kernel(
    before_ref, lq_ref, lk_ref, lv_ref, kern_ref, out_ref, mass_ref, q_ref, k_ref, v_ref, s0_ref, s1_ref, *, shards, bq, kc,
):
    rows = q_ref.shape[0]
    own = (shards - 1) * rows
    lane = lax.broadcasted_iota(jnp.int32, (bq, LANES), 1) < HS
    scale = 1.0 / math.sqrt(HS)
    convolve(lq_ref, kern_ref, 0, q_ref, lq_ref.shape[0] - rows)
    convolve(lk_ref, kern_ref, 1, k_ref, 0)
    convolve(lv_ref, kern_ref, 2, v_ref, 0)

    def block(at, first):
        query = q_ref[pl.ds(at, bq), :] * jnp.bfloat16(scale)
        zero = jnp.zeros_like(query)
        queries = (jnp.where(lane, query, zero), jnp.where(lane, zero, query))
        stores = (s0_ref, s1_ref)
        peaks = [None, None]
        parts = spans(first, own + at, kc) + [(own + at, bq)]
        for start, size in parts:
            key = k_ref[pl.ds(start, size), :]
            for h in range(2):
                s = dot(queries[h], key, NT)
                if start == own + at:
                    row = lax.broadcasted_iota(jnp.int32, (bq, size), 0)
                    col = lax.broadcasted_iota(jnp.int32, (bq, size), 1)
                    s = jnp.where(col <= row, s, -1e30)
                stores[h][:, pl.ds(start, size)] = s
                top = jnp.max(s, axis=1, keepdims=True)
                peaks[h] = top if peaks[h] is None else jnp.maximum(peaks[h], top)
        sums = [None, None]
        scaled = [peak * LOG2E for peak in peaks]
        for start, size in parts:
            value = v_ref[pl.ds(start, size), :]
            wide = lax.broadcasted_iota(jnp.int32, (size, LANES), 1) < HS
            one = jnp.ones_like(value)
            values = (jnp.where(wide, value, one), jnp.where(wide, one, value))
            for h in range(2):
                p = jnp.exp2(stores[h][:, pl.ds(start, size)] * LOG2E - scaled[h]).astype(jnp.bfloat16)
                o = dot(p, values[h])
                sums[h] = o if sums[h] is None else sums[h] + o
        total = pltpu.roll(jnp.where(lane, sums[1], sums[0]), HS, 1)
        out_ref[pl.ds(at, bq), :] = (jnp.where(lane, sums[0], sums[1]) / total).astype(out_ref.dtype)
        mass = jnp.where(lane, peaks[0], peaks[1]) + jnp.log(total)
        mass = mass.T
        mass_ref[0, 0:1, pl.ds(at, bq)] = mass[0:1]
        mass_ref[0, 1:2, pl.ds(at, bq)] = mass[HS:HS + 1]

    for before in range(shards):
        @pl.when(before_ref[0] == before)
        def _():
            for at in range(0, rows, bq):
                block(at, own - before * rows)


def column(n):
    return pl.BlockSpec((n, LANES), lambda i, b: (0, i))


def attention_forward(before, late, linear_k, linear_v, kern, rows):
    edged, width = late.shape
    window = linear_k.shape[0]
    shards = window // rows
    pairs = width // LANES
    bq = min(256, rows)
    return pl.pallas_call(
        functools.partial(forward_kernel, shards=shards, bq=bq, kc=512),
        out_shape=(jax.ShapeDtypeStruct((rows, width), jnp.bfloat16), jax.ShapeDtypeStruct((pairs, 8, rows), jnp.float32)),
        grid_spec=pltpu.PrefetchScalarGridSpec(
            num_scalar_prefetch=1, grid=(pairs,),
            in_specs=[column(edged), column(window), column(window), column(16)],
            out_specs=[column(rows), pl.BlockSpec((1, 8, rows), lambda i, b: (i, 0, 0))],
            scratch_shapes=[
                pltpu.VMEM((rows, LANES), jnp.bfloat16), pltpu.VMEM((window, LANES), jnp.bfloat16),
                pltpu.VMEM((window, LANES), jnp.bfloat16),
                pltpu.VMEM((bq, window), jnp.float32), pltpu.VMEM((bq, window), jnp.float32),
            ],
        ),
        compiler_params=pltpu.CompilerParams(vmem_limit_bytes=48 << 20),
    )(before, late, linear_k, linear_v, kern)


def backward_kernel(
    before_ref, lq_ref, lk_ref, lv_ref, kern_ref, g_ref, o_ref, mass_ref, gq_ref, gk_ref, gv_ref, sums_ref,
    q_ref, k_ref, v_ref, kt_ref, dq_ref, dk_ref, dv_ref, *, shards, bq, kc,
):
    rows = q_ref.shape[0]
    window = k_ref.shape[0]
    own = window - rows
    edge = lq_ref.shape[0] - rows
    lane = lax.broadcasted_iota(jnp.int32, (bq, LANES), 1) < HS
    scale = 1.0 / math.sqrt(HS)
    convolve(lq_ref, kern_ref, 0, q_ref, edge)
    convolve(lk_ref, kern_ref, 1, k_ref, 0)
    convolve(lv_ref, kern_ref, 2, v_ref, 0)
    dk_ref[...] = jnp.zeros_like(dk_ref)
    dv_ref[...] = jnp.zeros_like(dv_ref)
    if edge:
        dq_ref[pl.ds(0, edge), :] = jnp.zeros((edge, LANES), jnp.float32)
    dq_ref[pl.ds(edge + rows, 8), :] = jnp.zeros((8, LANES), jnp.float32)
    kt_ref[...] = k_ref[...].astype(jnp.float32).T.astype(jnp.bfloat16)

    def block(at, first):
        query = q_ref[pl.ds(at, bq), :] * jnp.bfloat16(scale)
        grad = g_ref[pl.ds(at, bq), :]
        zero = jnp.zeros_like(query)
        queries = (jnp.where(lane, query, zero), jnp.where(lane, zero, query))
        grads = (jnp.where(lane, grad, zero), jnp.where(lane, zero, grad))
        product = (grad.astype(jnp.float32) * o_ref[pl.ds(at, bq), :].astype(jnp.float32)).T
        query_grads = [jnp.zeros((HS, bq), jnp.float32)] * 2
        deltas = [jnp.sum(product[h * HS:(h + 1) * HS], axis=0, keepdims=True) for h in range(2)]
        masses = [mass_ref[0, h:h + 1, pl.ds(at, bq)] * LOG2E for h in range(2)]
        parts = spans(first, own + at, kc) + [(own + at, bq)]
        for start, size in parts:
            key = k_ref[pl.ds(start, size), :]
            value = v_ref[pl.ds(start, size), :]
            key_part = value_part = None
            for h in range(2):
                s = dot(key, queries[h], NT)
                if start == own + at:
                    row = lax.broadcasted_iota(jnp.int32, (size, bq), 1)
                    col = lax.broadcasted_iota(jnp.int32, (size, bq), 0)
                    s = jnp.where(col <= row, s, -1e30)
                p = jnp.exp2(s * LOG2E - masses[h])
                dp = dot(value, grads[h], NT)
                ds = (p * (dp - deltas[h])).astype(jnp.bfloat16)
                a = dot(p.astype(jnp.bfloat16), grads[h])
                b = dot(ds, queries[h])
                value_part = a if value_part is None else value_part + a
                key_part = b if key_part is None else key_part + b
                query_grads[h] += dot(kt_ref[h * HS:(h + 1) * HS, pl.ds(start, size)], ds)
            dk_ref[pl.ds(start, size), :] += key_part
            dv_ref[pl.ds(start, size), :] += value_part
        dq_ref[pl.ds(edge + at, bq), :] = jnp.concatenate(query_grads, axis=0).T * scale

    for before in range(shards):
        @pl.when(before_ref[0] == before)
        def _():
            for at in range(0, rows, bq):
                block(at, own - before * rows)

    sums_ref[...] = jnp.zeros_like(sums_ref)
    convolve_back(dq_ref, lq_ref, kern_ref, 0, gq_ref, sums_ref)
    convolve_back(dk_ref, lk_ref, kern_ref, 1, gk_ref, sums_ref)
    convolve_back(dv_ref, lv_ref, kern_ref, 2, gv_ref, sums_ref)


def attention_backward(before, late, linear_k, linear_v, kern, grads, outs, mass):
    rows = grads.shape[0]
    edged, width = late.shape
    window = linear_k.shape[0]
    shards = window // rows
    pairs = width // LANES
    bq = min(256, rows)
    bf = jnp.bfloat16
    return pl.pallas_call(
        functools.partial(backward_kernel, shards=shards, bq=bq, kc=256),
        out_shape=(jax.ShapeDtypeStruct((edged, width), bf), jax.ShapeDtypeStruct((window, width), bf),
                   jax.ShapeDtypeStruct((window, width), bf), jax.ShapeDtypeStruct((16, width), jnp.float32)),
        grid_spec=pltpu.PrefetchScalarGridSpec(
            num_scalar_prefetch=1, grid=(pairs,),
            in_specs=[column(edged), column(window), column(window), column(16), column(rows), column(rows),
                      pl.BlockSpec((1, 8, rows), lambda i, b: (i, 0, 0))],
            out_specs=[column(edged), column(window), column(window), column(16)],
            scratch_shapes=[
                pltpu.VMEM((rows, LANES), bf), pltpu.VMEM((window, LANES), bf), pltpu.VMEM((window, LANES), bf),
                pltpu.VMEM((LANES, window), bf), pltpu.VMEM((edged + 8, LANES), jnp.float32),
                pltpu.VMEM((window + 8, LANES), jnp.float32), pltpu.VMEM((window + 8, LANES), jnp.float32),
            ],
        ),
        compiler_params=pltpu.CompilerParams(vmem_limit_bytes=48 << 20),
    )(before, late, linear_k, linear_v, kern, grads, outs, mass)


MESH = pl.DeviceIdType.MESH


class Copies:
    def __init__(self, send_sems, recv_sems):
        self.send_sems, self.recv_sems, self.all = send_sems, recv_sems, []

    def start(self, source, target, device):
        n = len(self.all)
        copy = pltpu.make_async_remote_copy(
            src_ref=source, dst_ref=target, send_sem=self.send_sems.at[n], recv_sem=self.recv_sems.at[n],
            device_id=device, device_id_type=MESH,
        )
        copy.start()
        self.all.append(copy)
        return copy

    def finish(self):
        for copy in self.all:
            copy.wait_send()


class Place:
    def __init__(self, nz, ny, nx):
        self.nz, self.ny, self.nx = nz, ny, nx
        self.z, batch, self.x = lax.axis_index("head"), lax.axis_index("batch"), lax.axis_index("dp")
        self.y, self.c = batch // 2, batch % 2

    def along_z(self, step):
        return {"head": (self.z + step) % self.nz}

    def along_y(self, step):
        return {"batch": (self.y + step) % self.ny * 2 + self.c}

    def along_x(self, step):
        return {"dp": (self.x + step) % self.nx}

    def other_core(self):
        return {"batch": self.y * 2 + 1 - self.c}

    def meet(self, z_steps):
        partners = [self.along_z(s) for s in z_steps]
        partners += [self.along_y(s) for s in range(1, self.ny)] + [self.along_x(s) for s in range(1, self.nx)]
        partners.append(self.other_core())
        barrier = pltpu.get_barrier_semaphore()
        for partner in partners:
            pl.semaphore_signal(barrier, inc=1, device_id=partner, device_id_type=MESH)
        pl.semaphore_wait(barrier, len(partners))


def spread(place, copies, spot, members):
    ny, nx, y, c, x = place.ny, place.nx, place.y, place.c, place.x
    half = members // 2
    own = spot(y, c, x, 0, members)
    over_x = [copies.start(own, own, place.along_x(s)) for s in range(1, nx)]
    over_y = [copies.start(own, own, place.along_y(s)) for s in range(1, ny)]
    yield
    corner = []
    for s, copy in enumerate(over_x, 1):
        copy.wait_recv()
        part = spot(y, c, (x - s) % nx, 0, half)
        corner += [copies.start(part, part, place.along_y(t)) for t in range(1, ny)]
    for t, copy in enumerate(over_y, 1):
        copy.wait_recv()
        part = spot((y - t) % ny, c, x, half, members)
        corner += [copies.start(part, part, place.along_x(s)) for s in range(1, nx)]
    yield
    for copy in corner:
        copy.wait_recv()
    cores = []
    for row in range(ny):
        part = spot(row, c, None, 0, members)
        cores.append(copies.start(part, part, place.other_core()))
    yield
    for copy in cores:
        copy.wait_recv()


def run_staggered(makers):
    live = []
    makers = list(makers)
    while makers or live:
        if makers:
            live.append(makers.pop(0)())
        for task in list(live):
            try:
                next(task)
            except StopIteration:
                live.remove(task)


def gather_kernel(nz, ny, nx, shard_ref, full_ref, send_sems, recv_sems):
    place = Place(nz, ny, nx)
    copies = Copies(send_sems, recv_sems)
    height, width = shard_ref.shape[1], shard_ref.shape[2]
    rows = height // (ny * 2 * nx)
    z = place.z

    def spot_of(block):
        def spot(y, c, x, lo, hi):
            first = (y * 2 + c) * nx * rows
            size = nx * rows
            if x is not None:
                first, size = first + x * rows, rows
            return full_ref.at[lo:hi, pl.ds(pl.multiple_of(first, rows), size), pl.ds(pl.multiple_of(block * width, width), width)]
        return spot

    place.meet((1, nz - 1) if nz > 2 else (1,))
    own = ((place.y * 2 + place.c) * nx + place.x) * rows
    mine = shard_ref.at[:, pl.ds(pl.multiple_of(own, rows), rows), :]
    rings = [copies.start(mine, spot_of(z)(place.y, place.c, place.x, 0, shard_ref.shape[0]), place.along_z(1))]
    for m in range(shard_ref.shape[0]):
        full_ref[m, :, pl.ds(pl.multiple_of(z * width, width), width)] = shard_ref[m]

    def arrival(step):
        def task():
            rings[step].wait_recv()
            spot = spot_of((z - 1 - step) % nz)
            if step < nz - 2:
                part = spot(place.y, place.c, place.x, 0, shard_ref.shape[0])
                rings.append(copies.start(part, part, place.along_z(1)))
            yield from spread(place, copies, spot, shard_ref.shape[0])
        return task

    run_staggered(arrival(step) for step in range(nz - 1))
    copies.finish()


def gather(shard, nz, ny, nx):
    members, height, width = shard.shape
    per_step = (nx - 1) + (ny - 1) + 2 * (nx - 1) * (ny - 1) + ny
    count = (nz - 1) * (1 + per_step)
    return pl.pallas_call(
        functools.partial(gather_kernel, nz, ny, nx),
        out_shape=jax.ShapeDtypeStruct((members, height, width * nz), shard.dtype),
        in_specs=[pl.BlockSpec(memory_space=pltpu.VMEM)],
        out_specs=pl.BlockSpec(memory_space=pltpu.VMEM),
        scratch_shapes=[pltpu.SemaphoreType.DMA((count,)), pltpu.SemaphoreType.DMA((count,))],
        compiler_params=pltpu.CompilerParams(collective_id=0, has_side_effects=True, vmem_limit_bytes=48 << 20),
        cost_estimate=pl.CostEstimate(flops=0, bytes_accessed=2 * members * height * width * nz * 2, transcendentals=0),
    )(shard)


def reduce_kernel(
    nz, ny, nx, grad_ref, small_ref, out_ref, small_out_ref,
    core_buf, y1_buf, x1_buf, x2_buf, y2_buf, z_send, z_buf, s_acc, s_buf, send_sems, recv_sems,
):
    place = Place(nz, ny, nx)
    copies = Copies(send_sems, recv_sems)
    members, height, width = grad_ref.shape[1:]
    half = members // 2
    rows = height // (ny * 2 * nx)
    band = nx * rows
    y, c, x, z = place.y, place.c, place.x, place.z
    f32, bf = jnp.float32, jnp.bfloat16
    place.meet(range(1, nz))

    def bands(row, core):
        return pl.ds(pl.multiple_of((row * 2 + core) * band, band), band)

    def xrows(at):
        return pl.ds(pl.multiple_of(at * rows, rows), rows)

    def chunk(t):
        block = (z + 1 + t) % nz

        def task():
            sent = [
                copies.start(grad_ref.at[block, :, bands(row, 1 - c), :], core_buf.at[t, row], place.other_core())
                for row in range(ny)
            ]
            yield
            for row, copy in enumerate(sent):
                copy.wait_recv()
                for m in range(members):
                    total = core_buf[t, row, m].astype(f32) + grad_ref[block, m, bands(row, c), :].astype(f32)
                    core_buf[t, row, m] = total.astype(bf)
            over_y = [
                copies.start(core_buf.at[t, (y + s) % ny, 0:half], y1_buf.at[t, s - 1], place.along_y(s))
                for s in range(1, ny)
            ]
            over_x = [
                copies.start(core_buf.at[t, :, half:, xrows((x + s) % nx), :], x1_buf.at[t, s - 1], place.along_x(s))
                for s in range(1, nx)
            ]
            yield
            for copy in over_y:
                copy.wait_recv()
            for m in range(half):
                total = core_buf[t, y, m].astype(f32)
                for s in range(ny - 1):
                    total = total + y1_buf[t, s, m].astype(f32)
                core_buf[t, y, m] = total.astype(bf)
            last = [
                copies.start(core_buf.at[t, y, 0:half, xrows((x + s) % nx), :], x2_buf.at[t, s - 1], place.along_x(s))
                for s in range(1, nx)
            ]
            for copy in over_x:
                copy.wait_recv()
            for row in range(ny):
                for m in range(half):
                    total = core_buf[t, row, half + m, xrows(x), :].astype(f32)
                    for s in range(nx - 1):
                        total = total + x1_buf[t, s, row, m].astype(f32)
                    core_buf[t, row, half + m, xrows(x), :] = total.astype(bf)
            last += [
                copies.start(core_buf.at[t, (y + s) % ny, half:, xrows(x), :], y2_buf.at[t, s - 1], place.along_y(s))
                for s in range(1, ny)
            ]
            yield
            for copy in last:
                copy.wait_recv()
            for m in range(members):
                total = core_buf[t, y, m, xrows(x), :].astype(f32)
                buf, n = (x2_buf, nx - 1) if m < half else (y2_buf, ny - 1)
                for s in range(n):
                    total = total + buf[t, s, m % half].astype(f32)
                z_send[t, m] = total.astype(bf)
            if t < nz - 1:
                sums.append(copies.start(z_send.at[t], z_buf.at[t], place.along_z(1 + t)))
        return task

    def small():
        s_acc[0] = small_ref[...]
        stages = ([place.other_core()], [place.along_x(s) for s in range(1, nx)],
                  [place.along_y(s) for s in range(1, ny)], [place.along_z(s) for s in range(1, nz)])
        used = 0
        for k, partners in enumerate(stages):
            sent = [copies.start(s_acc.at[k], s_buf.at[used + i], partner) for i, partner in enumerate(partners)]
            yield
            total = s_acc[k]
            for i, copy in enumerate(sent):
                copy.wait_recv()
                total = total + s_buf[used + i]
            used += len(sent)
            if k < 3:
                s_acc[k + 1] = total
            else:
                small_out_ref[...] = total

    sums = []
    run_staggered([chunk(0), small] + [chunk(t) for t in range(1, nz)])
    for copy in sums:
        copy.wait_recv()

    def spot(y_at, c_at, x_at, lo, hi):
        first, size = (y_at * 2 + c_at) * band, band
        if x_at is not None:
            first, size = first + x_at * rows, rows
        return out_ref.at[lo:hi, pl.ds(pl.multiple_of(first, rows), size), :]

    own = pl.ds(pl.multiple_of(((y * 2 + c) * nx + x) * rows, rows), rows)
    for m in range(members):
        total = z_send[nz - 1, m].astype(f32)
        for t in range(nz - 1):
            total = total + z_buf[t, m].astype(f32)
        out_ref[m, own, :] = total.astype(bf)
    for _ in spread(place, copies, spot, members):
        pass
    copies.finish()


def reduce(grad, small, ny, nx, collective_id):
    nz, members, height, width = grad.shape
    half = members // 2
    rows = height // (ny * 2 * nx)
    band = nx * rows
    bf = jnp.bfloat16
    per_chunk = ny + 2 * (ny - 1) + 2 * (nx - 1)
    spread_count = (nx - 1) + (ny - 1) + 2 * (nx - 1) * (ny - 1) + ny
    small_count = 1 + (nx - 1) + (ny - 1) + (nz - 1)
    count = nz * per_chunk + (nz - 1) + spread_count + small_count
    vmem = pl.BlockSpec(memory_space=pltpu.VMEM)
    return pl.pallas_call(
        functools.partial(reduce_kernel, nz, ny, nx),
        out_shape=(jax.ShapeDtypeStruct((members, height, width), bf), jax.ShapeDtypeStruct(small.shape, jnp.float32)),
        in_specs=[vmem, vmem],
        out_specs=(vmem, vmem),
        scratch_shapes=[
            pltpu.VMEM((nz, ny, members, band, width), bf),
            pltpu.VMEM((nz, ny - 1, half, band, width), bf),
            pltpu.VMEM((nz, nx - 1, ny, half, rows, width), bf),
            pltpu.VMEM((nz, nx - 1, half, rows, width), bf),
            pltpu.VMEM((nz, ny - 1, half, rows, width), bf),
            pltpu.VMEM((nz, members, rows, width), bf),
            pltpu.VMEM((nz - 1, members, rows, width), bf),
            pltpu.VMEM((4,) + small.shape, jnp.float32),
            pltpu.VMEM((small_count,) + small.shape, jnp.float32),
            pltpu.SemaphoreType.DMA((count,)),
            pltpu.SemaphoreType.DMA((count,)),
        ],
        compiler_params=pltpu.CompilerParams(collective_id=collective_id, has_side_effects=True, vmem_limit_bytes=56 << 20),
        cost_estimate=pl.CostEstimate(flops=0, bytes_accessed=grad.size * 2, transcendentals=0),
    )(grad, small)


def factor_of(values):
    return lax.rsqrt(jnp.mean(values * values, axis=-1, keepdims=True) + EPSILON)


def norm_backward(values, gain, upstream):
    factor = factor_of(values)
    unit = values * factor
    scaled = gain * upstream
    result = factor * (scaled - unit * jnp.mean(scaled * unit, axis=-1, keepdims=True))
    return result, upstream * unit


def on_device(
    layer_input, lengths, norm1_gain, qkv_weight, kernels, out_weight, out_bias,
    norm2_gain, up_weight, up_bias, down_weight, down_bias, out_grad,
):
    rows = layer_input.shape[1]
    nz, nb, nx = lax.axis_size("head"), lax.axis_size("batch"), lax.axis_size("dp")
    ny, copies = nb // 2, nb * nx
    shards = max(1, LONG // rows)
    place = lax.axis_index("head")
    mine = lax.axis_index("batch") * nx + lax.axis_index("dp")
    width = qkv_weight.shape[2]
    hidden_units = up_weight.shape[1]

    first_row = place * rows
    ends = jnp.cumsum(lengths[0])
    begins = jnp.max(jnp.where(ends <= first_row, ends, 0))
    before = ((first_row - begins) // rows).astype(jnp.int32)

    own_float = layer_input[0].astype(jnp.float32)
    cotangent = out_grad[0]
    normed_own = (own_float * factor_of(own_float) * norm1_gain).astype(jnp.bfloat16)
    pieces = [normed_own]
    for hop in range(1, shards):
        came = lax.ppermute(normed_own, "head", [(i, i + hop) for i in range(nz - hop)])
        pieces.insert(0, jnp.where(before >= hop, came, jnp.zeros_like(came)))

    full = gather(jnp.concatenate([qkv_weight, out_weight.T[None]], axis=0), nz, ny, nx)

    def gathered(weight):
        share = weight.shape[0] // copies
        piece = lax.dynamic_slice_in_dim(weight, mine * share, share, 0)
        return lax.all_gather(piece, ALL, axis=0, tiled=True)

    up_rows = gathered(up_weight.T)
    down_rows = gathered(down_weight)
    kernel_all = lax.all_gather(kernels, "head", axis=2, tiled=True)
    up_bias_all = lax.all_gather(up_bias, "head", axis=0, tiled=True)
    kern = jnp.pad(kernel_all.reshape(9, -1), ((0, 7), (0, 0)))

    window = jnp.concatenate(pieces, axis=0)
    window_rows = shards * rows
    edge = EDGE if shards > 1 else 0
    late = window[window_rows - rows - edge:]
    linear_q = dot(late, full[0]).astype(jnp.bfloat16)
    linear_k = dot(window, full[1]).astype(jnp.bfloat16)
    linear_v = dot(window, full[2]).astype(jnp.bfloat16)
    attended, mass = attention_forward(before[None], linear_q, linear_k, linear_v, kern, rows)
    hidden = own_float + dot(attended, full[3], NT) + out_bias
    normed_two = (hidden * factor_of(hidden) * norm2_gain).astype(jnp.bfloat16)
    gate = jnp.maximum(dot(normed_two, up_rows, NT) + up_bias_all, 0.0)
    activation = jnp.square(gate).astype(jnp.bfloat16)
    gate_low = gate.astype(jnp.bfloat16)
    layer_output = (hidden + dot(activation, down_rows) + down_bias).astype(jnp.bfloat16)

    gate_grad = (2.0 * gate_low.astype(jnp.float32) * dot(cotangent, down_rows, NT)).astype(jnp.bfloat16)
    normed_two_grad = dot(gate_grad, up_rows)
    back_two, gain_rows = norm_backward(hidden, norm2_gain, normed_two_grad)
    hidden_grad = cotangent.astype(jnp.float32) + back_two
    hidden_low = hidden_grad.astype(jnp.bfloat16)
    attended_grad = dot(hidden_low, full[3]).astype(jnp.bfloat16)

    def blocks(columns):
        return columns.reshape(columns.shape[0], nz, -1).transpose(1, 0, 2)

    ff_grad = jnp.stack([
        jnp.stack([
            dot(normed_two, gate_grad[:, k * hidden_units:(k + 1) * hidden_units], TN).astype(jnp.bfloat16)
            if member == 0 else
            dot(cotangent, activation[:, k * hidden_units:(k + 1) * hidden_units], TN).astype(jnp.bfloat16)
            for member in range(2)
        ]) for k in range(nz)
    ])
    early = jnp.concatenate([
        jnp.sum(gain_rows, axis=0), jnp.sum(hidden_low.astype(jnp.float32), axis=0),
        jnp.sum(cotangent.astype(jnp.float32), axis=0), jnp.sum(gate_grad.astype(jnp.float32), axis=0),
    ]).reshape(-1, 1024)
    early = jnp.pad(early, ((0, -early.shape[0] % 8), (0, 0)))
    ff_sum, early = reduce(ff_grad, early, ny, nx, 1)

    grad_q, grad_k, grad_v, kernel_sums = attention_backward(
        before[None], linear_q, linear_k, linear_v, kern, attended_grad, attended, mass)
    normed_grad = dot(grad_k, full[1], NT) + dot(grad_v, full[2], NT)
    query_part = dot(grad_q, full[0], NT)
    normed_grad = normed_grad + jnp.pad(query_part, ((window_rows - rows - edge, 0), (0, 0)))
    normed_own_grad = normed_grad[window_rows - rows:]
    for hop in range(1, shards):
        at = window_rows - (hop + 1) * rows
        part = normed_grad[at:at + rows].astype(jnp.bfloat16)
        part = jnp.where(before >= hop, part, jnp.zeros_like(part))
        came = lax.ppermute(part, "head", [(i + hop, i) for i in range(nz - hop)])
        normed_own_grad = normed_own_grad + came.astype(jnp.float32)
    back_one, gain_rows_one = norm_backward(own_float, norm1_gain, normed_own_grad)
    layer_grad = (hidden_grad + back_one).astype(jnp.bfloat16)
    qkvo_grad = jnp.stack([
        blocks(dot(late, grad_q, TN).astype(jnp.bfloat16)),
        blocks(dot(window, grad_k, TN).astype(jnp.bfloat16)),
        blocks(dot(window, grad_v, TN).astype(jnp.bfloat16)),
        blocks(dot(hidden_low, attended, TN).astype(jnp.bfloat16)),
    ], axis=1)
    tail = jnp.concatenate([kernel_sums[:9], jnp.sum(gain_rows_one, axis=0)[None]], axis=0)
    tail = jnp.pad(tail, ((0, 6), (0, 0)))
    qkvo_sum, tail = reduce(qkvo_grad, tail, ny, nx, 2)

    width_all = norm1_gain.shape[0]
    early = early.reshape(-1)
    up_bias_grad = lax.dynamic_slice_in_dim(early[3 * width_all:], place * hidden_units, hidden_units, 0)
    kernels_grad = lax.dynamic_slice_in_dim(tail[:9].reshape(3, 3, -1), place * width, width, 2)
    f32 = jnp.float32
    return (
        layer_output[None], layer_grad[None], tail[9], qkvo_sum[:3].astype(f32), kernels_grad,
        qkvo_sum[3].T.astype(f32), early[width_all:2 * width_all], early[:width_all], ff_sum[0].astype(f32),
        up_bias_grad, ff_sum[1].T.astype(f32), early[2 * width_all:3 * width_all],
    )


def solution(mesh):
    rows = P(("batch", "dp"), "head", None)
    return jax.shard_map(
        on_device,
        mesh=mesh,
        in_specs=(
            rows, P(("batch", "dp"), None), P(), P(None, None, "head"), P(None, None, "head"), P("head", None), P(),
            P(), P(None, "head"), P("head"), P("head", None), P(), rows,
        ),
        out_specs=(
            rows, rows, P(), P(None, None, "head"), P(None, None, "head"), P("head", None),
            P(), P(), P(None, "head"), P("head"), P("head", None), P(),
        ),
        check_vma=False,
    )
```

```python
import functools
import math

import jax
import jax.numpy as jnp
from jax import lax
from jax.experimental import pallas as pl
from jax.experimental.pallas import tpu as pltpu
from jax.sharding import PartitionSpec as P

LONG = 2048
EPSILON = 1e-06
ALL = ("head", "batch", "dp")

MESH = pl.DeviceIdType.MESH
VMEM = pl.BlockSpec(memory_space=pltpu.VMEM)


class Copy:
    def __init__(self, source, target, device, send_sem, recv_sem):
        self.parts = source, target, device, send_sem, recv_sem

    def make(self):
        source, target, device, send_sem, recv_sem = self.parts
        return pltpu.make_async_remote_copy(
            src_ref=source(), dst_ref=target(), send_sem=send_sem(), recv_sem=recv_sem(), device_id=device(), device_id_type=MESH)

    def start(self):
        self.make().start()

    def wait_recv(self):
        self.make().wait_recv()

    def wait_send(self):
        self.make().wait_send()


class Copies:
    def __init__(self, send_sems, recv_sems):
        self.send_sems, self.recv_sems, self.made = send_sems, recv_sems, []

    def plan(self, source, target, device):
        n = len(self.made)
        copy = Copy(source, target, device, lambda: self.send_sems.at[n], lambda: self.recv_sems.at[n])
        self.made.append(copy)
        return copy

    def finish(self):
        for copy in self.made:
            copy.wait_send()


def start(copies):
    for copy in copies:
        copy.start()


def arrive(copies):
    for copy in copies:
        copy.wait_recv()


class Place:
    def __init__(self, nz, ny, nx):
        self.nz, self.ny, self.nx = nz, ny, nx
        self.z, batch, self.x = lax.axis_index("head"), lax.axis_index("batch"), lax.axis_index("dp")
        self.y, self.c = batch // 2, batch % 2

    def along_z(self, step):
        return lambda: {"head": (self.z + step) % self.nz}

    def along_y(self, step):
        return lambda: {"batch": (self.y + step) % self.ny * 2 + self.c}

    def along_x(self, step):
        return lambda: {"dp": (self.x + step) % self.nx}

    def other_core(self):
        return {"batch": self.y * 2 + 1 - self.c}

    def meet(self):
        partners = [self.along_z(s) for s in range(1, self.nz)]
        partners += [self.along_y(s) for s in range(1, self.ny)] + [self.along_x(s) for s in range(1, self.nx)]
        partners.append(self.other_core)
        barrier = pltpu.get_barrier_semaphore()
        for partner in partners:
            pl.semaphore_signal(barrier, inc=1, device_id=partner(), device_id_type=MESH)
        pl.semaphore_wait(barrier, len(partners))

    def band(self, rows, dy, core=0):
        size = self.nx * rows
        core = self.c if core == 0 else 1 - self.c
        return pl.ds(pl.multiple_of(((self.y - dy) % self.ny * 2 + core) * size, size), size)

    def piece(self, rows, dy, dx):
        if dx is None:
            return self.band(rows, dy)
        at = ((self.y - dy) % self.ny * 2 + self.c) * self.nx + (self.x - dx) % self.nx
        return pl.ds(pl.multiple_of(at * rows, rows), rows)


def spread(place, copies, spots):
    ny, nx = place.ny, place.nx

    def plan(spot, dy, dx, device):
        part = lambda: spot(dy, dx)
        return copies.plan(part, part, device)

    over_x = [[plan(spot, 0, 0, place.along_x(s)) for s in range(1, nx)] for spot in spots]
    over_y = [[plan(spot, 0, 0, place.along_y(t)) for t in range(1, ny)] for spot in spots]
    corner_y = [plan(spots[0], 0, s, place.along_y(t)) for s in range(1, nx) for t in range(1, ny)]
    corner_x = [plan(spots[1], t, 0, place.along_x(s)) for s in range(1, nx) for t in range(1, ny)]
    cores = [plan(spot, dy, None, place.other_core) for spot in spots for dy in range(ny)]

    def out():
        for k in (0, 1):
            start(over_x[k])
            start(over_y[k])

    def turn():
        arrive(over_x[0])
        start(corner_y)
        arrive(over_y[1])
        start(corner_x)
        arrive(over_x[1])
        arrive(over_y[0])

    def cross():
        arrive(corner_y)
        arrive(corner_x)
        start(cores)

    return [out, turn, cross, lambda: arrive(cores)]


def spread_count(ny, nx):
    return 2 * ((nx - 1) + (ny - 1) + (nx - 1) * (ny - 1) + ny)


def gather_tasks(place, copies, shards, fulls):
    nz = place.nz

    def part(k, step):
        return lambda: fulls[k]((place.z - step) % nz, 0, 0)

    rings = [
        [copies.plan(part(k, step) if step else shards[k], part(k, step), place.along_z(1)) for k in range(2)]
        for step in range(nz - 1)
    ]

    def task(step):
        spots = [lambda dy, dx, k=k: fulls[k]((place.z - 1 - step) % nz, dy, dx) for k in range(2)]
        out, *others = spread(place, copies, spots)

        def arrival():
            arrive(rings[step])
            if step < nz - 2:
                start(rings[step + 1])
            out()

        return [arrival] + others

    return lambda: start(rings[0]), [task(step) for step in range(nz - 1)]


def gather_count(nz, ny, nx):
    return (nz - 1) * (2 + spread_count(ny, nx))


def run_staggered(tasks):
    phases = [(at + n, n, phase) for n, task in enumerate(tasks) for at, phase in enumerate(task)]
    for _, _, phase in sorted(phases, key=lambda entry: entry[:2]):
        phase()


class Timetable:
    def __init__(self, per_step, steps):
        self.per_step, self.steps, self.at = per_step, steps, {}

    def add(self, task, times):
        for time, phase in zip(times, task, strict=True):
            self.at.setdefault(time, []).append(phase)

    def tick(self, slot):
        for time in range(slot, self.per_step * self.steps, self.per_step):
            if time in self.at:
                @pl.when(pl.program_id(0) == time // self.per_step)
                def _():
                    for phase in self.at[time]:
                        phase()

    def finish(self):
        for time in sorted(self.at):
            if time >= self.per_step * self.steps:
                for phase in self.at[time]:
                    phase()


def open_kernel(nz, ny, nx, shard_ref, small_ref, full_ref, all_ref, send_sems, recv_sems):
    place = Place(nz, ny, nx)
    copies = Copies(send_sems, recv_sems)
    members, height, width = shard_ref.shape
    half = members // 2
    rows = height // (ny * 2 * nx)

    def columns(block):
        return pl.ds(pl.multiple_of(block * width, width), width)

    fulls = [
        lambda block, dy, dx, lo=lo, hi=hi: full_ref.at[lo:hi, place.piece(rows, dy, dx), columns(block)]
        for lo, hi in ((0, half), (half, members))
    ]
    shards = [lambda lo=lo, hi=hi: shard_ref.at[lo:hi, place.piece(rows, 0, 0), :] for lo, hi in ((0, half), (half, members))]
    begin, tasks = gather_tasks(place, copies, shards, fulls)
    small = [copies.plan(lambda: small_ref, lambda: all_ref.at[place.z], place.along_z(s)) for s in range(1, nz)]
    place.meet()
    begin()
    start(small)
    all_ref[place.z] = small_ref[...]
    for m in range(members):
        full_ref[m, :, columns(place.z)] = shard_ref[m]
    run_staggered(tasks)
    arrive(small)
    copies.finish()


def gather_open(shard, small, nz, ny, nx):
    members, height, width = shard.shape
    count = gather_count(nz, ny, nx) + nz - 1
    return pl.pallas_call(
        functools.partial(open_kernel, nz, ny, nx),
        out_shape=(jax.ShapeDtypeStruct((members, height, width * nz), shard.dtype),
                   jax.ShapeDtypeStruct((nz,) + small.shape, small.dtype)),
        in_specs=[VMEM, VMEM],
        out_specs=(VMEM, VMEM),
        scratch_shapes=[pltpu.SemaphoreType.DMA((count,)), pltpu.SemaphoreType.DMA((count,))],
        compiler_params=pltpu.CompilerParams(collective_id=0, has_side_effects=True, vmem_limit_bytes=48 << 20),
        cost_estimate=pl.CostEstimate(flops=0, bytes_accessed=2 * members * height * width * nz * 2, transcendentals=0),
    )(shard, small)


class Reduction:
    def __init__(self, place, copies, grad_ref, out_ref, buffers):
        self.place, self.copies, self.grad, self.out = place, copies, grad_ref, out_ref
        self.core, self.y1, self.x1, self.x2, self.y2, self.z_send, self.z_buf = buffers
        self.members, self.height, self.width = grad_ref.shape[1:]
        self.half = self.members // 2
        self.rows = self.height // (place.ny * 2 * place.nx)
        self.sums = []

    @staticmethod
    def scratch(nz, ny, nx, members, height, width):
        half, rows, bf = members // 2, height // (ny * 2 * nx), jnp.bfloat16
        band = nx * rows
        return [
            pltpu.VMEM((nz, ny, members, band, width), bf),
            pltpu.VMEM((nz, ny - 1, half, band, width), bf),
            pltpu.VMEM((nz, nx - 1, ny, half, rows, width), bf),
            pltpu.VMEM((nz, nx - 1, half, rows, width), bf),
            pltpu.VMEM((nz, ny - 1, half, rows, width), bf),
            pltpu.VMEM((nz, members, rows, width), bf),
            pltpu.VMEM((nz - 1, members, rows, width), bf),
        ]

    @staticmethod
    def count(nz, ny, nx):
        return nz * (ny + 2 * (ny - 1) + 2 * (nx - 1)) + nz - 1 + spread_count(ny, nx)

    def chunk(self, t):
        place, copies, half, rows = self.place, self.copies, self.half, self.rows
        ny, nx, nz = place.ny, place.nx, place.nz
        core, x1, y1, x2, y2, f32, bf = self.core, self.x1, self.y1, self.x2, self.y2, jnp.float32, jnp.bfloat16

        def xrows(step):
            return pl.ds(pl.multiple_of((place.x + step) % nx * rows, rows), rows)

        sent = [
            copies.plan(
                lambda dy=dy: self.grad.at[(place.z + 1 + t) % nz, :, place.band(rows, dy, 1), :],
                lambda dy=dy: core.at[t, dy], place.other_core)
            for dy in range(ny)
        ]
        over_y = [
            copies.plan(lambda s=s: core.at[t, ny - s, 0:half], lambda s=s: y1.at[t, s - 1], place.along_y(s))
            for s in range(1, ny)
        ]
        over_x = [
            copies.plan(lambda s=s: core.at[t, :, half:, xrows(s), :], lambda s=s: x1.at[t, s - 1], place.along_x(s))
            for s in range(1, nx)
        ]
        then_x = [
            copies.plan(lambda s=s: core.at[t, 0, 0:half, xrows(s), :], lambda s=s: x2.at[t, s - 1], place.along_x(s))
            for s in range(1, nx)
        ]
        then_y = [
            copies.plan(lambda s=s: core.at[t, ny - s, half:, xrows(0), :], lambda s=s: y2.at[t, s - 1], place.along_y(s))
            for s in range(1, ny)
        ]
        along = [copies.plan(lambda: self.z_send.at[t], lambda: self.z_buf.at[t], place.along_z(1 + t))] if t < nz - 1 else []
        self.sums += along

        def both_cores():
            arrive(sent)
            for dy in range(ny):
                for m in range(self.members):
                    own = self.grad[(place.z + 1 + t) % nz, m, place.band(rows, dy), :]
                    core[t, dy, m] = (core[t, dy, m].astype(f32) + own.astype(f32)).astype(bf)
            start(over_y)
            start(over_x)

        def turn():
            arrive(over_y)
            for m in range(half):
                total = core[t, 0, m].astype(f32)
                for s in range(ny - 1):
                    total = total + y1[t, s, m].astype(f32)
                core[t, 0, m] = total.astype(bf)
            start(then_x)
            arrive(over_x)
            for dy in range(ny):
                for m in range(half):
                    total = core[t, dy, half + m, xrows(0), :].astype(f32)
                    for s in range(nx - 1):
                        total = total + x1[t, s, dy, m].astype(f32)
                    core[t, dy, half + m, xrows(0), :] = total.astype(bf)
            start(then_y)

        def send_on():
            arrive(then_x)
            arrive(then_y)
            for m in range(self.members):
                total = core[t, 0, m, xrows(0), :].astype(f32)
                buf, n = (x2, nx - 1) if m < half else (y2, ny - 1)
                for s in range(n):
                    total = total + buf[t, s, m % half].astype(f32)
                self.z_send[t, m] = total.astype(bf)
            start(along)

        return [lambda: start(sent), both_cores, turn, send_on]

    def ending(self):
        place, nz = self.place, self.place.nz
        spots = [
            lambda dy, dx, lo=lo, hi=hi: self.out.at[lo:hi, place.piece(self.rows, dy, dx), :]
            for lo, hi in ((0, self.half), (self.half, self.members))
        ]
        out, *others = spread(place, self.copies, spots)

        def total():
            arrive(self.sums)
            for m in range(self.members):
                total = self.z_send[nz - 1, m].astype(jnp.float32)
                for t in range(nz - 1):
                    total = total + self.z_buf[t, m].astype(jnp.float32)
                self.out[m, place.piece(self.rows, 0, 0), :] = total.astype(jnp.bfloat16)
            out()

        return [total] + others


def small_sum(place, copies, small_ref, out_ref, s_acc, s_buf):
    nz, ny, nx = place.nz, place.ny, place.nx
    stages = ([place.other_core], [place.along_x(s) for s in range(1, nx)],
              [place.along_y(s) for s in range(1, ny)], [place.along_z(s) for s in range(1, nz)])
    firsts = [0, 1, nx, nx + ny - 1]
    sent = [
        [copies.plan(lambda k=k: s_acc.at[k], lambda n=firsts[k] + i: s_buf.at[n], partner) for i, partner in enumerate(partners)]
        for k, partners in enumerate(stages)
    ]

    def add(k):
        arrive(sent[k])
        total = s_acc[k]
        for i in range(len(sent[k])):
            total = total + s_buf[firsts[k] + i]
        return total

    def first():
        s_acc[0] = small_ref[...]
        start(sent[0])

    def middle(k):
        s_acc[k + 1] = add(k)
        start(sent[k + 1])

    def last():
        out_ref[...] = add(3)

    return [first] + [functools.partial(middle, k) for k in range(3)] + [last]


def small_scratch(nz, ny, nx, shape):
    return [pltpu.VMEM((4,) + shape, jnp.float32), pltpu.VMEM((nx + ny + nz - 2,) + shape, jnp.float32)]


def reduce_kernel(nz, ny, nx, grad_ref, small_ref, out_ref, small_out_ref, *scratch):
    *buffers, s_acc, s_buf, send_sems, recv_sems = scratch
    place = Place(nz, ny, nx)
    copies = Copies(send_sems, recv_sems)
    place.meet()
    whole = Reduction(place, copies, grad_ref, out_ref, buffers)
    run_staggered([whole.chunk(0), small_sum(place, copies, small_ref, small_out_ref, s_acc, s_buf)]
                  + [whole.chunk(t) for t in range(1, nz)])
    for phase in whole.ending():
        phase()
    copies.finish()


def reduce(grad, small, ny, nx, collective_id):
    nz, members, height, width = grad.shape
    count = Reduction.count(nz, ny, nx) + nx + ny + nz - 2
    return pl.pallas_call(
        functools.partial(reduce_kernel, nz, ny, nx),
        out_shape=(jax.ShapeDtypeStruct((members, height, width), jnp.bfloat16), jax.ShapeDtypeStruct(small.shape, jnp.float32)),
        in_specs=[VMEM, VMEM],
        out_specs=(VMEM, VMEM),
        scratch_shapes=Reduction.scratch(nz, ny, nx, members, height, width) + small_scratch(nz, ny, nx, small.shape) + [
            pltpu.SemaphoreType.DMA((count,)), pltpu.SemaphoreType.DMA((count,)),
        ],
        compiler_params=pltpu.CompilerParams(collective_id=collective_id, has_side_effects=True, vmem_limit_bytes=56 << 20),
        cost_estimate=pl.CostEstimate(flops=0, bytes_accessed=grad.size * 2, transcendentals=0),
    )(grad, small)


HS = 64
LANES = 128
EDGE = 16
LOG2E = math.log2(math.e)
NT = (((1,), (1,)), ((), ()))
NN = (((1,), (0,)), ((), ()))
TN = (((0,), (0,)), ((), ()))


def dot(a, b, dims=NN):
    return lax.dot_general(a, b, dims, preferred_element_type=jnp.float32)


def spans(first, last, step):
    return [(at, min(step, last - at)) for at in range(first, last, step)]


def earlier(ref, start, size):
    if start == 0:
        rows = jnp.concatenate([jnp.zeros((EDGE, LANES), jnp.float32), ref[pl.ds(0, size), :].astype(jnp.float32)], axis=0)
    else:
        rows = ref[pl.ds(start - EDGE, size + EDGE), :].astype(jnp.float32)
    return [pltpu.roll(rows, i, 0)[EDGE:] if i else rows[EDGE:] for i in range(3)]


def convolve(linear_ref, kern_ref, member, target_ref, skip, step=256):
    total = linear_ref.shape[0]
    for start, size in spans(skip, total, step):
        taps = earlier(linear_ref, start, size)
        value = sum(kern_ref[3 * member + i:3 * member + i + 1, :] * taps[i] for i in range(3))
        target_ref[pl.ds(start - skip, size), :] = value.astype(jnp.bfloat16)


def convolve_back(grad_ref, linear_ref, kern_ref, member, target_ref, sums_ref, step=256):
    total = linear_ref.shape[0]
    parts = [jnp.zeros((8, LANES), jnp.float32)] * 3
    for start, size in spans(0, total, step):
        rows = grad_ref[pl.ds(start, size + 8), :]
        value = kern_ref[3 * member:3 * member + 1, :] * rows[:size]
        for i in (1, 2):
            value += kern_ref[3 * member + i:3 * member + i + 1, :] * pltpu.roll(rows, size + 8 - i, 0)[:size]
        target_ref[pl.ds(start, size), :] = value.astype(jnp.bfloat16)
        taps = earlier(linear_ref, start, size)
        for i in range(3):
            parts[i] += jnp.sum((rows[:size] * taps[i]).reshape(size // 8, 8, LANES), axis=0)
    for i in range(3):
        sums_ref[3 * member + i:3 * member + i + 1, :] = jnp.sum(parts[i], axis=0, keepdims=True)


def parts_of(rows, shards, at, size, step):
    own = (shards - 1) * rows
    pieces = []
    for hop in range(shards - 1, 0, -1):
        pieces += [(start, n, hop) for start, n in spans(own - hop * rows, own - (hop - 1) * rows, step)]
    pieces += [(start, n, 0) for start, n in spans(own, own + at, step)]
    return pieces + [(own + at, size, None)]


def forward_kernel(
    nz, ny, nx, steps, bq, kc, plan, far_ref, lq_ref, lk_ref, lv_ref, kern_ref, up_ref, down_ref,
    out_ref, mass_ref, up_out_ref, down_out_ref, q_ref, k_ref, v_ref, s0_ref, s1_ref, up_all_ref, down_all_ref,
    send_sems, recv_sems, out_sems,
):
    rows, window = q_ref.shape[0], k_ref.shape[0]
    shards = window // rows
    lane = lax.broadcasted_iota(jnp.int32, (bq, LANES), 1) < HS
    scale = 1.0 / math.sqrt(HS)

    place = Place(nz, ny, nx)
    copies = Copies(send_sems, recv_sems)
    units = up_ref.shape[0]
    share = units // (ny * 2 * nx)

    def spot(ref):
        def at(block, dy, dx):
            return ref.at[pl.ds(pl.multiple_of(block * units, units), units), :].at[place.piece(share, dy, dx), :]
        return at

    begin, tasks = gather_tasks(
        place, copies, [lambda ref=ref: ref.at[place.piece(share, 0, 0), :] for ref in (up_ref, down_ref)],
        [spot(up_all_ref), spot(down_all_ref)])

    def store(step):
        part = pl.ds(pl.multiple_of((place.z - step) % nz * units, units), units)
        pairs = ((up_ref, up_all_ref, up_out_ref), (down_ref, down_all_ref, down_out_ref))
        return [
            pltpu.make_async_copy(whole.at[part, :] if step else own, out.at[part, :], out_sems.at[2 * step + k])
            for k, (own, whole, out) in enumerate(pairs)
        ]

    def and_store(phase, step):
        def both():
            phase()
            start(store(step))
        return both

    @pl.when(pl.program_id(0) == 0)
    def _():
        place.meet()
        begin()
        start(store(0))

    table = Timetable(rows // bq, steps)
    for step, (task, ticks) in enumerate(zip(tasks, plan, strict=True)):
        table.add(task[:-1] + [and_store(task[-1], step + 1)], ticks)

    convolve(lq_ref, kern_ref, 0, q_ref, lq_ref.shape[0] - rows)
    convolve(lk_ref, kern_ref, 1, k_ref, 0)
    convolve(lv_ref, kern_ref, 2, v_ref, 0)

    def block(at):
        query = q_ref[pl.ds(at, bq), :] * jnp.bfloat16(scale)
        zero = jnp.zeros_like(query)
        queries = (jnp.where(lane, query, zero), jnp.where(lane, zero, query))
        stores = (s0_ref, s1_ref)
        peaks = [{}, {}]
        parts = parts_of(rows, shards, at, bq, kc)
        for start, size, hop in parts:
            key = k_ref[pl.ds(start, size), :]
            for h in range(2):
                s = dot(queries[h], key, NT)
                if hop is None:
                    row = lax.broadcasted_iota(jnp.int32, (bq, size), 0)
                    col = lax.broadcasted_iota(jnp.int32, (bq, size), 1)
                    s = jnp.where(col <= row, s, -1e30)
                stores[h][:, pl.ds(start, size)] = s
                top = jnp.max(s, axis=1, keepdims=True)
                group = hop or 0
                peaks[h][group] = jnp.maximum(peaks[h][group], top) if group in peaks[h] else top
        sums = [None, None]
        peak, scaled = [], [{}, {}]
        for h in range(2):
            top = peaks[h][0]
            for hop in range(1, shards):
                top = jnp.maximum(top, peaks[h][hop] - far_ref[hop - 1:hop, 0:1])
            peak.append(top)
            scaled[h][0] = top * LOG2E
            for hop in range(1, shards):
                scaled[h][hop] = scaled[h][0] + far_ref[hop - 1:hop, 0:1]
        for start, size, hop in parts:
            value = v_ref[pl.ds(start, size), :]
            wide = lax.broadcasted_iota(jnp.int32, (size, LANES), 1) < HS
            one = jnp.ones_like(value)
            values = (jnp.where(wide, value, one), jnp.where(wide, one, value))
            for h in range(2):
                p = jnp.exp2(stores[h][:, pl.ds(start, size)] * LOG2E - scaled[h][hop or 0]).astype(jnp.bfloat16)
                o = dot(p, values[h])
                sums[h] = o if sums[h] is None else sums[h] + o
        total = pltpu.roll(jnp.where(lane, sums[1], sums[0]), HS, 1)
        out_ref[pl.ds(at, bq), :] = (jnp.where(lane, sums[0], sums[1]) / total).astype(out_ref.dtype)
        mass = jnp.where(lane, peak[0], peak[1]) + jnp.log(total)
        mass = mass.T
        mass_ref[0, 0:1, pl.ds(at, bq)] = mass[0:1]
        mass_ref[0, 1:2, pl.ds(at, bq)] = mass[HS:HS + 1]

    for slot, at in enumerate(range(0, rows, bq)):
        table.tick(slot)
        block(at)

    @pl.when(pl.program_id(0) == steps - 1)
    def _():
        table.finish()
        for step in range(nz):
            for copy in store(step):
                copy.wait()
        copies.finish()


def column(n):
    return pl.BlockSpec((n, LANES), lambda i: (0, i))


ANY = pl.BlockSpec(memory_space=pl.ANY)
WHOLE = pl.BlockSpec((8, LANES), lambda i: (0, 0))


def attention_forward(far, late, linear_k, linear_v, kern, up, down, rows, nz, ny, nx):
    edged, width = late.shape
    window = linear_k.shape[0]
    pairs = width // LANES
    bq = min(512, rows)
    units, depth = up.shape
    bf = jnp.bfloat16
    count = gather_count(nz, ny, nx)
    slots = rows // bq
    first = [round(3.6 * (s + 1)) for s in range(nz - 1)]
    plan = [(f, f + 4, f + 6, f + 7) for f in first]
    return pl.pallas_call(
        functools.partial(forward_kernel, nz, ny, nx, pairs, bq, 512, plan),
        out_shape=(jax.ShapeDtypeStruct((rows, width), bf), jax.ShapeDtypeStruct((pairs, 8, rows), jnp.float32),
                   jax.ShapeDtypeStruct((nz * units, depth), bf), jax.ShapeDtypeStruct((nz * units, depth), bf)),
        grid=(pairs,),
        in_specs=[WHOLE, column(edged), column(window), column(window), column(16), VMEM, VMEM],
        out_specs=[column(rows), pl.BlockSpec((1, 8, rows), lambda i: (i, 0, 0)), ANY, ANY],
        scratch_shapes=[
            pltpu.VMEM((rows, LANES), bf), pltpu.VMEM((window, LANES), bf), pltpu.VMEM((window, LANES), bf),
            pltpu.VMEM((bq, window), jnp.float32), pltpu.VMEM((bq, window), jnp.float32),
            pltpu.VMEM((nz * units, depth), bf), pltpu.VMEM((nz * units, depth), bf),
            pltpu.SemaphoreType.DMA((count,)), pltpu.SemaphoreType.DMA((count,)), pltpu.SemaphoreType.DMA((2 * nz,)),
        ],
        compiler_params=pltpu.CompilerParams(collective_id=1, has_side_effects=True, vmem_limit_bytes=56 << 20),
    )(far, late, linear_k, linear_v, kern, up, down)


def backward_kernel(
    nz, ny, nx, steps, bq, kc, plan, far_ref, lq_ref, lk_ref, lv_ref, kern_ref, g_ref, o_ref, mass_ref, grad_ref, small_ref,
    gq_ref, gk_ref, gv_ref, sums_ref, total_ref, small_out_ref,
    q_ref, k_ref, v_ref, kt_ref, dq_ref, dk_ref, dv_ref, *scratch,
):
    rows, window = q_ref.shape[0], k_ref.shape[0]
    shards = window // rows
    edge = lq_ref.shape[0] - rows
    lane = lax.broadcasted_iota(jnp.int32, (bq, LANES), 1) < HS
    scale = 1.0 / math.sqrt(HS)

    *buffers, s_acc, s_buf, sum_ref, send_sems, recv_sems, out_sem = scratch
    place = Place(nz, ny, nx)
    copies = Copies(send_sems, recv_sems)

    @pl.when(pl.program_id(0) == 0)
    def _():
        place.meet()

    whole = Reduction(place, copies, grad_ref, sum_ref, buffers)
    table = Timetable(rows // bq, steps)
    chunk_plan, small_plan, ending_plan = plan
    for t, ticks in enumerate(chunk_plan):
        table.add(whole.chunk(t), ticks)
    table.add(small_sum(place, copies, small_ref, small_out_ref, s_acc, s_buf), small_plan)
    table.add(whole.ending(), ending_plan)

    convolve(lq_ref, kern_ref, 0, q_ref, edge)
    convolve(lk_ref, kern_ref, 1, k_ref, 0)
    convolve(lv_ref, kern_ref, 2, v_ref, 0)
    dk_ref[...] = jnp.zeros_like(dk_ref)
    dv_ref[...] = jnp.zeros_like(dv_ref)
    if edge:
        dq_ref[pl.ds(0, edge), :] = jnp.zeros((edge, LANES), jnp.float32)
    dq_ref[pl.ds(edge + rows, 8), :] = jnp.zeros((8, LANES), jnp.float32)
    kt_ref[...] = k_ref[...].astype(jnp.float32).T.astype(jnp.bfloat16)

    def block(at):
        query = q_ref[pl.ds(at, bq), :] * jnp.bfloat16(scale)
        grad = g_ref[pl.ds(at, bq), :]
        zero = jnp.zeros_like(query)
        queries = (jnp.where(lane, query, zero), jnp.where(lane, zero, query))
        grads = (jnp.where(lane, grad, zero), jnp.where(lane, zero, grad))
        product = (grad.astype(jnp.float32) * o_ref[pl.ds(at, bq), :].astype(jnp.float32)).T
        query_grads = [jnp.zeros((HS, bq), jnp.float32)] * 2
        deltas = [jnp.sum(product[h * HS:(h + 1) * HS], axis=0, keepdims=True) for h in range(2)]
        masses = [mass_ref[0, h:h + 1, pl.ds(at, bq)] * LOG2E for h in range(2)]
        for start, size, hop in parts_of(rows, shards, at, bq, kc):
            key = k_ref[pl.ds(start, size), :]
            value = v_ref[pl.ds(start, size), :]
            key_part = value_part = None
            for h in range(2):
                s = dot(key, queries[h], NT)
                if hop is None:
                    row = lax.broadcasted_iota(jnp.int32, (size, bq), 1)
                    col = lax.broadcasted_iota(jnp.int32, (size, bq), 0)
                    s = jnp.where(col <= row, s, -1e30)
                mass = masses[h] + far_ref[hop - 1:hop, 0:1] if hop else masses[h]
                p = jnp.exp2(s * LOG2E - mass)
                dp = dot(value, grads[h], NT)
                ds = (p * (dp - deltas[h])).astype(jnp.bfloat16)
                a = dot(p.astype(jnp.bfloat16), grads[h])
                b = dot(ds, queries[h])
                value_part = a if value_part is None else value_part + a
                key_part = b if key_part is None else key_part + b
                query_grads[h] += dot(kt_ref[h * HS:(h + 1) * HS, pl.ds(start, size)], ds)
            dk_ref[pl.ds(start, size), :] += key_part
            dv_ref[pl.ds(start, size), :] += value_part
        dq_ref[pl.ds(edge + at, bq), :] = jnp.concatenate(query_grads, axis=0).T * scale

    for slot, at in enumerate(range(0, rows, bq)):
        table.tick(slot)
        block(at)

    sums_ref[...] = jnp.zeros_like(sums_ref)
    convolve_back(dq_ref, lq_ref, kern_ref, 0, gq_ref, sums_ref)
    convolve_back(dk_ref, lk_ref, kern_ref, 1, gk_ref, sums_ref)
    convolve_back(dv_ref, lv_ref, kern_ref, 2, gv_ref, sums_ref)

    @pl.when(pl.program_id(0) == steps - 1)
    def _():
        table.finish()
        out = pltpu.make_async_copy(sum_ref, total_ref, out_sem)
        out.start()
        copies.finish()
        out.wait()


def attention_backward(far, late, linear_k, linear_v, kern, grads, outs, mass, ff_grad, small, ny, nx):
    rows = grads.shape[0]
    edged, width = late.shape
    window = linear_k.shape[0]
    pairs = width // LANES
    bq = min(256, rows)
    bf = jnp.bfloat16
    nz, members, height, columns = ff_grad.shape
    count = Reduction.count(nz, ny, nx) + nx + ny + nz - 2
    ticks = pairs * (rows // bq)
    gap = max(1, ticks // 2 // nz)
    chunks = [(gap * t, gap * t + 3, gap * t + 7, gap * t + 10) for t in range(nz)]
    end = max(chunks[-1][-1] + 1, ticks - 5)
    plan = (chunks, range(2, 12, 2), (end, end + 4, end + 6, end + 7))
    return pl.pallas_call(
        functools.partial(backward_kernel, nz, ny, nx, pairs, bq, 1024, plan),
        out_shape=(jax.ShapeDtypeStruct((edged, width), bf), jax.ShapeDtypeStruct((window, width), bf),
                   jax.ShapeDtypeStruct((window, width), bf), jax.ShapeDtypeStruct((16, width), jnp.float32),
                   jax.ShapeDtypeStruct((members, height, columns), bf), jax.ShapeDtypeStruct(small.shape, jnp.float32)),
        grid=(pairs,),
        in_specs=[WHOLE, column(edged), column(window), column(window), column(16), column(rows), column(rows),
                  pl.BlockSpec((1, 8, rows), lambda i: (i, 0, 0)), VMEM, VMEM],
        out_specs=[column(edged), column(window), column(window), column(16), ANY, VMEM],
        scratch_shapes=[
            pltpu.VMEM((rows, LANES), bf), pltpu.VMEM((window, LANES), bf), pltpu.VMEM((window, LANES), bf),
            pltpu.VMEM((LANES, window), bf), pltpu.VMEM((edged + 8, LANES), jnp.float32),
            pltpu.VMEM((window + 8, LANES), jnp.float32), pltpu.VMEM((window + 8, LANES), jnp.float32),
        ] + Reduction.scratch(nz, ny, nx, members, height, columns) + small_scratch(nz, ny, nx, small.shape) + [
            pltpu.VMEM((members, height, columns), bf),
            pltpu.SemaphoreType.DMA((count,)), pltpu.SemaphoreType.DMA((count,)), pltpu.SemaphoreType.DMA,
        ],
        compiler_params=pltpu.CompilerParams(collective_id=2, has_side_effects=True, vmem_limit_bytes=60 << 20),
    )(far, late, linear_k, linear_v, kern, grads, outs, mass, ff_grad, small)


def factor_of(values):
    return lax.rsqrt(jnp.mean(values * values, axis=-1, keepdims=True) + EPSILON)


def norm_backward(values, gain, upstream):
    factor = factor_of(values)
    unit = values * factor
    scaled = gain * upstream
    result = factor * (scaled - unit * jnp.mean(scaled * unit, axis=-1, keepdims=True))
    return result, upstream * unit


def on_device(
    layer_input, lengths, norm1_gain, qkv_weight, kernels, out_weight, out_bias,
    norm2_gain, up_weight, up_bias, down_weight, down_bias, out_grad,
):
    rows = layer_input.shape[1]
    nz, nb, nx = lax.axis_size("head"), lax.axis_size("batch"), lax.axis_size("dp")
    ny = nb // 2
    shards = max(1, LONG // rows)
    place = lax.axis_index("head")
    width = qkv_weight.shape[2]
    hidden_units = up_weight.shape[1]

    first_row = place * rows
    ends = jnp.cumsum(lengths[0])
    begins = jnp.max(jnp.where(ends <= first_row, ends, 0))
    before = ((first_row - begins) // rows).astype(jnp.int32)

    own_float = layer_input[0].astype(jnp.float32)
    cotangent = out_grad[0]
    normed_own = (own_float * factor_of(own_float) * norm1_gain).astype(jnp.bfloat16)
    pieces = [normed_own]
    for hop in range(1, shards):
        came = lax.ppermute(normed_own, "head", [(i, i + hop) for i in range(nz - hop)])
        pieces.insert(0, jnp.where(before >= hop, came, jnp.zeros_like(came)))

    small = jnp.concatenate([kernels.reshape(9, width), up_bias.reshape(-1, width)], axis=0)
    small = jnp.pad(small, ((0, -small.shape[0] % 8), (0, 0)))
    full, small = gather_open(jnp.concatenate([qkv_weight, out_weight.T[None]], axis=0), small, nz, ny, nx)
    kern = jnp.pad(small[:, :9].transpose(1, 0, 2).reshape(9, -1), ((0, 7), (0, 0)))
    up_bias_all = small[:, 9:9 + hidden_units // width].reshape(-1)

    window = jnp.concatenate(pieces, axis=0)
    window_rows = shards * rows
    edge = EDGE if shards > 1 else 0
    late = window[window_rows - rows - edge:]
    linear_q = dot(late, full[0]).astype(jnp.bfloat16)
    linear_k = dot(window, full[1]).astype(jnp.bfloat16)
    linear_v = dot(window, full[2]).astype(jnp.bfloat16)
    hops = jnp.arange(1, 9)[:, None]
    far = jnp.broadcast_to(jnp.where(before >= hops, 0.0, 1e30), (8, LANES)).astype(jnp.float32)
    attended, mass, up_rows, down_rows = attention_forward(
        far, linear_q, linear_k, linear_v, kern, up_weight.T, down_weight, rows, nz, ny, nx)
    hidden = own_float + dot(attended, full[3], NT) + out_bias
    normed_two = (hidden * factor_of(hidden) * norm2_gain).astype(jnp.bfloat16)
    gate = jnp.maximum(dot(normed_two, up_rows, NT) + up_bias_all, 0.0)
    activation = jnp.square(gate).astype(jnp.bfloat16)
    gate_low = gate.astype(jnp.bfloat16)
    layer_output = (hidden + dot(activation, down_rows) + down_bias).astype(jnp.bfloat16)

    gate_grad = (2.0 * gate_low.astype(jnp.float32) * dot(cotangent, down_rows, NT)).astype(jnp.bfloat16)
    normed_two_grad = dot(gate_grad, up_rows)
    back_two, gain_rows = norm_backward(hidden, norm2_gain, normed_two_grad)
    hidden_grad = cotangent.astype(jnp.float32) + back_two
    hidden_low = hidden_grad.astype(jnp.bfloat16)
    attended_grad = dot(hidden_low, full[3]).astype(jnp.bfloat16)

    def blocks(columns):
        return columns.reshape(columns.shape[0], nz, -1).transpose(1, 0, 2)

    ff_grad = jnp.stack([
        jnp.stack([
            dot(gate_grad[:, k * hidden_units:(k + 1) * hidden_units], normed_two, TN).astype(jnp.bfloat16)
            if member == 0 else
            dot(activation[:, k * hidden_units:(k + 1) * hidden_units], cotangent, TN).astype(jnp.bfloat16)
            for member in range(2)
        ]) for k in range(nz)
    ])
    early = jnp.concatenate([
        jnp.sum(gain_rows, axis=0), jnp.sum(hidden_low.astype(jnp.float32), axis=0),
        jnp.sum(cotangent.astype(jnp.float32), axis=0), jnp.sum(gate_grad.astype(jnp.float32), axis=0),
    ]).reshape(-1, 1024)
    early = jnp.pad(early, ((0, -early.shape[0] % 8), (0, 0)))
    grad_q, grad_k, grad_v, kernel_sums, ff_sum, early = attention_backward(
        far, linear_q, linear_k, linear_v, kern, attended_grad, attended, mass, ff_grad, early, ny, nx)
    normed_grad = dot(grad_k, full[1], NT) + dot(grad_v, full[2], NT)
    query_part = dot(grad_q, full[0], NT)
    normed_grad = normed_grad + jnp.pad(query_part, ((window_rows - rows - edge, 0), (0, 0)))
    normed_own_grad = normed_grad[window_rows - rows:]
    for hop in range(1, shards):
        at = window_rows - (hop + 1) * rows
        part = normed_grad[at:at + rows].astype(jnp.bfloat16)
        part = jnp.where(before >= hop, part, jnp.zeros_like(part))
        came = lax.ppermute(part, "head", [(i + hop, i) for i in range(nz - hop)])
        normed_own_grad = normed_own_grad + came.astype(jnp.float32)
    back_one, gain_rows_one = norm_backward(own_float, norm1_gain, normed_own_grad)
    layer_grad = (hidden_grad + back_one).astype(jnp.bfloat16)
    qkvo_grad = jnp.stack([
        blocks(dot(late, grad_q, TN).astype(jnp.bfloat16)),
        blocks(dot(window, grad_k, TN).astype(jnp.bfloat16)),
        blocks(dot(window, grad_v, TN).astype(jnp.bfloat16)),
        blocks(dot(hidden_low, attended, TN).astype(jnp.bfloat16)),
    ], axis=1)
    tail = jnp.concatenate([kernel_sums[:9], jnp.sum(gain_rows_one, axis=0)[None]], axis=0)
    tail = jnp.pad(tail, ((0, 6), (0, 0)))
    qkvo_sum, tail = reduce(qkvo_grad, tail, ny, nx, 3)

    width_all = norm1_gain.shape[0]
    early = early.reshape(-1)
    up_bias_grad = lax.dynamic_slice_in_dim(early[3 * width_all:], place * hidden_units, hidden_units, 0)
    kernels_grad = lax.dynamic_slice_in_dim(tail[:9].reshape(3, 3, -1), place * width, width, 2)
    f32 = jnp.float32
    return (
        layer_output[None], layer_grad[None], tail[9], qkvo_sum[:3].astype(f32), kernels_grad,
        qkvo_sum[3].T.astype(f32), early[width_all:2 * width_all], early[:width_all], ff_sum[0].T.astype(f32),
        up_bias_grad, ff_sum[1].astype(f32), early[2 * width_all:3 * width_all],
    )


def solution(mesh):
    rows = P(("batch", "dp"), "head", None)
    return jax.shard_map(
        on_device,
        mesh=mesh,
        in_specs=(
            rows, P(("batch", "dp"), None), P(), P(None, None, "head"), P(None, None, "head"), P("head", None), P(),
            P(), P(None, "head"), P("head"), P("head", None), P(), rows,
        ),
        out_specs=(
            rows, rows, P(), P(None, None, "head"), P(None, None, "head"), P("head", None),
            P(), P(), P(None, "head"), P("head"), P("head", None), P(),
        ),
        check_vma=False,
    )
```

```python
import functools
import math

import jax
import jax.numpy as jnp
from jax import lax
from jax.experimental import pallas as pl
from jax.experimental.pallas import tpu as pltpu
from jax.sharding import PartitionSpec as P

LONG = 2048
EPSILON = 1e-06
ALL = ("head", "batch", "dp")

MESH = pl.DeviceIdType.MESH
VMEM = pl.BlockSpec(memory_space=pltpu.VMEM)


class Copy:
    def __init__(self, source, target, device, send_sem, recv_sem):
        self.parts = source, target, device, send_sem, recv_sem

    def make(self):
        source, target, device, send_sem, recv_sem = self.parts
        return pltpu.make_async_remote_copy(
            src_ref=source(), dst_ref=target(), send_sem=send_sem(), recv_sem=recv_sem(), device_id=device(), device_id_type=MESH)

    def start(self):
        self.make().start()

    def wait_recv(self):
        self.make().wait_recv()

    def wait_send(self):
        self.make().wait_send()


class Copies:
    def __init__(self, send_sems, recv_sems):
        self.send_sems, self.recv_sems, self.made = send_sems, recv_sems, []

    def plan(self, source, target, device):
        n = len(self.made)
        copy = Copy(source, target, device, lambda: self.send_sems.at[n], lambda: self.recv_sems.at[n])
        self.made.append(copy)
        return copy

    def finish(self):
        for copy in self.made:
            copy.wait_send()


def start(copies):
    for copy in copies:
        copy.start()


def arrive(copies):
    for copy in copies:
        copy.wait_recv()


class Place:
    def __init__(self, nz, ny, nx):
        self.nz, self.ny, self.nx = nz, ny, nx
        self.z, batch, self.x = lax.axis_index("head"), lax.axis_index("batch"), lax.axis_index("dp")
        self.y, self.c = batch // 2, batch % 2

    def along_z(self, step):
        return lambda: {"head": (self.z + step) % self.nz}

    def along_y(self, step):
        return lambda: {"batch": (self.y + step) % self.ny * 2 + self.c}

    def along_x(self, step):
        return lambda: {"dp": (self.x + step) % self.nx}

    def other_core(self):
        return {"batch": self.y * 2 + 1 - self.c}

    def meet(self):
        partners = [self.along_z(s) for s in range(1, self.nz)]
        partners += [self.along_y(s) for s in range(1, self.ny)] + [self.along_x(s) for s in range(1, self.nx)]
        partners.append(self.other_core)
        barrier = pltpu.get_barrier_semaphore()
        for partner in partners:
            pl.semaphore_signal(barrier, inc=1, device_id=partner(), device_id_type=MESH)
        pl.semaphore_wait(barrier, len(partners))

    def band(self, rows, dy, core=0):
        size = self.nx * rows
        core = self.c if core == 0 else 1 - self.c
        return pl.ds(pl.multiple_of(((self.y - dy) % self.ny * 2 + core) * size, size), size)

    def piece(self, rows, dy, dx):
        if dx is None:
            return self.band(rows, dy)
        at = ((self.y - dy) % self.ny * 2 + self.c) * self.nx + (self.x - dx) % self.nx
        return pl.ds(pl.multiple_of(at * rows, rows), rows)


def spread(place, copies, spots):
    ny, nx = place.ny, place.nx

    def plan(spot, dy, dx, device):
        part = lambda: spot(dy, dx)
        return copies.plan(part, part, device)

    over_x = [[plan(spot, 0, 0, place.along_x(s)) for s in range(1, nx)] for spot in spots]
    over_y = [[plan(spot, 0, 0, place.along_y(t)) for t in range(1, ny)] for spot in spots]
    corner_y = [plan(spots[0], 0, s, place.along_y(t)) for s in range(1, nx) for t in range(1, ny)]
    corner_x = [plan(spots[1], t, 0, place.along_x(s)) for s in range(1, nx) for t in range(1, ny)]
    cores = [plan(spot, dy, None, place.other_core) for spot in spots for dy in range(ny)]

    def out():
        for k in (0, 1):
            start(over_x[k])
            start(over_y[k])

    def turn():
        arrive(over_x[0])
        start(corner_y)
        arrive(over_y[1])
        start(corner_x)
        arrive(over_x[1])
        arrive(over_y[0])

    def cross():
        arrive(corner_y)
        arrive(corner_x)
        start(cores)

    return [out, turn, cross, lambda: arrive(cores)]


def spread_count(ny, nx):
    return 2 * ((nx - 1) + (ny - 1) + (nx - 1) * (ny - 1) + ny)


def gather_tasks(place, copies, shards, fulls):
    nz = place.nz

    def part(k, step):
        return lambda: fulls[k]((place.z - step) % nz, 0, 0)

    rings = [
        [copies.plan(part(k, step) if step else shards[k], part(k, step), place.along_z(1)) for k in range(2)]
        for step in range(nz - 1)
    ]

    def task(step):
        spots = [lambda dy, dx, k=k: fulls[k]((place.z - 1 - step) % nz, dy, dx) for k in range(2)]
        out, *others = spread(place, copies, spots)

        def arrival():
            arrive(rings[step])
            if step < nz - 2:
                start(rings[step + 1])
            out()

        return [arrival] + others

    return lambda: start(rings[0]), [task(step) for step in range(nz - 1)]


def gather_count(nz, ny, nx):
    return (nz - 1) * (2 + spread_count(ny, nx))


def run_staggered(tasks):
    phases = [(at + n, n, phase) for n, task in enumerate(tasks) for at, phase in enumerate(task)]
    for _, _, phase in sorted(phases, key=lambda entry: entry[:2]):
        phase()


class Timetable:
    def __init__(self, per_step, steps):
        self.per_step, self.steps, self.at = per_step, steps, {}

    def add(self, task, times):
        for time, phase in zip(times, task, strict=True):
            self.at.setdefault(time, []).append(phase)

    def tick(self, slot):
        for time in range(slot, self.per_step * self.steps, self.per_step):
            if time in self.at:
                @pl.when(pl.program_id(0) == time // self.per_step)
                def _():
                    for phase in self.at[time]:
                        phase()

    def finish(self):
        for time in sorted(self.at):
            if time >= self.per_step * self.steps:
                for phase in self.at[time]:
                    phase()


def open_kernel(nz, ny, nx, shard_ref, small_ref, full_ref, all_ref, send_sems, recv_sems):
    place = Place(nz, ny, nx)
    copies = Copies(send_sems, recv_sems)
    members, height, width = shard_ref.shape
    half = members // 2
    rows = height // (ny * 2 * nx)

    def columns(block):
        return pl.ds(pl.multiple_of(block * width, width), width)

    fulls = [
        lambda block, dy, dx, lo=lo, hi=hi: full_ref.at[lo:hi, place.piece(rows, dy, dx), columns(block)]
        for lo, hi in ((0, half), (half, members))
    ]
    shards = [lambda lo=lo, hi=hi: shard_ref.at[lo:hi, place.piece(rows, 0, 0), :] for lo, hi in ((0, half), (half, members))]
    begin, tasks = gather_tasks(place, copies, shards, fulls)
    small = [copies.plan(lambda: small_ref, lambda: all_ref.at[place.z], place.along_z(s)) for s in range(1, nz)]
    place.meet()
    begin()
    start(small)
    all_ref[place.z] = small_ref[...]
    for m in range(members):
        full_ref[m, :, columns(place.z)] = shard_ref[m]
    run_staggered(tasks)
    arrive(small)
    copies.finish()


def gather_open(shard, small, nz, ny, nx):
    members, height, width = shard.shape
    count = gather_count(nz, ny, nx) + nz - 1
    return pl.pallas_call(
        functools.partial(open_kernel, nz, ny, nx),
        out_shape=(jax.ShapeDtypeStruct((members, height, width * nz), shard.dtype),
                   jax.ShapeDtypeStruct((nz,) + small.shape, small.dtype)),
        in_specs=[VMEM, VMEM],
        out_specs=(VMEM, VMEM),
        scratch_shapes=[pltpu.SemaphoreType.DMA((count,)), pltpu.SemaphoreType.DMA((count,))],
        compiler_params=pltpu.CompilerParams(collective_id=0, has_side_effects=True, vmem_limit_bytes=48 << 20),
        cost_estimate=pl.CostEstimate(flops=0, bytes_accessed=2 * members * height * width * nz * 2, transcendentals=0),
    )(shard, small)


class Reduction:
    def __init__(self, place, copies, grad_ref, out_ref, buffers):
        self.place, self.copies, self.grad, self.out = place, copies, grad_ref, out_ref
        self.core, self.y1, self.x1, self.x2, self.y2, self.z_send, self.z_buf = buffers
        self.members, self.height, self.width = grad_ref.shape[1:]
        self.half = self.members // 2
        self.rows = self.height // (place.ny * 2 * place.nx)
        self.sums = []

    @staticmethod
    def scratch(nz, ny, nx, members, height, width):
        half, rows, bf = members // 2, height // (ny * 2 * nx), jnp.bfloat16
        band = nx * rows
        return [
            pltpu.VMEM((nz, ny, members, band, width), bf),
            pltpu.VMEM((nz, ny - 1, half, band, width), bf),
            pltpu.VMEM((nz, nx - 1, ny, half, rows, width), bf),
            pltpu.VMEM((nz, nx - 1, half, rows, width), bf),
            pltpu.VMEM((nz, ny - 1, half, rows, width), bf),
            pltpu.VMEM((nz, members, rows, width), bf),
            pltpu.VMEM((nz - 1, members, rows, width), bf),
        ]

    @staticmethod
    def count(nz, ny, nx):
        return nz * (ny + 2 * (ny - 1) + 2 * (nx - 1)) + nz - 1 + spread_count(ny, nx)

    def source(self, t, dy):
        return self.grad.at[(self.place.z + 1 + t) % self.place.nz, :, self.place.band(self.rows, dy, 1), :]

    def own(self, t, dy, m):
        return self.grad[(self.place.z + 1 + t) % self.place.nz, m, self.place.band(self.rows, dy), :]

    def chunk(self, t):
        place, copies, half, rows = self.place, self.copies, self.half, self.rows
        ny, nx, nz = place.ny, place.nx, place.nz
        core, x1, y1, x2, y2, f32, bf = self.core, self.x1, self.y1, self.x2, self.y2, jnp.float32, jnp.bfloat16

        def xrows(step):
            return pl.ds(pl.multiple_of((place.x + step) % nx * rows, rows), rows)

        sent = [
            copies.plan(
                lambda dy=dy: self.source(t, dy),
                lambda dy=dy: core.at[t, dy], place.other_core)
            for dy in range(ny)
        ]
        over_y = [
            copies.plan(lambda s=s: core.at[t, ny - s, 0:half], lambda s=s: y1.at[t, s - 1], place.along_y(s))
            for s in range(1, ny)
        ]
        over_x = [
            copies.plan(lambda s=s: core.at[t, :, half:, xrows(s), :], lambda s=s: x1.at[t, s - 1], place.along_x(s))
            for s in range(1, nx)
        ]
        then_x = [
            copies.plan(lambda s=s: core.at[t, 0, 0:half, xrows(s), :], lambda s=s: x2.at[t, s - 1], place.along_x(s))
            for s in range(1, nx)
        ]
        then_y = [
            copies.plan(lambda s=s: core.at[t, ny - s, half:, xrows(0), :], lambda s=s: y2.at[t, s - 1], place.along_y(s))
            for s in range(1, ny)
        ]
        along = [copies.plan(lambda: self.z_send.at[t], lambda: self.z_buf.at[t], place.along_z(1 + t))] if t < nz - 1 else []
        self.sums += along

        def both_cores():
            arrive(sent)
            for dy in range(ny):
                for m in range(self.members):
                    core[t, dy, m] = (core[t, dy, m].astype(f32) + self.own(t, dy, m).astype(f32)).astype(bf)
            start(over_y)
            start(over_x)

        def turn():
            arrive(over_y)
            for m in range(half):
                total = core[t, 0, m].astype(f32)
                for s in range(ny - 1):
                    total = total + y1[t, s, m].astype(f32)
                core[t, 0, m] = total.astype(bf)
            start(then_x)
            arrive(over_x)
            for dy in range(ny):
                for m in range(half):
                    total = core[t, dy, half + m, xrows(0), :].astype(f32)
                    for s in range(nx - 1):
                        total = total + x1[t, s, dy, m].astype(f32)
                    core[t, dy, half + m, xrows(0), :] = total.astype(bf)
            start(then_y)

        def send_on():
            arrive(then_x)
            arrive(then_y)
            for m in range(self.members):
                total = core[t, 0, m, xrows(0), :].astype(f32)
                buf, n = (x2, nx - 1) if m < half else (y2, ny - 1)
                for s in range(n):
                    total = total + buf[t, s, m % half].astype(f32)
                self.z_send[t, m] = total.astype(bf)
            start(along)

        return [lambda: start(sent), both_cores, turn, send_on]

    def ending(self):
        place, nz = self.place, self.place.nz
        spots = [
            lambda dy, dx, lo=lo, hi=hi: self.out.at[lo:hi, place.piece(self.rows, dy, dx), :]
            for lo, hi in ((0, self.half), (self.half, self.members))
        ]
        out, *others = spread(place, self.copies, spots)

        def total():
            arrive(self.sums)
            for m in range(self.members):
                total = self.z_send[nz - 1, m].astype(jnp.float32)
                for t in range(nz - 1):
                    total = total + self.z_buf[t, m].astype(jnp.float32)
                self.out[m, place.piece(self.rows, 0, 0), :] = total.astype(jnp.bfloat16)
            out()

        return [total] + others


def small_sum(place, copies, small_ref, out_ref, s_acc, s_buf):
    nz, ny, nx = place.nz, place.ny, place.nx
    stages = ([place.other_core], [place.along_x(s) for s in range(1, nx)],
              [place.along_y(s) for s in range(1, ny)], [place.along_z(s) for s in range(1, nz)])
    firsts = [0, 1, nx, nx + ny - 1]
    sent = [
        [copies.plan(lambda k=k: s_acc.at[k], lambda n=firsts[k] + i: s_buf.at[n], partner) for i, partner in enumerate(partners)]
        for k, partners in enumerate(stages)
    ]

    def add(k):
        arrive(sent[k])
        total = s_acc[k]
        for i in range(len(sent[k])):
            total = total + s_buf[firsts[k] + i]
        return total

    def first():
        if small_ref is not None:
            s_acc[0] = small_ref[...]
        start(sent[0])

    def middle(k):
        s_acc[k + 1] = add(k)
        start(sent[k + 1])

    def last():
        out_ref[...] = add(3)

    return [first] + [functools.partial(middle, k) for k in range(3)] + [last]


def small_scratch(nz, ny, nx, shape):
    return [pltpu.VMEM((4,) + shape, jnp.float32), pltpu.VMEM((nx + ny + nz - 2,) + shape, jnp.float32)]


def reduce_kernel(nz, ny, nx, grad_ref, small_ref, out_ref, small_out_ref, *scratch):
    *buffers, s_acc, s_buf, send_sems, recv_sems = scratch
    place = Place(nz, ny, nx)
    copies = Copies(send_sems, recv_sems)
    place.meet()
    whole = Reduction(place, copies, grad_ref, out_ref, buffers)
    run_staggered([whole.chunk(0), small_sum(place, copies, small_ref, small_out_ref, s_acc, s_buf)]
                  + [whole.chunk(t) for t in range(1, nz)])
    for phase in whole.ending():
        phase()
    copies.finish()


def reduce(grad, small, ny, nx, collective_id):
    nz, members, height, width = grad.shape
    count = Reduction.count(nz, ny, nx) + nx + ny + nz - 2
    return pl.pallas_call(
        functools.partial(reduce_kernel, nz, ny, nx),
        out_shape=(jax.ShapeDtypeStruct((members, height, width), jnp.bfloat16), jax.ShapeDtypeStruct(small.shape, jnp.float32)),
        in_specs=[VMEM, VMEM],
        out_specs=(VMEM, VMEM),
        scratch_shapes=Reduction.scratch(nz, ny, nx, members, height, width) + small_scratch(nz, ny, nx, small.shape) + [
            pltpu.SemaphoreType.DMA((count,)), pltpu.SemaphoreType.DMA((count,)),
        ],
        compiler_params=pltpu.CompilerParams(collective_id=collective_id, has_side_effects=True, vmem_limit_bytes=56 << 20),
        cost_estimate=pl.CostEstimate(flops=0, bytes_accessed=grad.size * 2, transcendentals=0),
    )(grad, small)


HS = 64
LANES = 128
EDGE = 128
TAP = 16
LOG2E = math.log2(math.e)
NT = (((1,), (1,)), ((), ()))
NN = (((1,), (0,)), ((), ()))
TN = (((0,), (0,)), ((), ()))


def dot(a, b, dims=NN):
    return lax.dot_general(a, b, dims, preferred_element_type=jnp.float32)


def spans(first, last, step):
    return [(at, min(step, last - at)) for at in range(first, last, step)]


def earlier(ref, start, size):
    if start == 0:
        rows = jnp.concatenate([jnp.zeros((TAP, LANES), jnp.float32), ref[pl.ds(0, size), :].astype(jnp.float32)], axis=0)
    else:
        rows = ref[pl.ds(start - TAP, size + TAP), :].astype(jnp.float32)
    return [pltpu.roll(rows, i, 0)[TAP:] if i else rows[TAP:] for i in range(3)]


def convolve(linear_ref, kern_ref, member, target_ref, skip, step=256):
    total = linear_ref.shape[0]
    for start, size in spans(skip, total, step):
        taps = earlier(linear_ref, start, size)
        value = sum(kern_ref[3 * member + i:3 * member + i + 1, :] * taps[i] for i in range(3))
        target_ref[pl.ds(start - skip, size), :] = value.astype(jnp.bfloat16)


def convolve_back(grad_ref, linear_ref, kern_ref, member, target_ref, sums_ref, step=256):
    total = linear_ref.shape[0]
    parts = [jnp.zeros((8, LANES), jnp.float32)] * 3
    for start, size in spans(0, total, step):
        rows = grad_ref[pl.ds(start, size + 8), :]
        value = kern_ref[3 * member:3 * member + 1, :] * rows[:size]
        for i in (1, 2):
            value += kern_ref[3 * member + i:3 * member + i + 1, :] * pltpu.roll(rows, size + 8 - i, 0)[:size]
        target_ref[pl.ds(start, size), :] = value.astype(jnp.bfloat16)
        taps = earlier(linear_ref, start, size)
        for i in range(3):
            parts[i] += jnp.sum((rows[:size] * taps[i]).reshape(size // 8, 8, LANES), axis=0)
    for i in range(3):
        sums_ref[3 * member + i:3 * member + i + 1, :] = jnp.sum(parts[i], axis=0, keepdims=True)


def parts_of(rows, shards, at, size, step):
    own = (shards - 1) * rows
    pieces = []
    for hop in range(shards - 1, 0, -1):
        pieces += [(start, n, hop) for start, n in spans(own - hop * rows, own - (hop - 1) * rows, step)]
    pieces += [(start, n, 0) for start, n in spans(own, own + at, step)]
    return pieces + [(own + at, size, None)]


def forward_kernel(
    nz, ny, nx, steps, bq, kc, plan, far_ref, lq_ref, lk_ref, lv_ref, kern_ref, up_ref, down_ref,
    out_ref, mass_ref, up_out_ref, down_out_ref, q_ref, k_ref, v_ref, s0_ref, s1_ref, up_all_ref, down_all_ref,
    send_sems, recv_sems, out_sems,
):
    rows, window = q_ref.shape[0], k_ref.shape[0]
    shards = window // rows
    lane = lax.broadcasted_iota(jnp.int32, (bq, LANES), 1) < HS
    scale = 1.0 / math.sqrt(HS)

    place = Place(nz, ny, nx)
    copies = Copies(send_sems, recv_sems)
    units = up_ref.shape[0]
    share = units // (ny * 2 * nx)

    def spot(ref):
        def at(block, dy, dx):
            return ref.at[pl.ds(pl.multiple_of(block * units, units), units), :].at[place.piece(share, dy, dx), :]
        return at

    begin, tasks = gather_tasks(
        place, copies, [lambda ref=ref: ref.at[place.piece(share, 0, 0), :] for ref in (up_ref, down_ref)],
        [spot(up_all_ref), spot(down_all_ref)])

    def store(step):
        part = pl.ds(pl.multiple_of((place.z - step) % nz * units, units), units)
        pairs = ((up_ref, up_all_ref, up_out_ref), (down_ref, down_all_ref, down_out_ref))
        return [
            pltpu.make_async_copy(whole.at[part, :] if step else own, out.at[part, :], out_sems.at[2 * step + k])
            for k, (own, whole, out) in enumerate(pairs)
        ]

    def and_store(phase, step):
        def both():
            phase()
            start(store(step))
        return both

    @pl.when(pl.program_id(0) == 0)
    def _():
        place.meet()
        begin()
        start(store(0))

    table = Timetable(rows // bq, steps)
    for step, (task, ticks) in enumerate(zip(tasks, plan, strict=True)):
        table.add(task[:-1] + [and_store(task[-1], step + 1)], ticks)

    convolve(lq_ref, kern_ref, 0, q_ref, lq_ref.shape[0] - rows)
    convolve(lk_ref, kern_ref, 1, k_ref, 0)
    convolve(lv_ref, kern_ref, 2, v_ref, 0)

    def block(at):
        query = q_ref[pl.ds(at, bq), :] * jnp.bfloat16(scale)
        zero = jnp.zeros_like(query)
        queries = (jnp.where(lane, query, zero), jnp.where(lane, zero, query))
        stores = (s0_ref, s1_ref)
        peaks = [{}, {}]
        parts = parts_of(rows, shards, at, bq, kc)
        for start, size, hop in parts:
            key = k_ref[pl.ds(start, size), :]
            for h in range(2):
                s = dot(queries[h], key, NT)
                if hop is None:
                    row = lax.broadcasted_iota(jnp.int32, (bq, size), 0)
                    col = lax.broadcasted_iota(jnp.int32, (bq, size), 1)
                    s = jnp.where(col <= row, s, -1e30)
                stores[h][:, pl.ds(start, size)] = s
                top = jnp.max(s, axis=1, keepdims=True)
                group = hop or 0
                peaks[h][group] = jnp.maximum(peaks[h][group], top) if group in peaks[h] else top
        sums = [None, None]
        peak, scaled = [], [{}, {}]
        for h in range(2):
            top = peaks[h][0]
            for hop in range(1, shards):
                top = jnp.maximum(top, peaks[h][hop] - far_ref[hop - 1:hop, 0:1])
            peak.append(top)
            scaled[h][0] = top * LOG2E
            for hop in range(1, shards):
                scaled[h][hop] = scaled[h][0] + far_ref[hop - 1:hop, 0:1]
        for start, size, hop in parts:
            value = v_ref[pl.ds(start, size), :]
            wide = lax.broadcasted_iota(jnp.int32, (size, LANES), 1) < HS
            one = jnp.ones_like(value)
            values = (jnp.where(wide, value, one), jnp.where(wide, one, value))
            for h in range(2):
                p = jnp.exp2(stores[h][:, pl.ds(start, size)] * LOG2E - scaled[h][hop or 0]).astype(jnp.bfloat16)
                o = dot(p, values[h])
                sums[h] = o if sums[h] is None else sums[h] + o
        total = pltpu.roll(jnp.where(lane, sums[1], sums[0]), HS, 1)
        out_ref[pl.ds(at, bq), :] = (jnp.where(lane, sums[0], sums[1]) / total).astype(out_ref.dtype)
        mass = jnp.where(lane, peak[0], peak[1]) + jnp.log(total)
        mass = mass.T
        mass_ref[0, 0:1, pl.ds(at, bq)] = mass[0:1]
        mass_ref[0, 1:2, pl.ds(at, bq)] = mass[HS:HS + 1]

    for slot, at in enumerate(range(0, rows, bq)):
        table.tick(slot)
        block(at)

    @pl.when(pl.program_id(0) == steps - 1)
    def _():
        table.finish()
        for step in range(nz):
            for copy in store(step):
                copy.wait()
        copies.finish()


def column(n):
    return pl.BlockSpec((n, LANES), lambda i: (0, i))


ANY = pl.BlockSpec(memory_space=pl.ANY)
WHOLE = pl.BlockSpec((8, LANES), lambda i: (0, 0))


def attention_forward(far, late, linear_k, linear_v, kern, up, down, rows, nz, ny, nx):
    edged, width = late.shape
    window = linear_k.shape[0]
    pairs = width // LANES
    bq = min(512, rows)
    units, depth = up.shape
    bf = jnp.bfloat16
    count = gather_count(nz, ny, nx)
    slots = rows // bq
    first = [round(3.6 * (s + 1)) for s in range(nz - 1)]
    plan = [(f, f + 4, f + 6, f + 7) for f in first]
    return pl.pallas_call(
        functools.partial(forward_kernel, nz, ny, nx, pairs, bq, 512, plan),
        out_shape=(jax.ShapeDtypeStruct((rows, width), bf), jax.ShapeDtypeStruct((pairs, 8, rows), jnp.float32),
                   jax.ShapeDtypeStruct((nz * units, depth), bf), jax.ShapeDtypeStruct((nz * units, depth), bf)),
        grid=(pairs,),
        in_specs=[WHOLE, column(edged), column(window), column(window), column(16), VMEM, VMEM],
        out_specs=[column(rows), pl.BlockSpec((1, 8, rows), lambda i: (i, 0, 0)), ANY, ANY],
        scratch_shapes=[
            pltpu.VMEM((rows, LANES), bf), pltpu.VMEM((window, LANES), bf), pltpu.VMEM((window, LANES), bf),
            pltpu.VMEM((bq, window), jnp.float32), pltpu.VMEM((bq, window), jnp.float32),
            pltpu.VMEM((nz * units, depth), bf), pltpu.VMEM((nz * units, depth), bf),
            pltpu.SemaphoreType.DMA((count,)), pltpu.SemaphoreType.DMA((count,)), pltpu.SemaphoreType.DMA((2 * nz,)),
        ],
        compiler_params=pltpu.CompilerParams(collective_id=1, has_side_effects=True, vmem_limit_bytes=56 << 20),
    )(far, late, linear_k, linear_v, kern, up, down)


def backward_kernel(
    nz, ny, nx, steps, bq, kc, plan, far_ref, lq_ref, lk_ref, lv_ref, kern_ref, g_ref, o_ref, mass_ref, grad_ref, small_ref,
    gq_ref, gk_ref, gv_ref, sums_ref, total_ref, small_out_ref,
    q_ref, k_ref, v_ref, kt_ref, dq_ref, dk_ref, dv_ref, *scratch,
):
    rows, window = q_ref.shape[0], k_ref.shape[0]
    shards = window // rows
    edge = lq_ref.shape[0] - rows
    lane = lax.broadcasted_iota(jnp.int32, (bq, LANES), 1) < HS
    scale = 1.0 / math.sqrt(HS)

    *buffers, s_acc, s_buf, sum_ref, send_sems, recv_sems, out_sem = scratch
    place = Place(nz, ny, nx)
    copies = Copies(send_sems, recv_sems)

    @pl.when(pl.program_id(0) == 0)
    def _():
        place.meet()

    whole = Reduction(place, copies, grad_ref, sum_ref, buffers)
    table = Timetable(rows // bq, steps)
    chunk_plan, small_plan, ending_plan = plan
    for t, ticks in enumerate(chunk_plan):
        table.add(whole.chunk(t), ticks)
    table.add(small_sum(place, copies, small_ref, small_out_ref, s_acc, s_buf), small_plan)
    table.add(whole.ending(), ending_plan)

    convolve(lq_ref, kern_ref, 0, q_ref, edge)
    convolve(lk_ref, kern_ref, 1, k_ref, 0)
    convolve(lv_ref, kern_ref, 2, v_ref, 0)
    dk_ref[...] = jnp.zeros_like(dk_ref)
    dv_ref[...] = jnp.zeros_like(dv_ref)
    if edge:
        dq_ref[pl.ds(0, edge), :] = jnp.zeros((edge, LANES), jnp.float32)
    dq_ref[pl.ds(edge + rows, 8), :] = jnp.zeros((8, LANES), jnp.float32)
    kt_ref[...] = k_ref[...].astype(jnp.float32).T.astype(jnp.bfloat16)

    def block(at):
        query = q_ref[pl.ds(at, bq), :] * jnp.bfloat16(scale)
        grad = g_ref[pl.ds(at, bq), :]
        zero = jnp.zeros_like(query)
        queries = (jnp.where(lane, query, zero), jnp.where(lane, zero, query))
        grads = (jnp.where(lane, grad, zero), jnp.where(lane, zero, grad))
        product = (grad.astype(jnp.float32) * o_ref[pl.ds(at, bq), :].astype(jnp.float32)).T
        query_grads = [jnp.zeros((HS, bq), jnp.float32)] * 2
        deltas = [jnp.sum(product[h * HS:(h + 1) * HS], axis=0, keepdims=True) for h in range(2)]
        masses = [mass_ref[0, h:h + 1, pl.ds(at, bq)] * LOG2E for h in range(2)]
        for start, size, hop in parts_of(rows, shards, at, bq, kc):
            key = k_ref[pl.ds(start, size), :]
            value = v_ref[pl.ds(start, size), :]
            key_part = value_part = None
            for h in range(2):
                s = dot(key, queries[h], NT)
                if hop is None:
                    row = lax.broadcasted_iota(jnp.int32, (size, bq), 1)
                    col = lax.broadcasted_iota(jnp.int32, (size, bq), 0)
                    s = jnp.where(col <= row, s, -1e30)
                mass = masses[h] + far_ref[hop - 1:hop, 0:1] if hop else masses[h]
                p = jnp.exp2(s * LOG2E - mass)
                dp = dot(value, grads[h], NT)
                ds = (p * (dp - deltas[h])).astype(jnp.bfloat16)
                a = dot(p.astype(jnp.bfloat16), grads[h])
                b = dot(ds, queries[h])
                value_part = a if value_part is None else value_part + a
                key_part = b if key_part is None else key_part + b
                query_grads[h] += dot(kt_ref[h * HS:(h + 1) * HS, pl.ds(start, size)], ds)
            dk_ref[pl.ds(start, size), :] += key_part
            dv_ref[pl.ds(start, size), :] += value_part
        dq_ref[pl.ds(edge + at, bq), :] = jnp.concatenate(query_grads, axis=0).T * scale

    for slot, at in enumerate(range(0, rows, bq)):
        table.tick(slot)
        block(at)

    sums_ref[...] = jnp.zeros_like(sums_ref)
    convolve_back(dq_ref, lq_ref, kern_ref, 0, gq_ref, sums_ref)
    convolve_back(dk_ref, lk_ref, kern_ref, 1, gk_ref, sums_ref)
    convolve_back(dv_ref, lv_ref, kern_ref, 2, gv_ref, sums_ref)

    @pl.when(pl.program_id(0) == steps - 1)
    def _():
        table.finish()
        out = pltpu.make_async_copy(sum_ref, total_ref, out_sem)
        out.start()
        copies.finish()
        out.wait()


def attention_backward(far, late, linear_k, linear_v, kern, grads, outs, mass, ff_grad, small, ny, nx):
    rows = grads.shape[0]
    edged, width = late.shape
    window = linear_k.shape[0]
    pairs = width // LANES
    bq = min(256, rows)
    bf = jnp.bfloat16
    nz, members, height, columns = ff_grad.shape
    count = Reduction.count(nz, ny, nx) + nx + ny + nz - 2
    ticks = pairs * (rows // bq)
    gap = max(1, ticks // 2 // nz)
    chunks = [(gap * t, gap * t + 3, gap * t + 7, gap * t + 10) for t in range(nz)]
    end = max(chunks[-1][-1] + 1, ticks - 5)
    plan = (chunks, range(2, 12, 2), (end, end + 4, end + 6, end + 7))
    return pl.pallas_call(
        functools.partial(backward_kernel, nz, ny, nx, pairs, bq, 1024, plan),
        out_shape=(jax.ShapeDtypeStruct((edged, width), bf), jax.ShapeDtypeStruct((window, width), bf),
                   jax.ShapeDtypeStruct((window, width), bf), jax.ShapeDtypeStruct((16, width), jnp.float32),
                   jax.ShapeDtypeStruct((members, height, columns), bf), jax.ShapeDtypeStruct(small.shape, jnp.float32)),
        grid=(pairs,),
        in_specs=[WHOLE, column(edged), column(window), column(window), column(16), column(rows), column(rows),
                  pl.BlockSpec((1, 8, rows), lambda i: (i, 0, 0)), VMEM, VMEM],
        out_specs=[column(edged), column(window), column(window), column(16), ANY, VMEM],
        scratch_shapes=[
            pltpu.VMEM((rows, LANES), bf), pltpu.VMEM((window, LANES), bf), pltpu.VMEM((window, LANES), bf),
            pltpu.VMEM((LANES, window), bf), pltpu.VMEM((edged + 8, LANES), jnp.float32),
            pltpu.VMEM((window + 8, LANES), jnp.float32), pltpu.VMEM((window + 8, LANES), jnp.float32),
        ] + Reduction.scratch(nz, ny, nx, members, height, columns) + small_scratch(nz, ny, nx, small.shape) + [
            pltpu.VMEM((members, height, columns), bf),
            pltpu.SemaphoreType.DMA((count,)), pltpu.SemaphoreType.DMA((count,)), pltpu.SemaphoreType.DMA,
        ],
        compiler_params=pltpu.CompilerParams(collective_id=2, has_side_effects=True, vmem_limit_bytes=60 << 20),
    )(far, late, linear_k, linear_v, kern, grads, outs, mass, ff_grad, small)


class TailReduction(Reduction):
    def __init__(self, place, copies, lefts, rights, send_ref, out_ref, buffers, shape):
        self.place, self.copies, self.out = place, copies, out_ref
        self.core, self.y1, self.x1, self.x2, self.y2, self.z_send, self.z_buf = buffers
        self.lefts, self.rights, self.send = lefts, rights, send_ref
        self.members, self.height, self.width = shape
        self.half = self.members // 2
        self.rows = self.height // (place.ny * 2 * place.nx)
        self.sums = []

    def product(self, t, dy, m, core):
        block = (self.place.z + 1 + t) % self.place.nz
        columns = pl.ds(pl.multiple_of(block * self.width, self.width), self.width)
        left, first = self.lefts[m]
        return dot(left[self.place.band(self.rows, dy, core), first:], self.rights[m][:, columns])

    def source(self, t, dy):
        return self.send.at[t, dy]

    def own(self, t, dy, m):
        return self.product(t, dy, m, 0)

    def fill(self, t):
        for dy in range(self.place.ny):
            for m in range(self.members):
                self.send[t, dy, m] = self.product(t, dy, m, 1).astype(jnp.bfloat16)


def tail_kernel(
    nz, ny, nx, rows, shards, far_ref, gain_ref, sums_ref, gq_in, gk_in, gv_in, window_in, turned_in, low_turned_in,
    attended_in, weight_in, low_in, input_in, out_ref, small_out_ref, grad_out_ref, *scratch,
):
    (gq, gk, gv, window, turned, low_turned, attended, weight, low, own_input, partial, far_send, far_came, send,
     *buffers, s_acc, s_buf, load_sems, send_sems, recv_sems) = scratch
    place = Place(nz, ny, nx)
    copies = Copies(send_sems, recv_sems)
    edge = gq.shape[0] - rows
    window_rows = window.shape[0]
    f32, bf = jnp.float32, jnp.bfloat16
    loads = {}
    for n, (source, target) in enumerate((
        (gk_in, gk), (weight_in.at[1:3], weight.at[1:3]), (gv_in, gv), (window_in, window), (gq_in, gq),
        (weight_in.at[0:1], weight.at[0:1]), (turned_in, turned), (low_turned_in, low_turned), (attended_in, attended),
        (low_in, low), (input_in, own_input),
    )):
        loads[n] = pltpu.make_async_copy(source, target, load_sems.at[n])
        loads[n].start()

    step = min(256, rows)
    whole = TailReduction(
        place, copies, [(turned, window_rows - rows - edge), (turned, 0), (turned, 0), (low_turned, 0)],
        [gq, gk, gv, attended], send, out_ref, buffers, out_ref.shape)
    chunks = [whole.chunk(t) for t in range(nz)]
    ending = whole.ending()
    small = small_sum(place, copies, None, small_out_ref, s_acc, s_buf)
    backs = {
        (hop, at): copies.plan(
            lambda hop=hop, at=at: far_send.at[hop - 1, at:at + step, :], lambda hop=hop, at=at: far_came.at[hop - 1, at:at + step, :],
            place.along_z(-hop))
        for hop in range(1, shards) for at in range(0, rows, step)
    }
    place.meet()

    gains = [jnp.zeros((8, window.shape[1]), f32)]

    def normed_rows(at):
        part = dot(gk[at:at + step, :], weight[1], NT) + dot(gv[at:at + step, :], weight[2], NT)
        first = at - (window_rows - rows - edge)
        if first >= 0:
            part = part + dot(gq[first:first + step, :], weight[0], NT)
        elif first + step > 0:
            query = dot(gq[0:first + step, :], weight[0], NT)
            part = part + jnp.concatenate([jnp.zeros((-first, part.shape[1]), f32), query], axis=0)
        product = part * window[at:at + step, :].astype(f32)
        gains[0] = gains[0] + jnp.sum(product.reshape(step // 8, 8, -1), axis=0)
        return part

    for n in range(6):
        loads[n].wait()
    for hop in range(shards - 1, 0, -1):
        keep = jnp.where(far_ref[hop - 1:hop, 0:1] > 0, 0.0, 1.0)
        for at in range(0, rows, step):
            part = normed_rows(window_rows - (hop + 1) * rows + at) * keep
            far_send[hop - 1, at:at + step, :] = part.astype(bf)
            backs[hop, at].start()

    def own_rows(at):
        partial[at:at + step, :] = normed_rows(window_rows - rows + at).astype(bf)

    def begin(t):
        whole.fill(t)
        chunks[t][0]()

    for n in range(6, 9):
        loads[n].wait()
    owned = list(range(0, rows, step))
    for tick in range(nz + 3):
        for t in range(nz):
            if 0 <= tick - t < 4:
                if tick == t:
                    begin(t)
                else:
                    chunks[t][tick - t]()
        if tick and owned:
            own_rows(owned.pop(0))
    while owned:
        own_rows(owned.pop(0))
    s_acc[0] = sums_ref[...]
    s_acc[0, 9:10, :] = jnp.sum(gains[0], axis=0, keepdims=True)
    small[0]()
    ending[0]()
    small[1]()
    loads[9].wait()
    loads[10].wait()
    for copy in backs.values():
        copy.wait_recv()
    small[2]()
    gain = gain_ref[0:1, :]
    for at in range(0, rows, step):
        values = own_input[at:at + step, :].astype(f32)
        upstream = partial[at:at + step, :].astype(f32)
        for hop in range(1, shards):
            upstream = upstream + far_came[hop - 1, at:at + step, :].astype(f32)
        factor = lax.rsqrt(jnp.mean(values * values, axis=-1, keepdims=True) + EPSILON)
        unit = values * factor
        scaled = gain * upstream
        back = factor * (scaled - unit * jnp.mean(scaled * unit, axis=-1, keepdims=True))
        grad_out_ref[at:at + step, :] = (low[at:at + step, :].astype(f32) + back).astype(bf)
    small[3]()
    ending[1]()
    small[4]()
    ending[2]()
    ending[3]()
    copies.finish()


def tail(far, gain, sums, grads, window, turned, low_turned, attended, weight, low, own_input, rows, nz, ny, nx):
    grad_q, grad_k, grad_v = grads
    window_rows, depth = window.shape
    shards = window_rows // rows
    width = depth // nz
    members, bf = 4, jnp.bfloat16
    band = nx * (depth // (ny * 2 * nx))
    step = min(256, rows)
    count = Reduction.count(nz, ny, nx) + nx + ny + nz - 2 + (shards - 1) * (rows // step)
    buffers = [pltpu.VMEM(t.shape, bf) for t in (grad_q, grad_k, grad_v, window, turned, low_turned, attended)]
    hops = max(1, shards - 1)
    return pl.pallas_call(
        functools.partial(tail_kernel, nz, ny, nx, rows, shards),
        out_shape=(jax.ShapeDtypeStruct((members, depth, width), bf), jax.ShapeDtypeStruct(sums.shape, jnp.float32),
                   jax.ShapeDtypeStruct((rows, depth), bf)),
        in_specs=[VMEM, VMEM, VMEM] + [ANY] * 10,
        out_specs=(VMEM, VMEM, VMEM),
        scratch_shapes=buffers + [
            pltpu.VMEM((3, depth, depth), bf), pltpu.VMEM((rows, depth), bf), pltpu.VMEM((rows, depth), bf),
            pltpu.VMEM((rows, depth), bf), pltpu.VMEM((hops, rows, depth), bf), pltpu.VMEM((hops, rows, depth), bf),
            pltpu.VMEM((nz, ny, members, band, width), bf),
        ] + Reduction.scratch(nz, ny, nx, members, depth, width) + small_scratch(nz, ny, nx, sums.shape) + [
            pltpu.SemaphoreType.DMA((11,)), pltpu.SemaphoreType.DMA((count,)), pltpu.SemaphoreType.DMA((count,)),
        ],
        compiler_params=pltpu.CompilerParams(collective_id=3, has_side_effects=True, vmem_limit_bytes=62 << 20),
        cost_estimate=pl.CostEstimate(flops=24 << 30, bytes_accessed=60 << 20, transcendentals=0),
    )(far, gain, sums, grad_q, grad_k, grad_v, window, turned, low_turned, attended, weight, low, own_input)


def feed_forward_kernel(
    normed_ref, normed_t_ref, grad_ref, grad_t_ref, up_ref, down_ref, bias_ref, weights_ref, bias_grad_ref, normed_grad_ref, out_ref,
):
    @pl.when(pl.program_id(0) == 0)
    def _():
        normed_grad_ref[...] = jnp.zeros_like(normed_grad_ref)
        out_ref[...] = jnp.zeros_like(out_ref)

    bf = jnp.bfloat16
    gate = jnp.maximum(dot(up_ref[...], normed_t_ref[...]) + bias_ref[...], 0.0)
    activation = (gate * gate).astype(bf)
    gate_grad = (2.0 * gate * dot(down_ref[...], grad_t_ref[...])).astype(bf)
    weights_ref[0, 0] = dot(gate_grad, normed_ref[...]).astype(bf)
    weights_ref[0, 1] = dot(activation, grad_ref[...]).astype(bf)
    total = jnp.sum(gate_grad.astype(jnp.float32), axis=1, keepdims=True)
    bias_grad_ref[...] = jnp.broadcast_to(total, bias_grad_ref.shape)
    normed_grad_ref[...] += dot(gate_grad, up_ref[...], TN)
    out_ref[...] += dot(activation, down_ref[...], TN)


def feed_forward(normed, grad, up_rows, down_rows, bias, nz):
    rows, depth = normed.shape
    units = up_rows.shape[0] // nz
    step = min(1024, units)
    per = units // step
    whole = lambda shape: pl.BlockSpec(shape, lambda i: (0, 0))
    block = pl.BlockSpec((step, depth), lambda i: (i, 0))
    f32, bf = jnp.float32, jnp.bfloat16
    return pl.pallas_call(
        feed_forward_kernel,
        out_shape=(jax.ShapeDtypeStruct((nz, 2, units, depth), bf), jax.ShapeDtypeStruct((nz * units, LANES), f32),
                   jax.ShapeDtypeStruct((rows, depth), f32), jax.ShapeDtypeStruct((rows, depth), f32)),
        grid=(nz * per,),
        in_specs=[whole((rows, depth)), whole((depth, rows)), whole((rows, depth)), whole((depth, rows)), block, block,
                  pl.BlockSpec((step, 1), lambda i: (i, 0))],
        out_specs=[pl.BlockSpec((1, 2, step, depth), lambda i: (i // per, 0, i % per, 0)),
                   pl.BlockSpec((step, LANES), lambda i: (i, 0)), whole((rows, depth)), whole((rows, depth))],
        compiler_params=pltpu.CompilerParams(vmem_limit_bytes=56 << 20),
        cost_estimate=pl.CostEstimate(flops=12 * rows * depth * nz * units, bytes_accessed=48 << 20, transcendentals=0),
    )(normed, normed.T, grad, grad.T, up_rows, down_rows, bias[:, None])


def factor_of(values):
    return lax.rsqrt(jnp.mean(values * values, axis=-1, keepdims=True) + EPSILON)


def norm_backward(values, gain, upstream):
    factor = factor_of(values)
    unit = values * factor
    scaled = gain * upstream
    result = factor * (scaled - unit * jnp.mean(scaled * unit, axis=-1, keepdims=True))
    return result, upstream * unit


def on_device(
    layer_input, lengths, norm1_gain, qkv_weight, kernels, out_weight, out_bias,
    norm2_gain, up_weight, up_bias, down_weight, down_bias, out_grad,
):
    rows = layer_input.shape[1]
    nz, nb, nx = lax.axis_size("head"), lax.axis_size("batch"), lax.axis_size("dp")
    ny = nb // 2
    shards = max(1, LONG // rows)
    place = lax.axis_index("head")
    width = qkv_weight.shape[2]
    hidden_units = up_weight.shape[1]

    first_row = place * rows
    ends = jnp.cumsum(lengths[0])
    begins = jnp.max(jnp.where(ends <= first_row, ends, 0))
    before = ((first_row - begins) // rows).astype(jnp.int32)

    own_float = layer_input[0].astype(jnp.float32)
    cotangent = out_grad[0]
    normed_own = (own_float * factor_of(own_float) * norm1_gain).astype(jnp.bfloat16)
    pieces = [normed_own]
    for hop in range(1, shards):
        came = lax.ppermute(normed_own, "head", [(i, i + hop) for i in range(nz - hop)])
        pieces.insert(0, jnp.where(before >= hop, came, jnp.zeros_like(came)))

    small = jnp.concatenate([kernels.reshape(9, width), up_bias.reshape(-1, width)], axis=0)
    small = jnp.pad(small, ((0, -small.shape[0] % 8), (0, 0)))
    full, small = gather_open(jnp.concatenate([qkv_weight, out_weight.T[None]], axis=0), small, nz, ny, nx)
    kern = jnp.pad(small[:, :9].transpose(1, 0, 2).reshape(9, -1), ((0, 7), (0, 0)))
    up_bias_all = small[:, 9:9 + hidden_units // width].reshape(-1)

    window = jnp.concatenate(pieces, axis=0)
    window_rows = shards * rows
    edge = EDGE if shards > 1 else 0
    late = window[window_rows - rows - edge:]
    linear_q = dot(late, full[0]).astype(jnp.bfloat16)
    linear_k = dot(window, full[1]).astype(jnp.bfloat16)
    linear_v = dot(window, full[2]).astype(jnp.bfloat16)
    hops = jnp.arange(1, 9)[:, None]
    far = jnp.broadcast_to(jnp.where(before >= hops, 0.0, 1e30), (8, LANES)).astype(jnp.float32)
    attended, mass, up_rows, down_rows = attention_forward(
        far, linear_q, linear_k, linear_v, kern, up_weight.T, down_weight, rows, nz, ny, nx)
    hidden = own_float + dot(attended, full[3], NT) + out_bias
    normed_two = (hidden * factor_of(hidden) * norm2_gain).astype(jnp.bfloat16)
    ff_grad, up_bias_sums, normed_two_grad, ff_out = feed_forward(normed_two, cotangent, up_rows, down_rows, up_bias_all, nz)
    layer_output = (hidden + ff_out + down_bias).astype(jnp.bfloat16)
    back_two, gain_rows = norm_backward(hidden, norm2_gain, normed_two_grad)
    hidden_grad = cotangent.astype(jnp.float32) + back_two
    hidden_low = hidden_grad.astype(jnp.bfloat16)
    attended_grad = dot(hidden_low, full[3]).astype(jnp.bfloat16)

    early = jnp.concatenate([
        jnp.sum(gain_rows, axis=0), jnp.sum(hidden_low.astype(jnp.float32), axis=0),
        jnp.sum(cotangent.astype(jnp.float32), axis=0), up_bias_sums[:, 0],
    ]).reshape(-1, 1024)
    early = jnp.pad(early, ((0, -early.shape[0] % 8), (0, 0)))
    grad_q, grad_k, grad_v, kernel_sums, ff_sum, early = attention_backward(
        far, linear_q, linear_k, linear_v, kern, attended_grad, attended, mass, ff_grad, early, ny, nx)
    qkvo_sum, totals, layer_grad = tail(
        far, norm1_gain[None], kernel_sums, (grad_q, grad_k, grad_v), window, window.T, hidden_low.T, attended, full,
        hidden_low, layer_input[0], rows, nz, ny, nx)

    width_all = norm1_gain.shape[0]
    early = early.reshape(-1)
    up_bias_grad = lax.dynamic_slice_in_dim(early[3 * width_all:], place * hidden_units, hidden_units, 0)
    kernels_grad = lax.dynamic_slice_in_dim(totals[:9].reshape(3, 3, -1), place * width, width, 2)
    f32 = jnp.float32
    return (
        layer_output[None], layer_grad[None], totals[9] / norm1_gain, qkvo_sum[:3].astype(f32), kernels_grad,
        qkvo_sum[3].T.astype(f32), early[width_all:2 * width_all], early[:width_all], ff_sum[0].T.astype(f32),
        up_bias_grad, ff_sum[1].astype(f32), early[2 * width_all:3 * width_all],
    )


def solution(mesh):
    rows = P(("batch", "dp"), "head", None)
    return jax.shard_map(
        on_device,
        mesh=mesh,
        in_specs=(
            rows, P(("batch", "dp"), None), P(), P(None, None, "head"), P(None, None, "head"), P("head", None), P(),
            P(), P(None, "head"), P("head"), P("head", None), P(), rows,
        ),
        out_specs=(
            rows, rows, P(), P(None, None, "head"), P(None, None, "head"), P("head", None),
            P(), P(), P(None, "head"), P("head"), P("head", None), P(),
        ),
        check_vma=False,
    )
```

```python
import functools
import math

import jax
import jax.numpy as jnp
from jax import lax
from jax.experimental import pallas as pl
from jax.experimental.pallas import tpu as pltpu
from jax.sharding import PartitionSpec as P

LONG = 2048
EPSILON = 1e-06
ALL = ("head", "batch", "dp")

MESH = pl.DeviceIdType.MESH
VMEM = pl.BlockSpec(memory_space=pltpu.VMEM)


class Copy:
    def __init__(self, source, target, device, send_sem, recv_sem):
        self.parts = source, target, device, send_sem, recv_sem

    def make(self):
        source, target, device, send_sem, recv_sem = self.parts
        return pltpu.make_async_remote_copy(
            src_ref=source(), dst_ref=target(), send_sem=send_sem(), recv_sem=recv_sem(), device_id=device(), device_id_type=MESH)

    def start(self):
        self.make().start()

    def wait_recv(self):
        self.make().wait_recv()

    def wait_send(self):
        self.make().wait_send()


class Copies:
    def __init__(self, send_sems, recv_sems):
        self.send_sems, self.recv_sems, self.made = send_sems, recv_sems, []

    def plan(self, source, target, device):
        n = len(self.made)
        copy = Copy(source, target, device, lambda: self.send_sems.at[n], lambda: self.recv_sems.at[n])
        self.made.append(copy)
        return copy

    def finish(self):
        for copy in self.made:
            copy.wait_send()


def start(copies):
    for copy in copies:
        copy.start()


def arrive(copies):
    for copy in copies:
        copy.wait_recv()


class Place:
    def __init__(self, nz, ny, nx):
        self.nz, self.ny, self.nx = nz, ny, nx
        self.z, batch, self.x = lax.axis_index("head"), lax.axis_index("batch"), lax.axis_index("dp")
        self.y, self.c = batch // 2, batch % 2

    def along_z(self, step):
        return lambda: {"head": (self.z + step) % self.nz}

    def along_y(self, step):
        return lambda: {"batch": (self.y + step) % self.ny * 2 + self.c}

    def along_x(self, step):
        return lambda: {"dp": (self.x + step) % self.nx}

    def other_core(self):
        return {"batch": self.y * 2 + 1 - self.c}

    def meet(self):
        partners = [self.along_z(s) for s in range(1, self.nz)]
        partners += [self.along_y(s) for s in range(1, self.ny)] + [self.along_x(s) for s in range(1, self.nx)]
        partners.append(self.other_core)
        barrier = pltpu.get_barrier_semaphore()
        for partner in partners:
            pl.semaphore_signal(barrier, inc=1, device_id=partner(), device_id_type=MESH)
        pl.semaphore_wait(barrier, len(partners))

    def band(self, rows, dy, core=0):
        size = self.nx * rows
        core = self.c if core == 0 else 1 - self.c
        return pl.ds(pl.multiple_of(((self.y - dy) % self.ny * 2 + core) * size, size), size)

    def piece(self, rows, dy, dx):
        if dx is None:
            return self.band(rows, dy)
        at = ((self.y - dy) % self.ny * 2 + self.c) * self.nx + (self.x - dx) % self.nx
        return pl.ds(pl.multiple_of(at * rows, rows), rows)


def spread(place, copies, spots):
    ny, nx = place.ny, place.nx

    def plan(spot, dy, dx, device):
        part = lambda: spot(dy, dx)
        return copies.plan(part, part, device)

    over_x = [[plan(spot, 0, 0, place.along_x(s)) for s in range(1, nx)] for spot in spots]
    over_y = [[plan(spot, 0, 0, place.along_y(t)) for t in range(1, ny)] for spot in spots]
    corner_y = [plan(spots[0], 0, s, place.along_y(t)) for s in range(1, nx) for t in range(1, ny)]
    corner_x = [plan(spots[1], t, 0, place.along_x(s)) for s in range(1, nx) for t in range(1, ny)]
    cores = [plan(spot, dy, None, place.other_core) for spot in spots for dy in range(ny)]

    def out():
        for k in (0, 1):
            start(over_x[k])
            start(over_y[k])

    def turn():
        arrive(over_x[0])
        start(corner_y)
        arrive(over_y[1])
        start(corner_x)
        arrive(over_x[1])
        arrive(over_y[0])

    def cross():
        arrive(corner_y)
        arrive(corner_x)
        start(cores)

    return [out, turn, cross, lambda: arrive(cores)]


def spread_count(ny, nx):
    return 2 * ((nx - 1) + (ny - 1) + (nx - 1) * (ny - 1) + ny)


def gather_tasks(place, copies, shards, fulls):
    nz = place.nz

    def part(k, step):
        return lambda: fulls[k]((place.z - step) % nz, 0, 0)

    rings = [
        [copies.plan(part(k, step) if step else shards[k], part(k, step), place.along_z(1)) for k in range(2)]
        for step in range(nz - 1)
    ]

    def task(step):
        spots = [lambda dy, dx, k=k: fulls[k]((place.z - 1 - step) % nz, dy, dx) for k in range(2)]
        out, *others = spread(place, copies, spots)

        def arrival():
            arrive(rings[step])
            if step < nz - 2:
                start(rings[step + 1])
            out()

        return [arrival] + others

    return lambda: start(rings[0]), [task(step) for step in range(nz - 1)]


def gather_count(nz, ny, nx):
    return (nz - 1) * (2 + spread_count(ny, nx))


def run_staggered(tasks):
    phases = [(at + n, n, phase) for n, task in enumerate(tasks) for at, phase in enumerate(task)]
    for _, _, phase in sorted(phases, key=lambda entry: entry[:2]):
        phase()


class Timetable:
    def __init__(self, per_step, steps):
        self.per_step, self.steps, self.at = per_step, steps, {}

    def add(self, task, times):
        for time, phase in zip(times, task, strict=True):
            self.at.setdefault(time, []).append(phase)

    def tick(self, slot):
        for time in range(slot, self.per_step * self.steps, self.per_step):
            if time in self.at:
                @pl.when(pl.program_id(0) == time // self.per_step)
                def _():
                    for phase in self.at[time]:
                        phase()

    def finish(self):
        for time in sorted(self.at):
            if time >= self.per_step * self.steps:
                for phase in self.at[time]:
                    phase()


def open_kernel(nz, ny, nx, shard_ref, small_ref, full_ref, all_ref, send_sems, recv_sems):
    place = Place(nz, ny, nx)
    copies = Copies(send_sems, recv_sems)
    members, height, width = shard_ref.shape
    half = members // 2
    rows = height // (ny * 2 * nx)

    def columns(block):
        return pl.ds(pl.multiple_of(block * width, width), width)

    fulls = [
        lambda block, dy, dx, lo=lo, hi=hi: full_ref.at[lo:hi, place.piece(rows, dy, dx), columns(block)]
        for lo, hi in ((0, half), (half, members))
    ]
    shards = [lambda lo=lo, hi=hi: shard_ref.at[lo:hi, place.piece(rows, 0, 0), :] for lo, hi in ((0, half), (half, members))]
    begin, tasks = gather_tasks(place, copies, shards, fulls)
    small = [copies.plan(lambda: small_ref, lambda: all_ref.at[place.z], place.along_z(s)) for s in range(1, nz)]
    place.meet()
    begin()
    start(small)
    all_ref[place.z] = small_ref[...]
    for m in range(members):
        full_ref[m, :, columns(place.z)] = shard_ref[m]
    run_staggered(tasks)
    arrive(small)
    copies.finish()


def gather_open(shard, small, nz, ny, nx):
    members, height, width = shard.shape
    count = gather_count(nz, ny, nx) + nz - 1
    return pl.pallas_call(
        functools.partial(open_kernel, nz, ny, nx),
        out_shape=(jax.ShapeDtypeStruct((members, height, width * nz), shard.dtype),
                   jax.ShapeDtypeStruct((nz,) + small.shape, small.dtype)),
        in_specs=[VMEM, VMEM],
        out_specs=(VMEM, VMEM),
        scratch_shapes=[pltpu.SemaphoreType.DMA((count,)), pltpu.SemaphoreType.DMA((count,))],
        compiler_params=pltpu.CompilerParams(collective_id=0, has_side_effects=True, vmem_limit_bytes=48 << 20),
        cost_estimate=pl.CostEstimate(flops=0, bytes_accessed=2 * members * height * width * nz * 2, transcendentals=0),
    )(shard, small)


class Reduction:
    def __init__(self, place, copies, grad_ref, out_ref, buffers):
        self.place, self.copies, self.grad, self.out = place, copies, grad_ref, out_ref
        self.core, self.y1, self.x1, self.x2, self.y2, self.z_send, self.z_buf = buffers
        self.members, self.height, self.width = grad_ref.shape[1:]
        self.half = self.members // 2
        self.rows = self.height // (place.ny * 2 * place.nx)
        self.sums = []

    @staticmethod
    def scratch(nz, ny, nx, members, height, width):
        half, rows, bf = members // 2, height // (ny * 2 * nx), jnp.bfloat16
        band = nx * rows
        return [
            pltpu.VMEM((nz, ny, members, band, width), bf),
            pltpu.VMEM((nz, ny - 1, half, band, width), bf),
            pltpu.VMEM((nz, nx - 1, ny, half, rows, width), bf),
            pltpu.VMEM((nz, nx - 1, half, rows, width), bf),
            pltpu.VMEM((nz, ny - 1, half, rows, width), bf),
            pltpu.VMEM((nz, members, rows, width), bf),
            pltpu.VMEM((nz - 1, members, rows, width), bf),
        ]

    @staticmethod
    def count(nz, ny, nx):
        return nz * (ny + 2 * (ny - 1) + 2 * (nx - 1)) + nz - 1 + spread_count(ny, nx)

    def source(self, t, dy):
        return self.grad.at[(self.place.z + 1 + t) % self.place.nz, :, self.place.band(self.rows, dy, 1), :]

    def own(self, t, dy, m):
        return self.grad[(self.place.z + 1 + t) % self.place.nz, m, self.place.band(self.rows, dy), :]

    def chunk(self, t):
        place, copies, half, rows = self.place, self.copies, self.half, self.rows
        ny, nx, nz = place.ny, place.nx, place.nz
        core, x1, y1, x2, y2, f32, bf = self.core, self.x1, self.y1, self.x2, self.y2, jnp.float32, jnp.bfloat16

        def xrows(step):
            return pl.ds(pl.multiple_of((place.x + step) % nx * rows, rows), rows)

        sent = [
            copies.plan(
                lambda dy=dy: self.source(t, dy),
                lambda dy=dy: core.at[t, dy], place.other_core)
            for dy in range(ny)
        ]
        over_y = [
            copies.plan(lambda s=s: core.at[t, ny - s, 0:half], lambda s=s: y1.at[t, s - 1], place.along_y(s))
            for s in range(1, ny)
        ]
        over_x = [
            copies.plan(lambda s=s: core.at[t, :, half:, xrows(s), :], lambda s=s: x1.at[t, s - 1], place.along_x(s))
            for s in range(1, nx)
        ]
        then_x = [
            copies.plan(lambda s=s: core.at[t, 0, 0:half, xrows(s), :], lambda s=s: x2.at[t, s - 1], place.along_x(s))
            for s in range(1, nx)
        ]
        then_y = [
            copies.plan(lambda s=s: core.at[t, ny - s, half:, xrows(0), :], lambda s=s: y2.at[t, s - 1], place.along_y(s))
            for s in range(1, ny)
        ]
        along = [copies.plan(lambda: self.z_send.at[t], lambda: self.z_buf.at[t], place.along_z(1 + t))] if t < nz - 1 else []
        self.sums += along

        def both_cores():
            arrive(sent)
            for dy in range(ny):
                for m in range(self.members):
                    core[t, dy, m] = (core[t, dy, m].astype(f32) + self.own(t, dy, m).astype(f32)).astype(bf)
            start(over_y)
            start(over_x)

        def turn():
            arrive(over_y)
            for m in range(half):
                total = core[t, 0, m].astype(f32)
                for s in range(ny - 1):
                    total = total + y1[t, s, m].astype(f32)
                core[t, 0, m] = total.astype(bf)
            start(then_x)
            arrive(over_x)
            for dy in range(ny):
                for m in range(half):
                    total = core[t, dy, half + m, xrows(0), :].astype(f32)
                    for s in range(nx - 1):
                        total = total + x1[t, s, dy, m].astype(f32)
                    core[t, dy, half + m, xrows(0), :] = total.astype(bf)
            start(then_y)

        def send_on():
            arrive(then_x)
            arrive(then_y)
            for m in range(self.members):
                total = core[t, 0, m, xrows(0), :].astype(f32)
                buf, n = (x2, nx - 1) if m < half else (y2, ny - 1)
                for s in range(n):
                    total = total + buf[t, s, m % half].astype(f32)
                self.z_send[t, m] = total.astype(bf)
            start(along)

        return [lambda: start(sent), both_cores, turn, send_on]

    def ending(self):
        place, nz = self.place, self.place.nz
        spots = [
            lambda dy, dx, lo=lo, hi=hi: self.out.at[lo:hi, place.piece(self.rows, dy, dx), :]
            for lo, hi in ((0, self.half), (self.half, self.members))
        ]
        out, *others = spread(place, self.copies, spots)

        def total():
            arrive(self.sums)
            for m in range(self.members):
                total = self.z_send[nz - 1, m].astype(jnp.float32)
                for t in range(nz - 1):
                    total = total + self.z_buf[t, m].astype(jnp.float32)
                self.out[m, place.piece(self.rows, 0, 0), :] = total.astype(jnp.bfloat16)
            out()

        return [total] + others


def small_sum(place, copies, small_ref, out_ref, s_acc, s_buf):
    nz, ny, nx = place.nz, place.ny, place.nx
    stages = ([place.other_core], [place.along_x(s) for s in range(1, nx)],
              [place.along_y(s) for s in range(1, ny)], [place.along_z(s) for s in range(1, nz)])
    firsts = [0, 1, nx, nx + ny - 1]
    sent = [
        [copies.plan(lambda k=k: s_acc.at[k], lambda n=firsts[k] + i: s_buf.at[n], partner) for i, partner in enumerate(partners)]
        for k, partners in enumerate(stages)
    ]

    def add(k):
        arrive(sent[k])
        total = s_acc[k]
        for i in range(len(sent[k])):
            total = total + s_buf[firsts[k] + i]
        return total

    def first():
        if small_ref is not None:
            s_acc[0] = small_ref[...]
        start(sent[0])

    def middle(k):
        s_acc[k + 1] = add(k)
        start(sent[k + 1])

    def last():
        out_ref[...] = add(3)

    return [first] + [functools.partial(middle, k) for k in range(3)] + [last]


def small_scratch(nz, ny, nx, shape):
    return [pltpu.VMEM((4,) + shape, jnp.float32), pltpu.VMEM((nx + ny + nz - 2,) + shape, jnp.float32)]


def reduce_kernel(nz, ny, nx, grad_ref, small_ref, out_ref, small_out_ref, *scratch):
    *buffers, s_acc, s_buf, send_sems, recv_sems = scratch
    place = Place(nz, ny, nx)
    copies = Copies(send_sems, recv_sems)
    place.meet()
    whole = Reduction(place, copies, grad_ref, out_ref, buffers)
    run_staggered([whole.chunk(0), small_sum(place, copies, small_ref, small_out_ref, s_acc, s_buf)]
                  + [whole.chunk(t) for t in range(1, nz)])
    for phase in whole.ending():
        phase()
    copies.finish()


def reduce(grad, small, ny, nx, collective_id):
    nz, members, height, width = grad.shape
    count = Reduction.count(nz, ny, nx) + nx + ny + nz - 2
    return pl.pallas_call(
        functools.partial(reduce_kernel, nz, ny, nx),
        out_shape=(jax.ShapeDtypeStruct((members, height, width), jnp.bfloat16), jax.ShapeDtypeStruct(small.shape, jnp.float32)),
        in_specs=[VMEM, VMEM],
        out_specs=(VMEM, VMEM),
        scratch_shapes=Reduction.scratch(nz, ny, nx, members, height, width) + small_scratch(nz, ny, nx, small.shape) + [
            pltpu.SemaphoreType.DMA((count,)), pltpu.SemaphoreType.DMA((count,)),
        ],
        compiler_params=pltpu.CompilerParams(collective_id=collective_id, has_side_effects=True, vmem_limit_bytes=56 << 20),
        cost_estimate=pl.CostEstimate(flops=0, bytes_accessed=grad.size * 2, transcendentals=0),
    )(grad, small)


HS = 64
LANES = 128
EDGE = 128
TAP = 16
LOG2E = math.log2(math.e)
NT = (((1,), (1,)), ((), ()))
NN = (((1,), (0,)), ((), ()))
TN = (((0,), (0,)), ((), ()))


def dot(a, b, dims=NN):
    return lax.dot_general(a, b, dims, preferred_element_type=jnp.float32)


def spans(first, last, step):
    return [(at, min(step, last - at)) for at in range(first, last, step)]


def earlier(ref, start, size):
    if start == 0:
        rows = jnp.concatenate([jnp.zeros((TAP, LANES), jnp.float32), ref[pl.ds(0, size), :].astype(jnp.float32)], axis=0)
    else:
        rows = ref[pl.ds(start - TAP, size + TAP), :].astype(jnp.float32)
    return [pltpu.roll(rows, i, 0)[TAP:] if i else rows[TAP:] for i in range(3)]


def convolve(linear_ref, kern_ref, member, target_ref, skip, step=256):
    total = linear_ref.shape[0]
    for start, size in spans(skip, total, step):
        taps = earlier(linear_ref, start, size)
        value = sum(kern_ref[3 * member + i:3 * member + i + 1, :] * taps[i] for i in range(3))
        target_ref[pl.ds(start - skip, size), :] = value.astype(jnp.bfloat16)


def convolve_back(grad_ref, linear_ref, kern_ref, member, target_ref, sums_ref, step=256):
    total = linear_ref.shape[0]
    parts = [jnp.zeros((8, LANES), jnp.float32)] * 3
    for start, size in spans(0, total, step):
        rows = grad_ref[pl.ds(start, size + 8), :]
        value = kern_ref[3 * member:3 * member + 1, :] * rows[:size]
        for i in (1, 2):
            value += kern_ref[3 * member + i:3 * member + i + 1, :] * pltpu.roll(rows, size + 8 - i, 0)[:size]
        target_ref[pl.ds(start, size), :] = value.astype(jnp.bfloat16)
        taps = earlier(linear_ref, start, size)
        for i in range(3):
            parts[i] += jnp.sum((rows[:size] * taps[i]).reshape(size // 8, 8, LANES), axis=0)
    for i in range(3):
        sums_ref[3 * member + i:3 * member + i + 1, :] = jnp.sum(parts[i], axis=0, keepdims=True)


def parts_of(rows, shards, at, size, step):
    own = (shards - 1) * rows
    pieces = []
    for hop in range(shards - 1, 0, -1):
        pieces += [(start, n, hop) for start, n in spans(own - hop * rows, own - (hop - 1) * rows, step)]
    pieces += [(start, n, 0) for start, n in spans(own, own + at, step)]
    return pieces + [(own + at, size, None)]


def column(n):
    return pl.BlockSpec((n, LANES), lambda i: (0, i))


ANY = pl.BlockSpec(memory_space=pl.ANY)
WHOLE = pl.BlockSpec((8, LANES), lambda i: (0, 0))


def backward_kernel(
    nz, ny, nx, steps, bq, kc, plan, far_ref, lq_ref, lk_ref, lv_ref, kern_ref, g_ref, o_ref, mass_ref, grad_ref, small_ref,
    gq_ref, gk_ref, gv_ref, sums_ref, total_ref, small_out_ref,
    q_ref, k_ref, v_ref, kt_ref, dq_ref, dk_ref, dv_ref, *scratch,
):
    rows, window = q_ref.shape[0], k_ref.shape[0]
    shards = window // rows
    edge = lq_ref.shape[0] - rows
    lane = lax.broadcasted_iota(jnp.int32, (bq, LANES), 1) < HS
    scale = 1.0 / math.sqrt(HS)

    *buffers, s_acc, s_buf, sum_ref, send_sems, recv_sems, out_sem = scratch
    place = Place(nz, ny, nx)
    copies = Copies(send_sems, recv_sems)

    @pl.when(pl.program_id(0) == 0)
    def _():
        place.meet()

    whole = Reduction(place, copies, grad_ref, sum_ref, buffers)
    table = Timetable(rows // bq, steps)
    chunk_plan, small_plan, ending_plan = plan
    for t, ticks in enumerate(chunk_plan):
        table.add(whole.chunk(t), ticks)
    table.add(small_sum(place, copies, small_ref, small_out_ref, s_acc, s_buf), small_plan)
    table.add(whole.ending(), ending_plan)

    convolve(lq_ref, kern_ref, 0, q_ref, edge)
    convolve(lk_ref, kern_ref, 1, k_ref, 0)
    convolve(lv_ref, kern_ref, 2, v_ref, 0)
    dk_ref[...] = jnp.zeros_like(dk_ref)
    dv_ref[...] = jnp.zeros_like(dv_ref)
    if edge:
        dq_ref[pl.ds(0, edge), :] = jnp.zeros((edge, LANES), jnp.float32)
    dq_ref[pl.ds(edge + rows, 8), :] = jnp.zeros((8, LANES), jnp.float32)
    kt_ref[...] = k_ref[...].astype(jnp.float32).T.astype(jnp.bfloat16)

    def block(at):
        query = q_ref[pl.ds(at, bq), :] * jnp.bfloat16(scale)
        grad = g_ref[pl.ds(at, bq), :]
        zero = jnp.zeros_like(query)
        queries = (jnp.where(lane, query, zero), jnp.where(lane, zero, query))
        grads = (jnp.where(lane, grad, zero), jnp.where(lane, zero, grad))
        product = (grad.astype(jnp.float32) * o_ref[pl.ds(at, bq), :].astype(jnp.float32)).T
        query_grads = [jnp.zeros((HS, bq), jnp.float32)] * 2
        deltas = [jnp.sum(product[h * HS:(h + 1) * HS], axis=0, keepdims=True) for h in range(2)]
        masses = [mass_ref[0, h:h + 1, pl.ds(at, bq)] * LOG2E for h in range(2)]
        for start, size, hop in parts_of(rows, shards, at, bq, kc):
            key = k_ref[pl.ds(start, size), :]
            value = v_ref[pl.ds(start, size), :]
            key_part = value_part = None
            for h in range(2):
                s = dot(key, queries[h], NT)
                if hop is None:
                    row = lax.broadcasted_iota(jnp.int32, (size, bq), 1)
                    col = lax.broadcasted_iota(jnp.int32, (size, bq), 0)
                    s = jnp.where(col <= row, s, -1e30)
                mass = masses[h] + far_ref[hop - 1:hop, 0:1] if hop else masses[h]
                p = jnp.exp2(s * LOG2E - mass)
                dp = dot(value, grads[h], NT)
                ds = (p * (dp - deltas[h])).astype(jnp.bfloat16)
                a = dot(p.astype(jnp.bfloat16), grads[h])
                b = dot(ds, queries[h])
                value_part = a if value_part is None else value_part + a
                key_part = b if key_part is None else key_part + b
                query_grads[h] += dot(kt_ref[h * HS:(h + 1) * HS, pl.ds(start, size)], ds)
            dk_ref[pl.ds(start, size), :] += key_part
            dv_ref[pl.ds(start, size), :] += value_part
        dq_ref[pl.ds(edge + at, bq), :] = jnp.concatenate(query_grads, axis=0).T * scale

    for slot, at in enumerate(range(0, rows, bq)):
        table.tick(slot)
        block(at)

    sums_ref[...] = jnp.zeros_like(sums_ref)
    convolve_back(dq_ref, lq_ref, kern_ref, 0, gq_ref, sums_ref)
    convolve_back(dk_ref, lk_ref, kern_ref, 1, gk_ref, sums_ref)
    convolve_back(dv_ref, lv_ref, kern_ref, 2, gv_ref, sums_ref)

    @pl.when(pl.program_id(0) == steps - 1)
    def _():
        table.finish()
        out = pltpu.make_async_copy(sum_ref, total_ref, out_sem)
        out.start()
        copies.finish()
        out.wait()


def attention_backward(far, late, linear_k, linear_v, kern, grads, outs, mass, ff_grad, small, ny, nx):
    rows = grads.shape[0]
    edged, width = late.shape
    window = linear_k.shape[0]
    pairs = width // LANES
    bq = min(256, rows)
    bf = jnp.bfloat16
    nz, members, height, columns = ff_grad.shape
    count = Reduction.count(nz, ny, nx) + nx + ny + nz - 2
    ticks = pairs * (rows // bq)
    gap = max(1, ticks // 2 // nz)
    chunks = [(gap * t, gap * t + 3, gap * t + 7, gap * t + 10) for t in range(nz)]
    end = max(chunks[-1][-1] + 1, ticks - 5)
    plan = (chunks, range(2, 12, 2), (end, end + 4, end + 6, end + 7))
    return pl.pallas_call(
        functools.partial(backward_kernel, nz, ny, nx, pairs, bq, 1024, plan),
        out_shape=(jax.ShapeDtypeStruct((edged, width), bf), jax.ShapeDtypeStruct((window, width), bf),
                   jax.ShapeDtypeStruct((window, width), bf), jax.ShapeDtypeStruct((16, width), jnp.float32),
                   jax.ShapeDtypeStruct((members, height, columns), bf), jax.ShapeDtypeStruct(small.shape, jnp.float32)),
        grid=(pairs,),
        in_specs=[WHOLE, column(edged), column(window), column(window), column(16), column(rows), column(rows),
                  pl.BlockSpec((1, 8, rows), lambda i: (i, 0, 0)), VMEM, VMEM],
        out_specs=[column(edged), column(window), column(window), column(16), ANY, VMEM],
        scratch_shapes=[
            pltpu.VMEM((rows, LANES), bf), pltpu.VMEM((window, LANES), bf), pltpu.VMEM((window, LANES), bf),
            pltpu.VMEM((LANES, window), bf), pltpu.VMEM((edged + 8, LANES), jnp.float32),
            pltpu.VMEM((window + 8, LANES), jnp.float32), pltpu.VMEM((window + 8, LANES), jnp.float32),
        ] + Reduction.scratch(nz, ny, nx, members, height, columns) + small_scratch(nz, ny, nx, small.shape) + [
            pltpu.VMEM((members, height, columns), bf),
            pltpu.SemaphoreType.DMA((count,)), pltpu.SemaphoreType.DMA((count,)), pltpu.SemaphoreType.DMA,
        ],
        compiler_params=pltpu.CompilerParams(collective_id=2, has_side_effects=True, vmem_limit_bytes=60 << 20),
    )(far, late, linear_k, linear_v, kern, grads, outs, mass, ff_grad, small)


def taps_of(rows, size):
    return [pltpu.roll(rows, i, 0)[TAP:TAP + size] if i else rows[TAP:TAP + size] for i in range(3)]


def front_kernel(
    nz, ny, nx, shards, bq, kc, far_ref, gain_ref, small_ref, shard_ref, input_ref, up_ref, down_ref,
    out_ref, mass_ref, small_out_ref, full_out, window_out, lq_out, lk_out, lv_out, up_out, down_out,
    full, window, lq, lk, lv, small_all, q_ref, k_ref, v_ref, s0_ref, s1_ref, acc_ref, total_ref, peak_ref,
    send_sems, recv_sems, out_sems,
):
    rows, depth = input_ref.shape
    window_rows = window.shape[0]
    own = window_rows - rows
    edge = lq.shape[0] - rows
    members, _, width = shard_ref.shape
    per = width // LANES
    half = members // 2
    share = depth // (ny * 2 * nx)
    units = up_ref.shape[0]
    part = units // (ny * 2 * nx)
    step_at = pl.program_id(0)
    f32, bf = jnp.float32, jnp.bfloat16
    scale = 1.0 / math.sqrt(HS)
    lane = lax.broadcasted_iota(jnp.int32, (bq, LANES), 1) < HS

    place = Place(nz, ny, nx)
    copies = Copies(send_sems, recv_sems)

    def columns(block, size=width, first=0):
        return pl.ds(pl.multiple_of(block * width + first, LANES), size)

    begin, tasks = gather_tasks(
        place, copies,
        [lambda lo=lo, hi=hi: shard_ref.at[lo:hi, place.piece(share, 0, 0), :] for lo, hi in ((0, half), (half, members))],
        [lambda block, dy, dx, lo=lo, hi=hi: full.at[lo:hi, place.piece(share, dy, dx), columns(block)]
         for lo, hi in ((0, half), (half, members))])
    smalls = [copies.plan(lambda: small_ref, lambda: small_all.at[place.z], place.along_z(s)) for s in range(1, nz)]

    def rows_to(hop, at, size):
        return copies.plan(
            lambda: window.at[pl.ds(own + at, size), :], lambda: window.at[pl.ds(own - hop * rows + at, size), :],
            place.along_z(hop))

    near = [rows_to(1, rows - edge, edge)] if shards > 1 else []
    distant = []
    for hop in range(1, shards):
        distant += [rows_to(hop, at, size) for at, size in spans(0, rows - (edge if hop == 1 else 0), 256)]

    def spot(ref):
        return lambda block, dy, dx: ref.at[pl.ds(pl.multiple_of(block * units, units), units), :].at[place.piece(part, dy, dx), :]

    ff_begin, ff_tasks = gather_tasks(
        place, copies, [lambda ref=ref: ref.at[place.piece(part, 0, 0), :] for ref in (up_ref, down_ref)],
        [spot(up_out), spot(down_out)])

    def local(n, source, target):
        return pltpu.make_async_copy(source, target, out_sems.at[n])

    def stores(which):
        mine = pl.ds(pl.multiple_of(place.z * units, units), units)
        return {
            "units": lambda: [local(0, up_ref, up_out.at[mine, :]), local(1, down_ref, down_out.at[mine, :])],
            "full": lambda: [local(2, full, full_out)],
            "window": lambda: [local(3, window, window_out)],
            "linear": lambda: [local(4, lq, lq_out), local(5, lk, lk_out), local(6, lv, lv_out)],
        }[which]()

    def keep_valid(hop, first, size):
        for at, n in spans(first, first + size, 256):
            at_rows = pl.ds(own - hop * rows + at, n)
            window[at_rows, :] = jnp.where(far_ref[hop - 1:hop, 0:1] > 0, jnp.zeros((n, depth), bf), window[at_rows, :])

    @pl.when(step_at == 0)
    def _():
        for at, size in spans(0, rows, 256):
            values = input_ref[at:at + size, :].astype(f32)
            factor = lax.rsqrt(jnp.mean(values * values, axis=-1, keepdims=True) + EPSILON)
            window[pl.ds(own + at, size), :] = (values * factor * gain_ref[0:1, :]).astype(bf)
        small_all[place.z] = small_ref[...]
        place.meet()
        start(near)
        begin()
        start(smalls)
        start(stores("units"))
        for m in range(members):
            full[m, :, columns(place.z)] = shard_ref[m]
        arrive(near)
        if shards > 1:
            keep_valid(1, rows - edge, edge)

    def all_rows():
        arrive(distant)
        for hop in range(1, shards):
            keep_valid(hop, 0, rows - (edge if hop == 1 else 0))
        start(stores("window"))

    slots = per + 1
    table = Timetable(slots, 2 * nz)
    for s, (arrival, turn, cross, done) in enumerate(tasks):
        table.add([arrival, turn], (slots * s if s else 1, slots * s + (1 if s else per)))
    for s, (arrival, turn, cross, done) in enumerate(tasks):
        table.add([cross, done], (slots * (s + 1), slots * (s + 1)))
    for s in range(nz - 1):
        waiting = distant[s:s + 1] if s < nz - 2 else distant[s:]
        table.add([lambda waiting=waiting: start(waiting)], [slots * s if s else 1])
    table.add([lambda: arrive(smalls)], [slots])
    table.add([lambda: start(stores("full")), all_rows], [slots * (nz - 1), slots * nz])
    table.add([ff_begin], [slots * nz - 1])
    for s, task in enumerate(ff_tasks):
        first = slots * nz + 3 * (s + 1) - 1
        table.add(task, (first, first + 3, first + 5, first + 6))

    relative = step_at % nz
    block = (place.z - relative) % nz

    def filtered(source, member, target, first, size, source_first, p):
        lanes = columns(block, LANES, p * LANES)
        for at, n in spans(first, first + size, 256):
            inside = at - source_first
            if inside == 0:
                rows_in = source[pl.ds(0, n), lanes].astype(f32)
                rows_in = jnp.concatenate([jnp.zeros((TAP, LANES), f32), rows_in], axis=0)
            else:
                rows_in = source[pl.ds(inside - TAP, n + TAP), lanes].astype(f32)
            taps = taps_of(rows_in, n)
            value = sum(small_all[block, 3 * member + i:3 * member + i + 1, p * LANES:(p + 1) * LANES] * taps[i] for i in range(3))
            target(at, n, value.astype(bf))

    def into(ref, shift=0):
        def put(at, n, value):
            ref[pl.ds(at - shift, n), :] = value
        return put

    def queries_of(at):
        query = q_ref[pl.ds(at, bq), :] * jnp.bfloat16(scale)
        zero = jnp.zeros_like(query)
        return jnp.where(lane, query, zero), jnp.where(lane, zero, query)

    def scores(queries, parts, shift):
        peaks = [{}, {}]
        for start_at, size, hop in parts:
            key = k_ref[pl.ds(start_at, size), :]
            for h, store in enumerate((s0_ref, s1_ref)):
                s = dot(queries[h], key, NT)
                if hop is None:
                    row = lax.broadcasted_iota(jnp.int32, (bq, size), 0)
                    col = lax.broadcasted_iota(jnp.int32, (bq, size), 1)
                    s = jnp.where(col <= row, s, -1e30)
                store[:, pl.ds(start_at - shift, size)] = s
                top = jnp.max(s, axis=1, keepdims=True)
                group = hop or 0
                peaks[h][group] = jnp.maximum(peaks[h][group], top) if group in peaks[h] else top
        return peaks

    def weighted(parts, shift, bases):
        sums = [None, None]
        for start_at, size, hop in parts:
            value = v_ref[pl.ds(start_at, size), :]
            wide = lax.broadcasted_iota(jnp.int32, (size, LANES), 1) < HS
            one = jnp.ones_like(value)
            values = (jnp.where(wide, value, one), jnp.where(wide, one, value))
            for h, store in enumerate((s0_ref, s1_ref)):
                p = jnp.exp2(store[:, pl.ds(start_at - shift, size)] * LOG2E - bases[h][hop or 0]).astype(bf)
                o = dot(p, values[h])
                sums[h] = o if sums[h] is None else sums[h] + o
        return jnp.where(lane, sums[0], sums[1]), pltpu.roll(jnp.where(lane, sums[1], sums[0]), HS, 1)

    def finish_rows(p, at, acc, total, peak):
        out_ref[pl.ds(at, bq), columns(block, LANES, p * LANES)] = (acc / total).astype(bf)
        mass = (peak + jnp.log(total)).T
        mass_ref[block * per + p, 0:1, pl.ds(at, bq)] = mass[0:1]
        mass_ref[block * per + p, 1:2, pl.ds(at, bq)] = mass[HS:HS + 1]

    def linear(target, member, first, last, target_first):
        for at, n in spans(first, last, 256):
            value = dot(window[pl.ds(at, n), :], full[member, :, columns(block)])
            target[pl.ds(at - target_first, n), columns(block)] = value.astype(bf)

    table.tick(0)

    @pl.when(step_at < nz)
    def _():
        linear(lq, 0, own - edge, window_rows, own - edge)
        linear(lk, 1, own - edge, window_rows, 0)
        linear(lv, 2, own - edge, window_rows, 0)

    @pl.when(step_at >= nz)
    def _():
        if shards > 1:
            linear(lk, 1, 0, own - edge, 0)
            linear(lv, 2, 0, own - edge, 0)

    for p in range(per):
        state = relative * per + p

        @pl.when(step_at < nz)
        def _():
            filtered(lq, 0, into(q_ref, own), own, rows, own - edge, p)
            filtered(lk, 1, into(k_ref), own, rows, 0, p)
            filtered(lv, 2, into(v_ref), own, rows, 0, p)
            for at in range(0, rows, bq):
                parts = [(start_at, n, 0) for start_at, n in spans(own, own + at, kc)] + [(own + at, bq, None)]
                peaks = scores(queries_of(at), parts, own)
                acc, total = weighted(parts, own, [{0: peaks[h][0] * LOG2E} for h in range(2)])
                here = pl.ds(at, bq)
                peak = jnp.where(lane, peaks[0][0], peaks[1][0])
                if shards > 1:
                    acc_ref[state, here, :] = acc
                    total_ref[state, here, :] = total
                    peak_ref[state, here, :] = peak
                else:
                    finish_rows(p, at, acc, total, peak)

        if shards > 1:
            @pl.when(step_at >= nz)
            def _():
                filtered(lq, 0, into(q_ref, own), own, rows, own - edge, p)
                filtered(lk, 1, into(k_ref), 0, own, 0, p)
                filtered(lv, 2, into(v_ref), 0, own, 0, p)
                for at in range(0, rows, bq):
                    here = pl.ds(at, bq)
                    parts = []
                    for hop in range(shards - 1, 0, -1):
                        parts += [(s, n, hop) for s, n in spans(own - hop * rows, own - (hop - 1) * rows, kc)]
                    peaks = scores(queries_of(at), parts, 0)
                    old = peak_ref[state, here, :]
                    tops, bases = [], []
                    for h in range(2):
                        top = old[:, h * HS:h * HS + 1]
                        for hop in range(1, shards):
                            top = jnp.maximum(top, peaks[h][hop] - far_ref[hop - 1:hop, 0:1])
                        tops.append(top)
                        bases.append({hop: top * LOG2E + far_ref[hop - 1:hop, 0:1] for hop in range(1, shards)})
                    acc, total = weighted(parts, 0, bases)
                    peak = jnp.where(lane, tops[0], tops[1])
                    fade = jnp.exp2((old - peak) * LOG2E)
                    finish_rows(p, at, acc_ref[state, here, :] * fade + acc, total_ref[state, here, :] * fade + total, peak)

        table.tick(p + 1)

    @pl.when(step_at == 2 * nz - 1)
    def _():
        start(stores("linear"))
        small_out_ref[...] = small_all[...]
        table.finish()
        for which in ("units", "full", "window", "linear"):
            for copy in stores(which):
                copy.wait()
        copies.finish()


def front(far, gain, small, shard, layer_input, up, down, nz, ny, nx, shards):
    rows, depth = layer_input.shape
    members, _, width = shard.shape
    window_rows = shards * rows
    edge = EDGE if shards > 1 else 0
    pairs = depth // LANES
    units = up.shape[0]
    bq = min(512, rows)
    f32, bf = jnp.float32, jnp.bfloat16
    sent = sum(len(spans(0, rows - (edge if hop == 1 else 0), 256)) for hop in range(1, shards)) + (1 if shards > 1 else 0)
    count = 2 * gather_count(nz, ny, nx) + nz - 1 + sent
    store = pltpu.VMEM((bq, max(rows, window_rows - rows)), f32)
    state = pltpu.VMEM((pairs, rows, LANES), f32)
    return pl.pallas_call(
        functools.partial(front_kernel, nz, ny, nx, shards, bq, 512),
        out_shape=(
            jax.ShapeDtypeStruct((rows, depth), bf), jax.ShapeDtypeStruct((pairs, 8, rows), f32),
            jax.ShapeDtypeStruct((nz,) + small.shape, f32), jax.ShapeDtypeStruct((members, depth, depth), bf),
            jax.ShapeDtypeStruct((window_rows, depth), bf), jax.ShapeDtypeStruct((rows + edge, depth), bf),
            jax.ShapeDtypeStruct((window_rows, depth), bf), jax.ShapeDtypeStruct((window_rows, depth), bf),
            jax.ShapeDtypeStruct((nz * units, depth), bf), jax.ShapeDtypeStruct((nz * units, depth), bf),
        ),
        grid=(2 * nz,),
        in_specs=[VMEM] * 7,
        out_specs=[VMEM] * 3 + [ANY] * 7,
        scratch_shapes=[
            pltpu.VMEM((members, depth, depth), bf), pltpu.VMEM((window_rows, depth), bf),
            pltpu.VMEM((rows + edge, depth), bf), pltpu.VMEM((window_rows, depth), bf), pltpu.VMEM((window_rows, depth), bf),
            pltpu.VMEM((nz,) + small.shape, f32),
            pltpu.VMEM((rows, LANES), bf), pltpu.VMEM((window_rows, LANES), bf), pltpu.VMEM((window_rows, LANES), bf),
            store, store, state, state, state,
            pltpu.SemaphoreType.DMA((count,)), pltpu.SemaphoreType.DMA((count,)), pltpu.SemaphoreType.DMA((7,)),
        ],
        compiler_params=pltpu.CompilerParams(collective_id=0, has_side_effects=True, vmem_limit_bytes=62 << 20),
        cost_estimate=pl.CostEstimate(flops=30 << 30, bytes_accessed=60 << 20, transcendentals=0),
    )(far, gain, small, shard, layer_input, up, down)


class TailReduction(Reduction):
    def __init__(self, place, copies, lefts, rights, send_ref, out_ref, buffers, shape):
        self.place, self.copies, self.out = place, copies, out_ref
        self.core, self.y1, self.x1, self.x2, self.y2, self.z_send, self.z_buf = buffers
        self.lefts, self.rights, self.send = lefts, rights, send_ref
        self.members, self.height, self.width = shape
        self.half = self.members // 2
        self.rows = self.height // (place.ny * 2 * place.nx)
        self.sums = []

    def product(self, t, dy, m, core):
        block = (self.place.z + 1 + t) % self.place.nz
        columns = pl.ds(pl.multiple_of(block * self.width, self.width), self.width)
        left, first = self.lefts[m]
        return dot(left[self.place.band(self.rows, dy, core), first:], self.rights[m][:, columns])

    def source(self, t, dy):
        return self.send.at[t, dy]

    def own(self, t, dy, m):
        return self.product(t, dy, m, 0)

    def fill(self, t):
        for dy in range(self.place.ny):
            for m in range(self.members):
                self.send[t, dy, m] = self.product(t, dy, m, 1).astype(jnp.bfloat16)


def tail_kernel(
    nz, ny, nx, rows, shards, far_ref, gain_ref, sums_ref, gq_in, gk_in, gv_in, window_in, turned_in, low_turned_in,
    attended_in, weight_in, low_in, input_in, out_ref, small_out_ref, grad_out_ref, *scratch,
):
    (gq, gk, gv, window, turned, low_turned, attended, weight, low, own_input, partial, far_send, far_came, send,
     *buffers, s_acc, s_buf, load_sems, send_sems, recv_sems) = scratch
    place = Place(nz, ny, nx)
    copies = Copies(send_sems, recv_sems)
    edge = gq.shape[0] - rows
    window_rows = window.shape[0]
    f32, bf = jnp.float32, jnp.bfloat16
    loads = {}
    for n, (source, target) in enumerate((
        (gk_in, gk), (weight_in.at[1:3], weight.at[1:3]), (gv_in, gv), (window_in, window), (gq_in, gq),
        (weight_in.at[0:1], weight.at[0:1]), (turned_in, turned), (low_turned_in, low_turned), (attended_in, attended),
        (low_in, low), (input_in, own_input),
    )):
        loads[n] = pltpu.make_async_copy(source, target, load_sems.at[n])
        loads[n].start()

    step = min(256, rows)
    whole = TailReduction(
        place, copies, [(turned, window_rows - rows - edge), (turned, 0), (turned, 0), (low_turned, 0)],
        [gq, gk, gv, attended], send, out_ref, buffers, out_ref.shape)
    chunks = [whole.chunk(t) for t in range(nz)]
    ending = whole.ending()
    small = small_sum(place, copies, None, small_out_ref, s_acc, s_buf)
    backs = {
        (hop, at): copies.plan(
            lambda hop=hop, at=at: far_send.at[hop - 1, at:at + step, :], lambda hop=hop, at=at: far_came.at[hop - 1, at:at + step, :],
            place.along_z(-hop))
        for hop in range(1, shards) for at in range(0, rows, step)
    }
    place.meet()

    gains = [jnp.zeros((8, window.shape[1]), f32)]

    def normed_rows(at):
        part = dot(gk[at:at + step, :], weight[1], NT) + dot(gv[at:at + step, :], weight[2], NT)
        first = at - (window_rows - rows - edge)
        if first >= 0:
            part = part + dot(gq[first:first + step, :], weight[0], NT)
        elif first + step > 0:
            query = dot(gq[0:first + step, :], weight[0], NT)
            part = part + jnp.concatenate([jnp.zeros((-first, part.shape[1]), f32), query], axis=0)
        product = part * window[at:at + step, :].astype(f32)
        gains[0] = gains[0] + jnp.sum(product.reshape(step // 8, 8, -1), axis=0)
        return part

    for n in range(6):
        loads[n].wait()
    for hop in range(shards - 1, 0, -1):
        keep = jnp.where(far_ref[hop - 1:hop, 0:1] > 0, 0.0, 1.0)
        for at in range(0, rows, step):
            part = normed_rows(window_rows - (hop + 1) * rows + at) * keep
            far_send[hop - 1, at:at + step, :] = part.astype(bf)
            backs[hop, at].start()

    def own_rows(at):
        partial[at:at + step, :] = normed_rows(window_rows - rows + at).astype(bf)

    def begin(t):
        whole.fill(t)
        chunks[t][0]()

    for n in range(6, 9):
        loads[n].wait()
    owned = list(range(0, rows, step))
    for tick in range(nz + 3):
        for t in range(nz):
            if 0 <= tick - t < 4:
                if tick == t:
                    begin(t)
                else:
                    chunks[t][tick - t]()
        if tick and owned:
            own_rows(owned.pop(0))
    while owned:
        own_rows(owned.pop(0))
    s_acc[0] = sums_ref[...]
    s_acc[0, 9:10, :] = jnp.sum(gains[0], axis=0, keepdims=True)
    small[0]()
    ending[0]()
    small[1]()
    loads[9].wait()
    loads[10].wait()
    for copy in backs.values():
        copy.wait_recv()
    small[2]()
    gain = gain_ref[0:1, :]
    for at in range(0, rows, step):
        values = own_input[at:at + step, :].astype(f32)
        upstream = partial[at:at + step, :].astype(f32)
        for hop in range(1, shards):
            upstream = upstream + far_came[hop - 1, at:at + step, :].astype(f32)
        factor = lax.rsqrt(jnp.mean(values * values, axis=-1, keepdims=True) + EPSILON)
        unit = values * factor
        scaled = gain * upstream
        back = factor * (scaled - unit * jnp.mean(scaled * unit, axis=-1, keepdims=True))
        grad_out_ref[at:at + step, :] = (low[at:at + step, :].astype(f32) + back).astype(bf)
    small[3]()
    ending[1]()
    small[4]()
    ending[2]()
    ending[3]()
    copies.finish()


def tail(far, gain, sums, grads, window, turned, low_turned, attended, weight, low, own_input, rows, nz, ny, nx):
    grad_q, grad_k, grad_v = grads
    window_rows, depth = window.shape
    shards = window_rows // rows
    width = depth // nz
    members, bf = 4, jnp.bfloat16
    band = nx * (depth // (ny * 2 * nx))
    step = min(256, rows)
    count = Reduction.count(nz, ny, nx) + nx + ny + nz - 2 + (shards - 1) * (rows // step)
    buffers = [pltpu.VMEM(t.shape, bf) for t in (grad_q, grad_k, grad_v, window, turned, low_turned, attended)]
    hops = max(1, shards - 1)
    return pl.pallas_call(
        functools.partial(tail_kernel, nz, ny, nx, rows, shards),
        out_shape=(jax.ShapeDtypeStruct((members, depth, width), bf), jax.ShapeDtypeStruct(sums.shape, jnp.float32),
                   jax.ShapeDtypeStruct((rows, depth), bf)),
        in_specs=[VMEM, VMEM, VMEM] + [ANY] * 10,
        out_specs=(VMEM, VMEM, VMEM),
        scratch_shapes=buffers + [
            pltpu.VMEM((3, depth, depth), bf), pltpu.VMEM((rows, depth), bf), pltpu.VMEM((rows, depth), bf),
            pltpu.VMEM((rows, depth), bf), pltpu.VMEM((hops, rows, depth), bf), pltpu.VMEM((hops, rows, depth), bf),
            pltpu.VMEM((nz, ny, members, band, width), bf),
        ] + Reduction.scratch(nz, ny, nx, members, depth, width) + small_scratch(nz, ny, nx, sums.shape) + [
            pltpu.SemaphoreType.DMA((11,)), pltpu.SemaphoreType.DMA((count,)), pltpu.SemaphoreType.DMA((count,)),
        ],
        compiler_params=pltpu.CompilerParams(collective_id=3, has_side_effects=True, vmem_limit_bytes=62 << 20),
        cost_estimate=pl.CostEstimate(flops=24 << 30, bytes_accessed=60 << 20, transcendentals=0),
    )(far, gain, sums, grad_q, grad_k, grad_v, window, turned, low_turned, attended, weight, low, own_input)


def feed_forward_kernel(
    normed_ref, normed_t_ref, grad_ref, grad_t_ref, up_ref, down_ref, bias_ref, weights_ref, bias_grad_ref, normed_grad_ref, out_ref,
):
    @pl.when(pl.program_id(0) == 0)
    def _():
        normed_grad_ref[...] = jnp.zeros_like(normed_grad_ref)
        out_ref[...] = jnp.zeros_like(out_ref)

    bf = jnp.bfloat16
    gate = jnp.maximum(dot(up_ref[...], normed_t_ref[...]) + bias_ref[...], 0.0)
    activation = (gate * gate).astype(bf)
    gate_grad = (2.0 * gate * dot(down_ref[...], grad_t_ref[...])).astype(bf)
    weights_ref[0, 0] = dot(gate_grad, normed_ref[...]).astype(bf)
    weights_ref[0, 1] = dot(activation, grad_ref[...]).astype(bf)
    total = jnp.sum(gate_grad.astype(jnp.float32), axis=1, keepdims=True)
    bias_grad_ref[...] = jnp.broadcast_to(total, bias_grad_ref.shape)
    normed_grad_ref[...] += dot(gate_grad, up_ref[...], TN)
    out_ref[...] += dot(activation, down_ref[...], TN)


def feed_forward(normed, grad, up_rows, down_rows, bias, nz):
    rows, depth = normed.shape
    units = up_rows.shape[0] // nz
    step = min(1024, units)
    per = units // step
    whole = lambda shape: pl.BlockSpec(shape, lambda i: (0, 0))
    block = pl.BlockSpec((step, depth), lambda i: (i, 0))
    f32, bf = jnp.float32, jnp.bfloat16
    return pl.pallas_call(
        feed_forward_kernel,
        out_shape=(jax.ShapeDtypeStruct((nz, 2, units, depth), bf), jax.ShapeDtypeStruct((nz * units, LANES), f32),
                   jax.ShapeDtypeStruct((rows, depth), f32), jax.ShapeDtypeStruct((rows, depth), f32)),
        grid=(nz * per,),
        in_specs=[whole((rows, depth)), whole((depth, rows)), whole((rows, depth)), whole((depth, rows)), block, block,
                  pl.BlockSpec((step, 1), lambda i: (i, 0))],
        out_specs=[pl.BlockSpec((1, 2, step, depth), lambda i: (i // per, 0, i % per, 0)),
                   pl.BlockSpec((step, LANES), lambda i: (i, 0)), whole((rows, depth)), whole((rows, depth))],
        compiler_params=pltpu.CompilerParams(vmem_limit_bytes=56 << 20),
        cost_estimate=pl.CostEstimate(flops=12 * rows * depth * nz * units, bytes_accessed=48 << 20, transcendentals=0),
    )(normed, normed.T, grad, grad.T, up_rows, down_rows, bias[:, None])


def factor_of(values):
    return lax.rsqrt(jnp.mean(values * values, axis=-1, keepdims=True) + EPSILON)


def norm_backward(values, gain, upstream):
    factor = factor_of(values)
    unit = values * factor
    scaled = gain * upstream
    result = factor * (scaled - unit * jnp.mean(scaled * unit, axis=-1, keepdims=True))
    return result, upstream * unit


def on_device(
    layer_input, lengths, norm1_gain, qkv_weight, kernels, out_weight, out_bias,
    norm2_gain, up_weight, up_bias, down_weight, down_bias, out_grad,
):
    rows = layer_input.shape[1]
    nz, nb, nx = lax.axis_size("head"), lax.axis_size("batch"), lax.axis_size("dp")
    ny = nb // 2
    shards = max(1, LONG // rows)
    place = lax.axis_index("head")
    width = qkv_weight.shape[2]
    hidden_units = up_weight.shape[1]

    first_row = place * rows
    ends = jnp.cumsum(lengths[0])
    begins = jnp.max(jnp.where(ends <= first_row, ends, 0))
    before = ((first_row - begins) // rows).astype(jnp.int32)

    own_float = layer_input[0].astype(jnp.float32)
    cotangent = out_grad[0]
    hops = jnp.arange(1, 9)[:, None]
    far = jnp.broadcast_to(jnp.where(before >= hops, 0.0, 1e30), (8, LANES)).astype(jnp.float32)
    small = jnp.concatenate([kernels.reshape(9, width), up_bias.reshape(-1, width)], axis=0)
    small = jnp.pad(small, ((0, -small.shape[0] % 8), (0, 0)))
    shard = jnp.concatenate([qkv_weight, out_weight.T[None]], axis=0)
    attended, mass, small, full, window, linear_q, linear_k, linear_v, up_rows, down_rows = front(
        far, norm1_gain[None], small, shard, layer_input[0], up_weight.T, down_weight, nz, ny, nx, shards)
    kern = jnp.pad(small[:, :9].transpose(1, 0, 2).reshape(9, -1), ((0, 7), (0, 0)))
    up_bias_all = small[:, 9:9 + hidden_units // width].reshape(-1)
    hidden = own_float + dot(attended, full[3], NT) + out_bias
    normed_two = (hidden * factor_of(hidden) * norm2_gain).astype(jnp.bfloat16)
    ff_grad, up_bias_sums, normed_two_grad, ff_out = feed_forward(normed_two, cotangent, up_rows, down_rows, up_bias_all, nz)
    layer_output = (hidden + ff_out + down_bias).astype(jnp.bfloat16)
    back_two, gain_rows = norm_backward(hidden, norm2_gain, normed_two_grad)
    hidden_grad = cotangent.astype(jnp.float32) + back_two
    hidden_low = hidden_grad.astype(jnp.bfloat16)
    attended_grad = dot(hidden_low, full[3]).astype(jnp.bfloat16)

    early = jnp.concatenate([
        jnp.sum(gain_rows, axis=0), jnp.sum(hidden_low.astype(jnp.float32), axis=0),
        jnp.sum(cotangent.astype(jnp.float32), axis=0), up_bias_sums[:, 0],
    ]).reshape(-1, 1024)
    early = jnp.pad(early, ((0, -early.shape[0] % 8), (0, 0)))
    grad_q, grad_k, grad_v, kernel_sums, ff_sum, early = attention_backward(
        far, linear_q, linear_k, linear_v, kern, attended_grad, attended, mass, ff_grad, early, ny, nx)
    qkvo_sum, totals, layer_grad = tail(
        far, norm1_gain[None], kernel_sums, (grad_q, grad_k, grad_v), window, window.T, hidden_low.T, attended, full,
        hidden_low, layer_input[0], rows, nz, ny, nx)

    width_all = norm1_gain.shape[0]
    early = early.reshape(-1)
    up_bias_grad = lax.dynamic_slice_in_dim(early[3 * width_all:], place * hidden_units, hidden_units, 0)
    kernels_grad = lax.dynamic_slice_in_dim(totals[:9].reshape(3, 3, -1), place * width, width, 2)
    f32 = jnp.float32
    return (
        layer_output[None], layer_grad[None], totals[9] / norm1_gain, qkvo_sum[:3].astype(f32), kernels_grad,
        qkvo_sum[3].T.astype(f32), early[width_all:2 * width_all], early[:width_all], ff_sum[0].T.astype(f32),
        up_bias_grad, ff_sum[1].astype(f32), early[2 * width_all:3 * width_all],
    )


def solution(mesh):
    rows = P(("batch", "dp"), "head", None)
    return jax.shard_map(
        on_device,
        mesh=mesh,
        in_specs=(
            rows, P(("batch", "dp"), None), P(), P(None, None, "head"), P(None, None, "head"), P("head", None), P(),
            P(), P(None, "head"), P("head"), P("head", None), P(), rows,
        ),
        out_specs=(
            rows, rows, P(), P(None, None, "head"), P(None, None, "head"), P("head", None),
            P(), P(), P(None, "head"), P("head"), P("head", None), P(),
        ),
        check_vma=False,
    )
```

```python
import functools
import math

import jax
import jax.numpy as jnp
from jax import lax
from jax.experimental import pallas as pl
from jax.experimental.pallas import tpu as pltpu
from jax.sharding import PartitionSpec as P

LONG = 2048
EPSILON = 1e-06
ALL = ("head", "batch", "dp")

MESH = pl.DeviceIdType.MESH
VMEM = pl.BlockSpec(memory_space=pltpu.VMEM)


class Copy:
    def __init__(self, source, target, device, send_sem, recv_sem):
        self.parts = source, target, device, send_sem, recv_sem

    def make(self):
        source, target, device, send_sem, recv_sem = self.parts
        return pltpu.make_async_remote_copy(
            src_ref=source(), dst_ref=target(), send_sem=send_sem(), recv_sem=recv_sem(), device_id=device(), device_id_type=MESH)

    def start(self):
        self.make().start()

    def wait_recv(self):
        self.make().wait_recv()

    def wait_send(self):
        self.make().wait_send()


class Copies:
    def __init__(self, send_sems, recv_sems):
        self.send_sems, self.recv_sems, self.made = send_sems, recv_sems, []

    def plan(self, source, target, device):
        n = len(self.made)
        copy = Copy(source, target, device, lambda: self.send_sems.at[n], lambda: self.recv_sems.at[n])
        self.made.append(copy)
        return copy

    def finish(self):
        for copy in self.made:
            copy.wait_send()


def start(copies):
    for copy in copies:
        copy.start()


def arrive(copies):
    for copy in copies:
        copy.wait_recv()


class Place:
    def __init__(self, nz, ny, nx):
        self.nz, self.ny, self.nx = nz, ny, nx
        self.z, batch, self.x = lax.axis_index("head"), lax.axis_index("batch"), lax.axis_index("dp")
        self.y, self.c = batch // 2, batch % 2

    def along_z(self, step):
        return lambda: {"head": (self.z + step) % self.nz}

    def along_y(self, step):
        return lambda: {"batch": (self.y + step) % self.ny * 2 + self.c}

    def along_x(self, step):
        return lambda: {"dp": (self.x + step) % self.nx}

    def other_core(self):
        return {"batch": self.y * 2 + 1 - self.c}

    def meet(self):
        partners = [self.along_z(s) for s in range(1, self.nz)]
        partners += [self.along_y(s) for s in range(1, self.ny)] + [self.along_x(s) for s in range(1, self.nx)]
        partners.append(self.other_core)
        barrier = pltpu.get_barrier_semaphore()
        for partner in partners:
            pl.semaphore_signal(barrier, inc=1, device_id=partner(), device_id_type=MESH)
        pl.semaphore_wait(barrier, len(partners))

    def band(self, rows, dy, core=0):
        size = self.nx * rows
        core = self.c if core == 0 else 1 - self.c
        return pl.ds(pl.multiple_of(((self.y - dy) % self.ny * 2 + core) * size, size), size)

    def piece(self, rows, dy, dx):
        if dx is None:
            return self.band(rows, dy)
        at = ((self.y - dy) % self.ny * 2 + self.c) * self.nx + (self.x - dx) % self.nx
        return pl.ds(pl.multiple_of(at * rows, rows), rows)


def spread(place, copies, spots):
    ny, nx = place.ny, place.nx

    def plan(spot, dy, dx, device):
        part = lambda: spot(dy, dx)
        return copies.plan(part, part, device)

    over_x = [[plan(spot, 0, 0, place.along_x(s)) for s in range(1, nx)] for spot in spots]
    over_y = [[plan(spot, 0, 0, place.along_y(t)) for t in range(1, ny)] for spot in spots]
    corner_y = [plan(spots[0], 0, s, place.along_y(t)) for s in range(1, nx) for t in range(1, ny)]
    corner_x = [plan(spots[1], t, 0, place.along_x(s)) for s in range(1, nx) for t in range(1, ny)]
    cores = [plan(spot, dy, None, place.other_core) for spot in spots for dy in range(ny)]

    def out():
        for k in (0, 1):
            start(over_x[k])
            start(over_y[k])

    def turn():
        arrive(over_x[0])
        start(corner_y)
        arrive(over_y[1])
        start(corner_x)
        arrive(over_x[1])
        arrive(over_y[0])

    def cross():
        arrive(corner_y)
        arrive(corner_x)
        start(cores)

    return [out, turn, cross, lambda: arrive(cores)]


def spread_count(ny, nx):
    return 2 * ((nx - 1) + (ny - 1) + (nx - 1) * (ny - 1) + ny)


def gather_tasks(place, copies, shards, fulls):
    nz = place.nz

    def part(k, step):
        return lambda: fulls[k]((place.z - step) % nz, 0, 0)

    rings = [
        [copies.plan(part(k, step) if step else shards[k], part(k, step), place.along_z(1)) for k in range(2)]
        for step in range(nz - 1)
    ]

    def task(step):
        spots = [lambda dy, dx, k=k: fulls[k]((place.z - 1 - step) % nz, dy, dx) for k in range(2)]
        out, *others = spread(place, copies, spots)

        def arrival():
            arrive(rings[step])
            if step < nz - 2:
                start(rings[step + 1])
            out()

        return [arrival] + others

    return lambda: start(rings[0]), [task(step) for step in range(nz - 1)]


def gather_count(nz, ny, nx):
    return (nz - 1) * (2 + spread_count(ny, nx))


def run_staggered(tasks):
    phases = [(at + n, n, phase) for n, task in enumerate(tasks) for at, phase in enumerate(task)]
    for _, _, phase in sorted(phases, key=lambda entry: entry[:2]):
        phase()


class Timetable:
    def __init__(self, per_step, steps):
        self.per_step, self.steps, self.at = per_step, steps, {}

    def add(self, task, times):
        for time, phase in zip(times, task, strict=True):
            self.at.setdefault(time, []).append(phase)

    def tick(self, slot):
        for time in range(slot, self.per_step * self.steps, self.per_step):
            if time in self.at:
                @pl.when(pl.program_id(0) == time // self.per_step)
                def _():
                    for phase in self.at[time]:
                        phase()

    def finish(self):
        for time in sorted(self.at):
            if time >= self.per_step * self.steps:
                for phase in self.at[time]:
                    phase()


class Reduction:
    def __init__(self, place, copies, grad_ref, out_ref, buffers, own_ref, own_sems):
        self.place, self.copies, self.grad, self.out = place, copies, grad_ref, out_ref
        self.own_ref, self.own_sems = own_ref, own_sems
        self.core, self.y1, self.x1, self.x2, self.y2, self.z_send, self.z_buf = buffers
        self.members, self.height, self.width = grad_ref.shape[1:]
        self.half = self.members // 2
        self.rows = self.height // (place.ny * 2 * place.nx)
        self.sums = []

    @staticmethod
    def scratch(nz, ny, nx, members, height, width):
        half, rows, bf = members // 2, height // (ny * 2 * nx), jnp.bfloat16
        band = nx * rows
        return [
            pltpu.VMEM((nz, ny, members, band, width), bf),
            pltpu.VMEM((nz, ny - 1, half, band, width), bf),
            pltpu.VMEM((nz, nx - 1, ny, half, rows, width), bf),
            pltpu.VMEM((nz, nx - 1, half, rows, width), bf),
            pltpu.VMEM((nz, ny - 1, half, rows, width), bf),
            pltpu.VMEM((nz, members, rows, width), bf),
            pltpu.VMEM((nz - 1, members, rows, width), bf),
        ]

    @staticmethod
    def count(nz, ny, nx):
        return nz * (ny + 2 * (ny - 1) + 2 * (nx - 1)) + nz - 1 + spread_count(ny, nx)

    def source(self, t, dy):
        return self.grad.at[(self.place.z + 1 + t) % self.place.nz, :, self.place.band(self.rows, dy, 1), :]

    def staged(self, t):
        block = (self.place.z + 1 + t) % self.place.nz
        return [
            pltpu.make_async_copy(self.grad.at[block, :, self.place.band(self.rows, dy), :], self.own_ref.at[t, dy], self.own_sems.at[t, dy])
            for dy in range(self.place.ny)
        ]

    def prepare(self, t):
        start(self.staged(t))

    def prepared(self, t):
        for copy in self.staged(t):
            copy.wait()

    def own(self, t, dy, m):
        return self.own_ref[t, dy, m]

    def chunk(self, t):
        place, copies, half, rows = self.place, self.copies, self.half, self.rows
        ny, nx, nz = place.ny, place.nx, place.nz
        core, x1, y1, x2, y2, f32, bf = self.core, self.x1, self.y1, self.x2, self.y2, jnp.float32, jnp.bfloat16

        def xrows(step):
            return pl.ds(pl.multiple_of((place.x + step) % nx * rows, rows), rows)

        sent = [
            copies.plan(
                lambda dy=dy: self.source(t, dy),
                lambda dy=dy: core.at[t, dy], place.other_core)
            for dy in range(ny)
        ]
        over_y = [
            copies.plan(lambda s=s: core.at[t, ny - s, 0:half], lambda s=s: y1.at[t, s - 1], place.along_y(s))
            for s in range(1, ny)
        ]
        over_x = [
            copies.plan(lambda s=s: core.at[t, :, half:, xrows(s), :], lambda s=s: x1.at[t, s - 1], place.along_x(s))
            for s in range(1, nx)
        ]
        then_x = [
            copies.plan(lambda s=s: core.at[t, 0, 0:half, xrows(s), :], lambda s=s: x2.at[t, s - 1], place.along_x(s))
            for s in range(1, nx)
        ]
        then_y = [
            copies.plan(lambda s=s: core.at[t, ny - s, half:, xrows(0), :], lambda s=s: y2.at[t, s - 1], place.along_y(s))
            for s in range(1, ny)
        ]
        along = [copies.plan(lambda: self.z_send.at[t], lambda: self.z_buf.at[t], place.along_z(1 + t))] if t < nz - 1 else []
        self.sums += along

        def first():
            start(sent)
            self.prepare(t)

        def both_cores():
            arrive(sent)
            self.prepared(t)
            for dy in range(ny):
                for m in range(self.members):
                    core[t, dy, m] = (core[t, dy, m].astype(f32) + self.own(t, dy, m).astype(f32)).astype(bf)
            start(over_y)
            start(over_x)

        def turn():
            arrive(over_y)
            for m in range(half):
                total = core[t, 0, m].astype(f32)
                for s in range(ny - 1):
                    total = total + y1[t, s, m].astype(f32)
                core[t, 0, m] = total.astype(bf)
            start(then_x)
            arrive(over_x)
            for dy in range(ny):
                for m in range(half):
                    total = core[t, dy, half + m, xrows(0), :].astype(f32)
                    for s in range(nx - 1):
                        total = total + x1[t, s, dy, m].astype(f32)
                    core[t, dy, half + m, xrows(0), :] = total.astype(bf)
            start(then_y)

        def send_on():
            arrive(then_x)
            arrive(then_y)
            for m in range(self.members):
                total = core[t, 0, m, xrows(0), :].astype(f32)
                buf, n = (x2, nx - 1) if m < half else (y2, ny - 1)
                for s in range(n):
                    total = total + buf[t, s, m % half].astype(f32)
                self.z_send[t, m] = total.astype(bf)
            start(along)

        return [first, both_cores, turn, send_on]

    def ending(self):
        place, nz = self.place, self.place.nz
        spots = [
            lambda dy, dx, lo=lo, hi=hi: self.out.at[lo:hi, place.piece(self.rows, dy, dx), :]
            for lo, hi in ((0, self.half), (self.half, self.members))
        ]
        out, *others = spread(place, self.copies, spots)

        def total():
            arrive(self.sums)
            for m in range(self.members):
                total = self.z_send[nz - 1, m].astype(jnp.float32)
                for t in range(nz - 1):
                    total = total + self.z_buf[t, m].astype(jnp.float32)
                self.out[m, place.piece(self.rows, 0, 0), :] = total.astype(jnp.bfloat16)
            out()

        return [total] + others


def small_sum(place, copies, small_ref, out_ref, s_acc, s_buf):
    nz, ny, nx = place.nz, place.ny, place.nx
    stages = ([place.other_core], [place.along_x(s) for s in range(1, nx)],
              [place.along_y(s) for s in range(1, ny)], [place.along_z(s) for s in range(1, nz)])
    firsts = [0, 1, nx, nx + ny - 1]
    sent = [
        [copies.plan(lambda k=k: s_acc.at[k], lambda n=firsts[k] + i: s_buf.at[n], partner) for i, partner in enumerate(partners)]
        for k, partners in enumerate(stages)
    ]

    def add(k):
        arrive(sent[k])
        total = s_acc[k]
        for i in range(len(sent[k])):
            total = total + s_buf[firsts[k] + i]
        return total

    def first():
        if small_ref is not None:
            s_acc[0] = small_ref[...]
        start(sent[0])

    def middle(k):
        s_acc[k + 1] = add(k)
        start(sent[k + 1])

    def last():
        out_ref[...] = add(3)

    return [first] + [functools.partial(middle, k) for k in range(3)] + [last]


def small_scratch(nz, ny, nx, shape):
    return [pltpu.VMEM((4,) + shape, jnp.float32), pltpu.VMEM((nx + ny + nz - 2,) + shape, jnp.float32)]


HS = 64
LANES = 128
EDGE = 128
TAP = 16
LOG2E = math.log2(math.e)
NT = (((1,), (1,)), ((), ()))
NN = (((1,), (0,)), ((), ()))
TN = (((0,), (0,)), ((), ()))


def dot(a, b, dims=NN):
    return lax.dot_general(a, b, dims, preferred_element_type=jnp.float32)


def spans(first, last, step):
    return [(at, min(step, last - at)) for at in range(first, last, step)]


def earlier(ref, start, size):
    if start == 0:
        rows = jnp.concatenate([jnp.zeros((TAP, LANES), jnp.float32), ref[pl.ds(0, size), :].astype(jnp.float32)], axis=0)
    else:
        rows = ref[pl.ds(start - TAP, size + TAP), :].astype(jnp.float32)
    return [pltpu.roll(rows, i, 0)[TAP:] if i else rows[TAP:] for i in range(3)]


def convolve(linear_ref, kern_ref, member, target_ref, skip, step=256):
    total = linear_ref.shape[0]
    for start, size in spans(skip, total, step):
        taps = earlier(linear_ref, start, size)
        value = sum(kern_ref[3 * member + i:3 * member + i + 1, :] * taps[i] for i in range(3))
        target_ref[pl.ds(start - skip, size), :] = value.astype(jnp.bfloat16)


def convolve_back(grad_ref, linear_ref, kern_ref, member, target_ref, sums_ref, step=256):
    total = linear_ref.shape[0]
    parts = [jnp.zeros((8, LANES), jnp.float32)] * 3
    for start, size in spans(0, total, step):
        rows = grad_ref[pl.ds(start, size + 8), :]
        value = kern_ref[3 * member:3 * member + 1, :] * rows[:size]
        for i in (1, 2):
            value += kern_ref[3 * member + i:3 * member + i + 1, :] * pltpu.roll(rows, size + 8 - i, 0)[:size]
        target_ref[pl.ds(start, size), :] = value.astype(jnp.bfloat16)
        taps = earlier(linear_ref, start, size)
        for i in range(3):
            parts[i] += jnp.sum((rows[:size] * taps[i]).reshape(size // 8, 8, LANES), axis=0)
    for i in range(3):
        sums_ref[3 * member + i:3 * member + i + 1, :] = jnp.sum(parts[i], axis=0, keepdims=True)


def parts_of(rows, shards, at, size, step):
    own = (shards - 1) * rows
    pieces = []
    for hop in range(shards - 1, 0, -1):
        pieces += [(start, n, hop) for start, n in spans(own - hop * rows, own - (hop - 1) * rows, step)]
    pieces += [(start, n, 0) for start, n in spans(own, own + at, step)]
    return pieces + [(own + at, size, None)]


def column(n):
    return pl.BlockSpec((n, LANES), lambda i: (0, i))


ANY = pl.BlockSpec(memory_space=pl.ANY)
WHOLE = pl.BlockSpec((8, LANES), lambda i: (0, 0))


def backward_kernel(
    nz, ny, nx, steps, bq, kc, plan, far_ref, lq_ref, lk_ref, lv_ref, kern_ref, g_ref, o_ref, mass_ref, grad_ref, small_ref,
    gq_ref, gk_ref, gv_ref, sums_ref, up_ref, down_ref, small_out_ref,
    q_ref, k_ref, v_ref, kt_ref, dq_ref, dk_ref, dv_ref, *scratch,
):
    rows, window = q_ref.shape[0], k_ref.shape[0]
    shards = window // rows
    edge = lq_ref.shape[0] - rows
    lane = lax.broadcasted_iota(jnp.int32, (bq, LANES), 1) < HS
    scale = 1.0 / math.sqrt(HS)

    *buffers, s_acc, s_buf, sum_ref, own_ref, send_sems, recv_sems, own_sems = scratch
    place = Place(nz, ny, nx)
    copies = Copies(send_sems, recv_sems)

    @pl.when(pl.program_id(0) == 0)
    def _():
        place.meet()

    whole = Reduction(place, copies, grad_ref, sum_ref, buffers, own_ref, own_sems)
    table = Timetable(rows // bq, steps)
    chunk_plan, small_plan, ending_plan = plan
    for t, ticks in enumerate(chunk_plan):
        table.add(whole.chunk(t), ticks)
    table.add(small_sum(place, copies, small_ref, small_out_ref, s_acc, s_buf), small_plan)
    table.add(whole.ending(), ending_plan)

    convolve(lq_ref, kern_ref, 0, q_ref, edge)
    convolve(lk_ref, kern_ref, 1, k_ref, 0)
    convolve(lv_ref, kern_ref, 2, v_ref, 0)
    dk_ref[...] = jnp.zeros_like(dk_ref)
    dv_ref[...] = jnp.zeros_like(dv_ref)
    if edge:
        dq_ref[pl.ds(0, edge), :] = jnp.zeros((edge, LANES), jnp.float32)
    dq_ref[pl.ds(edge + rows, 8), :] = jnp.zeros((8, LANES), jnp.float32)
    kt_ref[...] = k_ref[...].astype(jnp.float32).T.astype(jnp.bfloat16)

    def block(at):
        query = q_ref[pl.ds(at, bq), :] * jnp.bfloat16(scale)
        grad = g_ref[pl.ds(at, bq), :]
        zero = jnp.zeros_like(query)
        queries = (jnp.where(lane, query, zero), jnp.where(lane, zero, query))
        grads = (jnp.where(lane, grad, zero), jnp.where(lane, zero, grad))
        product = (grad.astype(jnp.float32) * o_ref[pl.ds(at, bq), :].astype(jnp.float32)).T
        query_grads = [jnp.zeros((HS, bq), jnp.float32)] * 2
        deltas = [jnp.sum(product[h * HS:(h + 1) * HS], axis=0, keepdims=True) for h in range(2)]
        masses = [mass_ref[0, h:h + 1, pl.ds(at, bq)] * LOG2E for h in range(2)]
        for start, size, hop in parts_of(rows, shards, at, bq, kc):
            key = k_ref[pl.ds(start, size), :]
            value = v_ref[pl.ds(start, size), :]
            key_part = value_part = None
            for h in range(2):
                s = dot(key, queries[h], NT)
                if hop is None:
                    row = lax.broadcasted_iota(jnp.int32, (size, bq), 1)
                    col = lax.broadcasted_iota(jnp.int32, (size, bq), 0)
                    s = jnp.where(col <= row, s, -1e30)
                mass = masses[h] + far_ref[hop - 1:hop, 0:1] if hop else masses[h]
                p = jnp.exp2(s * LOG2E - mass)
                dp = dot(value, grads[h], NT)
                ds = (p * (dp - deltas[h])).astype(jnp.bfloat16)
                a = dot(p.astype(jnp.bfloat16), grads[h])
                b = dot(ds, queries[h])
                value_part = a if value_part is None else value_part + a
                key_part = b if key_part is None else key_part + b
                query_grads[h] += dot(kt_ref[h * HS:(h + 1) * HS, pl.ds(start, size)], ds)
            dk_ref[pl.ds(start, size), :] += key_part
            dv_ref[pl.ds(start, size), :] += value_part
        dq_ref[pl.ds(edge + at, bq), :] = jnp.concatenate(query_grads, axis=0).T * scale

    for slot, at in enumerate(range(0, rows, bq)):
        table.tick(slot)
        block(at)

    sums_ref[...] = jnp.zeros_like(sums_ref)
    convolve_back(dq_ref, lq_ref, kern_ref, 0, gq_ref, sums_ref)
    convolve_back(dk_ref, lk_ref, kern_ref, 1, gk_ref, sums_ref)
    convolve_back(dv_ref, lv_ref, kern_ref, 2, gv_ref, sums_ref)

    @pl.when(pl.program_id(0) == steps - 1)
    def _():
        table.finish()
        for at, size in spans(0, sum_ref.shape[1], 256):
            up_ref[:, pl.ds(at, size)] = sum_ref[0, pl.ds(at, size), :].astype(jnp.float32).T
            down_ref[pl.ds(at, size), :] = sum_ref[1, pl.ds(at, size), :].astype(jnp.float32)
        copies.finish()


def attention_backward(far, late, linear_k, linear_v, kern, grads, outs, mass, ff_grad, small, ny, nx):
    rows = grads.shape[0]
    edged, width = late.shape
    window = linear_k.shape[0]
    pairs = width // LANES
    bq = min(256, rows)
    bf = jnp.bfloat16
    nz, members, height, columns = ff_grad.shape
    count = Reduction.count(nz, ny, nx) + nx + ny + nz - 2
    ticks = pairs * (rows // bq)
    gap = max(1, 5 * ticks // 32)
    chunks = [(gap * t, gap * t + 2, gap * t + 7, gap * t + 10) for t in range(nz)]
    end = max(chunks[-1][-1] + 1, ticks - 8)
    plan = (chunks, range(2, 12, 2), (end, end + 4, end + 6, end + 7))
    return pl.pallas_call(
        functools.partial(backward_kernel, nz, ny, nx, pairs, bq, 1024, plan),
        out_shape=(jax.ShapeDtypeStruct((edged, width), bf), jax.ShapeDtypeStruct((window, width), bf),
                   jax.ShapeDtypeStruct((window, width), bf), jax.ShapeDtypeStruct((16, width), jnp.float32),
                   jax.ShapeDtypeStruct((columns, height), jnp.float32), jax.ShapeDtypeStruct((height, columns), jnp.float32),
                   jax.ShapeDtypeStruct(small.shape, jnp.float32)),
        grid=(pairs,),
        in_specs=[WHOLE, column(edged), column(window), column(window), column(16), column(rows), column(rows),
                  pl.BlockSpec((1, 8, rows), lambda i: (i, 0, 0)), ANY, VMEM],
        out_specs=[column(edged), column(window), column(window), column(16), VMEM, VMEM, VMEM],
        scratch_shapes=[
            pltpu.VMEM((rows, LANES), bf), pltpu.VMEM((window, LANES), bf), pltpu.VMEM((window, LANES), bf),
            pltpu.VMEM((LANES, window), bf), pltpu.VMEM((edged + 8, LANES), jnp.float32),
            pltpu.VMEM((window + 8, LANES), jnp.float32), pltpu.VMEM((window + 8, LANES), jnp.float32),
        ] + Reduction.scratch(nz, ny, nx, members, height, columns) + small_scratch(nz, ny, nx, small.shape) + [
            pltpu.VMEM((members, height, columns), bf),
            pltpu.VMEM((nz, ny, members, nx * (height // (ny * 2 * nx)), columns), bf),
            pltpu.SemaphoreType.DMA((count,)), pltpu.SemaphoreType.DMA((count,)), pltpu.SemaphoreType.DMA((nz, ny)),
        ],
        compiler_params=pltpu.CompilerParams(collective_id=2, has_side_effects=True, vmem_limit_bytes=60 << 20),
    )(far, late, linear_k, linear_v, kern, grads, outs, mass, ff_grad, small)


def taps_of(rows, size):
    return [pltpu.roll(rows, i, 0)[TAP:TAP + size] if i else rows[TAP:TAP + size] for i in range(3)]


def front_kernel(
    nz, ny, nx, shards, bq, kc, far_ref, gain_ref, small_ref, shard_ref, input_ref, up_ref, down_ref,
    out_ref, mass_ref, small_out_ref, full_out, window_out, lq_out, lk_out, lv_out, up_out, down_out,
    full, window, lq, lk, lv, small_all, q_ref, k_ref, v_ref, s0_ref, s1_ref, acc_ref, total_ref, peak_ref,
    send_sems, recv_sems, out_sems,
):
    rows, depth = input_ref.shape
    window_rows = window.shape[0]
    own = window_rows - rows
    edge = lq.shape[0] - rows
    members, _, width = shard_ref.shape
    per = width // LANES
    half = members // 2
    share = depth // (ny * 2 * nx)
    units = up_ref.shape[0]
    part = units // (ny * 2 * nx)
    step_at = pl.program_id(0)
    f32, bf = jnp.float32, jnp.bfloat16
    scale = 1.0 / math.sqrt(HS)
    lane = lax.broadcasted_iota(jnp.int32, (bq, LANES), 1) < HS

    place = Place(nz, ny, nx)
    copies = Copies(send_sems, recv_sems)

    def columns(block, size=width, first=0):
        return pl.ds(pl.multiple_of(block * width + first, LANES), size)

    begin, tasks = gather_tasks(
        place, copies,
        [lambda lo=lo, hi=hi: shard_ref.at[lo:hi, place.piece(share, 0, 0), :] for lo, hi in ((0, half), (half, members))],
        [lambda block, dy, dx, lo=lo, hi=hi: full.at[lo:hi, place.piece(share, dy, dx), columns(block)]
         for lo, hi in ((0, half), (half, members))])
    smalls = [copies.plan(lambda: small_ref, lambda: small_all.at[place.z], place.along_z(s)) for s in range(1, nz)]

    def rows_to(hop, at, size):
        return copies.plan(
            lambda: window.at[pl.ds(own + at, size), :], lambda: window.at[pl.ds(own - hop * rows + at, size), :],
            place.along_z(hop))

    near = [rows_to(1, rows - edge, edge)] if shards > 1 else []
    distant = []
    for hop in range(1, shards):
        distant += [rows_to(hop, at, size) for at, size in spans(0, rows - (edge if hop == 1 else 0), 256)]

    def spot(ref):
        return lambda block, dy, dx: ref.at[pl.ds(pl.multiple_of(block * units, units), units), :].at[place.piece(part, dy, dx), :]

    ff_begin, ff_tasks = gather_tasks(
        place, copies, [lambda ref=ref: ref.at[place.piece(part, 0, 0), :] for ref in (up_ref, down_ref)],
        [spot(up_out), spot(down_out)])

    def local(n, source, target):
        return pltpu.make_async_copy(source, target, out_sems.at[n])

    def stores(which):
        mine = pl.ds(pl.multiple_of(place.z * units, units), units)
        return {
            "units": lambda: [local(0, up_ref, up_out.at[mine, :]), local(1, down_ref, down_out.at[mine, :])],
            "full": lambda: [local(2, full, full_out)],
            "window": lambda: [local(3, window, window_out)],
            "linear": lambda: [local(4, lq, lq_out), local(5, lk, lk_out), local(6, lv, lv_out)],
        }[which]()

    def keep_valid(hop, first, size):
        for at, n in spans(first, first + size, 256):
            at_rows = pl.ds(own - hop * rows + at, n)
            window[at_rows, :] = jnp.where(far_ref[hop - 1:hop, 0:1] > 0, jnp.zeros((n, depth), bf), window[at_rows, :])

    @pl.when(step_at == 0)
    def _():
        for at, size in spans(0, rows, 256):
            values = input_ref[at:at + size, :].astype(f32)
            factor = lax.rsqrt(jnp.mean(values * values, axis=-1, keepdims=True) + EPSILON)
            window[pl.ds(own + at, size), :] = (values * factor * gain_ref[0:1, :]).astype(bf)
        small_all[place.z] = small_ref[...]
        place.meet()
        start(near)
        begin()
        start(smalls)
        start(stores("units"))
        for m in range(members):
            full[m, :, columns(place.z)] = shard_ref[m]
        arrive(near)
        if shards > 1:
            keep_valid(1, rows - edge, edge)

    def all_rows():
        arrive(distant)
        for hop in range(1, shards):
            keep_valid(hop, 0, rows - (edge if hop == 1 else 0))
        start(stores("window"))

    slots = per + 1
    table = Timetable(slots, 2 * nz)
    for s, (arrival, turn, cross, done) in enumerate(tasks):
        table.add([arrival, turn], (slots * s if s else 1, slots * s + (1 if s else per)))
    for s, (arrival, turn, cross, done) in enumerate(tasks):
        table.add([cross, done], (slots * (s + 1), slots * (s + 1)))
    for s in range(nz - 1):
        waiting = distant[s:s + 1] if s < nz - 2 else distant[s:]
        table.add([lambda waiting=waiting: start(waiting)], [slots * s if s else 1])
    table.add([lambda: arrive(smalls)], [slots])
    table.add([lambda: start(stores("full")), all_rows], [slots * (nz - 1), slots * nz])
    table.add([ff_begin], [slots * nz - 1])
    for s, task in enumerate(ff_tasks):
        first = slots * nz + 3 * (s + 1) - 1
        table.add(task, (first, first + 3, first + 5, first + 6))

    relative = step_at % nz
    block = (place.z - relative) % nz

    def filtered(source, member, target, first, size, source_first, p):
        lanes = columns(block, LANES, p * LANES)
        for at, n in spans(first, first + size, 256):
            inside = at - source_first
            if inside == 0:
                rows_in = source[pl.ds(0, n), lanes].astype(f32)
                rows_in = jnp.concatenate([jnp.zeros((TAP, LANES), f32), rows_in], axis=0)
            else:
                rows_in = source[pl.ds(inside - TAP, n + TAP), lanes].astype(f32)
            taps = taps_of(rows_in, n)
            value = sum(small_all[block, 3 * member + i:3 * member + i + 1, p * LANES:(p + 1) * LANES] * taps[i] for i in range(3))
            target(at, n, value.astype(bf))

    def into(ref, shift=0):
        def put(at, n, value):
            ref[pl.ds(at - shift, n), :] = value
        return put

    def queries_of(at):
        query = q_ref[pl.ds(at, bq), :] * jnp.bfloat16(scale)
        zero = jnp.zeros_like(query)
        return jnp.where(lane, query, zero), jnp.where(lane, zero, query)

    def scores(queries, parts, shift):
        peaks = [{}, {}]
        for start_at, size, hop in parts:
            key = k_ref[pl.ds(start_at, size), :]
            for h, store in enumerate((s0_ref, s1_ref)):
                s = dot(queries[h], key, NT)
                if hop is None:
                    row = lax.broadcasted_iota(jnp.int32, (bq, size), 0)
                    col = lax.broadcasted_iota(jnp.int32, (bq, size), 1)
                    s = jnp.where(col <= row, s, -1e30)
                store[:, pl.ds(start_at - shift, size)] = s
                top = jnp.max(s, axis=1, keepdims=True)
                group = hop or 0
                peaks[h][group] = jnp.maximum(peaks[h][group], top) if group in peaks[h] else top
        return peaks

    def weighted(parts, shift, bases):
        sums = [None, None]
        for start_at, size, hop in parts:
            value = v_ref[pl.ds(start_at, size), :]
            wide = lax.broadcasted_iota(jnp.int32, (size, LANES), 1) < HS
            one = jnp.ones_like(value)
            values = (jnp.where(wide, value, one), jnp.where(wide, one, value))
            for h, store in enumerate((s0_ref, s1_ref)):
                p = jnp.exp2(store[:, pl.ds(start_at - shift, size)] * LOG2E - bases[h][hop or 0]).astype(bf)
                o = dot(p, values[h])
                sums[h] = o if sums[h] is None else sums[h] + o
        return jnp.where(lane, sums[0], sums[1]), pltpu.roll(jnp.where(lane, sums[1], sums[0]), HS, 1)

    def finish_rows(p, at, acc, total, peak):
        out_ref[pl.ds(at, bq), columns(block, LANES, p * LANES)] = (acc / total).astype(bf)
        mass = (peak + jnp.log(total)).T
        mass_ref[block * per + p, 0:1, pl.ds(at, bq)] = mass[0:1]
        mass_ref[block * per + p, 1:2, pl.ds(at, bq)] = mass[HS:HS + 1]

    def linear(target, member, first, last, target_first):
        for at, n in spans(first, last, 256):
            value = dot(window[pl.ds(at, n), :], full[member, :, columns(block)])
            target[pl.ds(at - target_first, n), columns(block)] = value.astype(bf)

    table.tick(0)

    @pl.when(step_at < nz)
    def _():
        linear(lq, 0, own - edge, window_rows, own - edge)
        linear(lk, 1, own - edge, window_rows, 0)
        linear(lv, 2, own - edge, window_rows, 0)

    @pl.when(step_at >= nz)
    def _():
        if shards > 1:
            linear(lk, 1, 0, own - edge, 0)
            linear(lv, 2, 0, own - edge, 0)

    for p in range(per):
        state = relative * per + p

        @pl.when(step_at < nz)
        def _():
            filtered(lq, 0, into(q_ref, own), own, rows, own - edge, p)
            filtered(lk, 1, into(k_ref), own, rows, 0, p)
            filtered(lv, 2, into(v_ref), own, rows, 0, p)
            for at in range(0, rows, bq):
                parts = [(start_at, n, 0) for start_at, n in spans(own, own + at, kc)] + [(own + at, bq, None)]
                peaks = scores(queries_of(at), parts, own)
                acc, total = weighted(parts, own, [{0: peaks[h][0] * LOG2E} for h in range(2)])
                here = pl.ds(at, bq)
                peak = jnp.where(lane, peaks[0][0], peaks[1][0])
                if shards > 1:
                    acc_ref[state, here, :] = acc
                    total_ref[state, here, :] = total
                    peak_ref[state, here, :] = peak
                else:
                    finish_rows(p, at, acc, total, peak)

        if shards > 1:
            @pl.when(step_at >= nz)
            def _():
                filtered(lq, 0, into(q_ref, own), own, rows, own - edge, p)
                filtered(lk, 1, into(k_ref), 0, own, 0, p)
                filtered(lv, 2, into(v_ref), 0, own, 0, p)
                for at in range(0, rows, bq):
                    here = pl.ds(at, bq)
                    parts = []
                    for hop in range(shards - 1, 0, -1):
                        parts += [(s, n, hop) for s, n in spans(own - hop * rows, own - (hop - 1) * rows, kc)]
                    peaks = scores(queries_of(at), parts, 0)
                    old = peak_ref[state, here, :]
                    tops, bases = [], []
                    for h in range(2):
                        top = old[:, h * HS:h * HS + 1]
                        for hop in range(1, shards):
                            top = jnp.maximum(top, peaks[h][hop] - far_ref[hop - 1:hop, 0:1])
                        tops.append(top)
                        bases.append({hop: top * LOG2E + far_ref[hop - 1:hop, 0:1] for hop in range(1, shards)})
                    acc, total = weighted(parts, 0, bases)
                    peak = jnp.where(lane, tops[0], tops[1])
                    fade = jnp.exp2((old - peak) * LOG2E)
                    finish_rows(p, at, acc_ref[state, here, :] * fade + acc, total_ref[state, here, :] * fade + total, peak)

        table.tick(p + 1)

    @pl.when(step_at == 2 * nz - 1)
    def _():
        start(stores("linear"))
        small_out_ref[...] = small_all[...]
        table.finish()
        for which in ("units", "full", "window", "linear"):
            for copy in stores(which):
                copy.wait()
        copies.finish()


def front(far, gain, small, shard, layer_input, up, down, nz, ny, nx, shards):
    rows, depth = layer_input.shape
    members, _, width = shard.shape
    window_rows = shards * rows
    edge = EDGE if shards > 1 else 0
    pairs = depth // LANES
    units = up.shape[0]
    bq = min(512, rows)
    f32, bf = jnp.float32, jnp.bfloat16
    sent = sum(len(spans(0, rows - (edge if hop == 1 else 0), 256)) for hop in range(1, shards)) + (1 if shards > 1 else 0)
    count = 2 * gather_count(nz, ny, nx) + nz - 1 + sent
    store = pltpu.VMEM((bq, max(rows, window_rows - rows)), f32)
    state = pltpu.VMEM((pairs, rows, LANES), f32)
    return pl.pallas_call(
        functools.partial(front_kernel, nz, ny, nx, shards, bq, 512),
        out_shape=(
            jax.ShapeDtypeStruct((rows, depth), bf), jax.ShapeDtypeStruct((pairs, 8, rows), f32),
            jax.ShapeDtypeStruct((nz,) + small.shape, f32), jax.ShapeDtypeStruct((members, depth, depth), bf),
            jax.ShapeDtypeStruct((window_rows, depth), bf), jax.ShapeDtypeStruct((rows + edge, depth), bf),
            jax.ShapeDtypeStruct((window_rows, depth), bf), jax.ShapeDtypeStruct((window_rows, depth), bf),
            jax.ShapeDtypeStruct((nz * units, depth), bf), jax.ShapeDtypeStruct((nz * units, depth), bf),
        ),
        grid=(2 * nz,),
        in_specs=[VMEM] * 7,
        out_specs=[VMEM] * 3 + [ANY] * 7,
        scratch_shapes=[
            pltpu.VMEM((members, depth, depth), bf), pltpu.VMEM((window_rows, depth), bf),
            pltpu.VMEM((rows + edge, depth), bf), pltpu.VMEM((window_rows, depth), bf), pltpu.VMEM((window_rows, depth), bf),
            pltpu.VMEM((nz,) + small.shape, f32),
            pltpu.VMEM((rows, LANES), bf), pltpu.VMEM((window_rows, LANES), bf), pltpu.VMEM((window_rows, LANES), bf),
            store, store, state, state, state,
            pltpu.SemaphoreType.DMA((count,)), pltpu.SemaphoreType.DMA((count,)), pltpu.SemaphoreType.DMA((7,)),
        ],
        compiler_params=pltpu.CompilerParams(collective_id=0, has_side_effects=True, vmem_limit_bytes=62 << 20),
        cost_estimate=pl.CostEstimate(flops=30 << 30, bytes_accessed=60 << 20, transcendentals=0),
    )(far, gain, small, shard, layer_input, up, down)


class TailReduction(Reduction):
    def __init__(self, place, copies, lefts, rights, send_ref, out_ref, buffers, shape):
        self.place, self.copies, self.out = place, copies, out_ref
        self.core, self.y1, self.x1, self.x2, self.y2, self.z_send, self.z_buf = buffers
        self.lefts, self.rights, self.send = lefts, rights, send_ref
        self.members, self.height, self.width = shape
        self.half = self.members // 2
        self.rows = self.height // (place.ny * 2 * place.nx)
        self.sums = []

    def product(self, t, dy, m, core):
        block = (self.place.z + 1 + t) % self.place.nz
        columns = pl.ds(pl.multiple_of(block * self.width, self.width), self.width)
        left, first = self.lefts[m]
        return dot(left[self.place.band(self.rows, dy, core), first:], self.rights[m][:, columns])

    def source(self, t, dy):
        return self.send.at[t, dy]

    def prepare(self, t):
        pass

    def prepared(self, t):
        pass

    def own(self, t, dy, m):
        return self.product(t, dy, m, 0)

    def fill(self, t):
        for dy in range(self.place.ny):
            for m in range(self.members):
                self.send[t, dy, m] = self.product(t, dy, m, 1).astype(jnp.bfloat16)


def tail_kernel(
    nz, ny, nx, rows, shards, far_ref, gain_ref, sums_ref, gq_in, gk_in, gv_in, window_in, turned_in, low_turned_in,
    attended_in, weight_in, low_in, input_in, out_ref, small_out_ref, grad_out_ref, *scratch,
):
    (gq, gk, gv, window, turned, low_turned, attended, weight, low, own_input, partial, far_send, far_came, send,
     *buffers, s_acc, s_buf, load_sems, send_sems, recv_sems) = scratch
    place = Place(nz, ny, nx)
    copies = Copies(send_sems, recv_sems)
    edge = gq.shape[0] - rows
    window_rows = window.shape[0]
    f32, bf = jnp.float32, jnp.bfloat16
    loads = {}
    for n, (source, target) in enumerate((
        (gk_in, gk), (weight_in.at[1:3], weight.at[1:3]), (gv_in, gv), (window_in, window), (gq_in, gq),
        (weight_in.at[0:1], weight.at[0:1]), (turned_in, turned), (low_turned_in, low_turned), (attended_in, attended),
        (low_in, low), (input_in, own_input),
    )):
        loads[n] = pltpu.make_async_copy(source, target, load_sems.at[n])
        loads[n].start()

    step = min(256, rows)
    whole = TailReduction(
        place, copies, [(turned, window_rows - rows - edge), (turned, 0), (turned, 0), (low_turned, 0)],
        [gq, gk, gv, attended], send, out_ref, buffers, out_ref.shape)
    chunks = [whole.chunk(t) for t in range(nz)]
    ending = whole.ending()
    small = small_sum(place, copies, None, small_out_ref, s_acc, s_buf)
    backs = {
        (hop, at): copies.plan(
            lambda hop=hop, at=at: far_send.at[hop - 1, at:at + step, :], lambda hop=hop, at=at: far_came.at[hop - 1, at:at + step, :],
            place.along_z(-hop))
        for hop in range(1, shards) for at in range(0, rows, step)
    }
    place.meet()

    gains = [jnp.zeros((8, window.shape[1]), f32)]

    def normed_rows(at):
        part = dot(gk[at:at + step, :], weight[1], NT) + dot(gv[at:at + step, :], weight[2], NT)
        first = at - (window_rows - rows - edge)
        if first >= 0:
            part = part + dot(gq[first:first + step, :], weight[0], NT)
        elif first + step > 0:
            query = dot(gq[0:first + step, :], weight[0], NT)
            part = part + jnp.concatenate([jnp.zeros((-first, part.shape[1]), f32), query], axis=0)
        product = part * window[at:at + step, :].astype(f32)
        gains[0] = gains[0] + jnp.sum(product.reshape(step // 8, 8, -1), axis=0)
        return part

    for n in range(6):
        loads[n].wait()
    for hop in range(shards - 1, 0, -1):
        keep = jnp.where(far_ref[hop - 1:hop, 0:1] > 0, 0.0, 1.0)
        for at in range(0, rows, step):
            part = normed_rows(window_rows - (hop + 1) * rows + at) * keep
            far_send[hop - 1, at:at + step, :] = part.astype(bf)
            backs[hop, at].start()

    def own_rows(at):
        partial[at:at + step, :] = normed_rows(window_rows - rows + at).astype(bf)

    def begin(t):
        whole.fill(t)
        chunks[t][0]()

    for n in range(6, 9):
        loads[n].wait()
    owned = list(range(0, rows, step))
    begin(0)
    for t in range(nz + 2):
        if t + 1 < nz:
            begin(t + 1)
        if t < nz:
            chunks[t][1]()
        if owned:
            own_rows(owned.pop(0))
        if 0 <= t - 1 < nz:
            chunks[t - 1][2]()
        if 0 <= t - 2 < nz:
            chunks[t - 2][3]()
    while owned:
        own_rows(owned.pop(0))
    s_acc[0] = sums_ref[...]
    s_acc[0, 9:10, :] = jnp.sum(gains[0], axis=0, keepdims=True)
    small[0]()
    ending[0]()
    small[1]()
    loads[9].wait()
    loads[10].wait()
    for copy in backs.values():
        copy.wait_recv()
    small[2]()
    gain = gain_ref[0:1, :]
    for at in range(0, rows, step):
        values = own_input[at:at + step, :].astype(f32)
        upstream = partial[at:at + step, :].astype(f32)
        for hop in range(1, shards):
            upstream = upstream + far_came[hop - 1, at:at + step, :].astype(f32)
        factor = lax.rsqrt(jnp.mean(values * values, axis=-1, keepdims=True) + EPSILON)
        unit = values * factor
        scaled = gain * upstream
        back = factor * (scaled - unit * jnp.mean(scaled * unit, axis=-1, keepdims=True))
        grad_out_ref[at:at + step, :] = (low[at:at + step, :].astype(f32) + back).astype(bf)
    small[3]()
    ending[1]()
    small[4]()
    ending[2]()
    ending[3]()
    copies.finish()


def tail(far, gain, sums, grads, window, turned, low_turned, attended, weight, low, own_input, rows, nz, ny, nx):
    grad_q, grad_k, grad_v = grads
    window_rows, depth = window.shape
    shards = window_rows // rows
    width = depth // nz
    members, bf = 4, jnp.bfloat16
    band = nx * (depth // (ny * 2 * nx))
    step = min(256, rows)
    count = Reduction.count(nz, ny, nx) + nx + ny + nz - 2 + (shards - 1) * (rows // step)
    buffers = [pltpu.VMEM(t.shape, bf) for t in (grad_q, grad_k, grad_v, window, turned, low_turned, attended)]
    hops = max(1, shards - 1)
    return pl.pallas_call(
        functools.partial(tail_kernel, nz, ny, nx, rows, shards),
        out_shape=(jax.ShapeDtypeStruct((members, depth, width), bf), jax.ShapeDtypeStruct(sums.shape, jnp.float32),
                   jax.ShapeDtypeStruct((rows, depth), bf)),
        in_specs=[VMEM, VMEM, VMEM] + [ANY] * 10,
        out_specs=(VMEM, VMEM, VMEM),
        scratch_shapes=buffers + [
            pltpu.VMEM((3, depth, depth), bf), pltpu.VMEM((rows, depth), bf), pltpu.VMEM((rows, depth), bf),
            pltpu.VMEM((rows, depth), bf), pltpu.VMEM((hops, rows, depth), bf), pltpu.VMEM((hops, rows, depth), bf),
            pltpu.VMEM((nz, ny, members, band, width), bf),
        ] + Reduction.scratch(nz, ny, nx, members, depth, width) + small_scratch(nz, ny, nx, sums.shape) + [
            pltpu.SemaphoreType.DMA((11,)), pltpu.SemaphoreType.DMA((count,)), pltpu.SemaphoreType.DMA((count,)),
        ],
        compiler_params=pltpu.CompilerParams(collective_id=3, has_side_effects=True, vmem_limit_bytes=62 << 20),
        cost_estimate=pl.CostEstimate(flops=24 << 30, bytes_accessed=60 << 20, transcendentals=0),
    )(far, gain, sums, grad_q, grad_k, grad_v, window, turned, low_turned, attended, weight, low, own_input)


def rows_norm(values):
    return lax.rsqrt(jnp.mean(values * values, axis=-1, keepdims=True) + EPSILON)


def turned(values):
    return values.astype(jnp.float32).T.astype(jnp.bfloat16)


def fold(values):
    return jnp.sum(values.reshape(values.shape[0] // 8, 8, values.shape[1]), axis=0)


def middle_kernel(
    steps, step, attended_ref, input_ref, grad_ref, project_ref, out_bias_ref, gain_ref, down_bias_ref, up_ref, down_ref, bias_ref,
    weights_ref, out_ref, low_ref, low_t_ref, attended_grad_ref, sums_ref,
    hidden, normed, normed_t, grad_t, normed_grad, total,
):
    rows, depth = input_ref.shape
    f32, bf = jnp.float32, jnp.bfloat16
    step_at = pl.program_id(0)
    pieces = spans(0, rows, 256)

    @pl.when(step_at == 0)
    def _():
        for at, size in pieces:
            here = pl.ds(at, size)
            state = input_ref[here, :].astype(f32) + dot(attended_ref[here, :], project_ref[...], NT) + out_bias_ref[0:1, :]
            hidden[here, :] = state
            value = state * rows_norm(state) * gain_ref[0:1, :]
            normed[here, :] = value.astype(bf)
            normed_t[:, here] = value.T.astype(bf)
            grad_t[:, here] = turned(grad_ref[here, :])
        normed_grad[...] = jnp.zeros_like(normed_grad)
        total[...] = jnp.zeros_like(total)
        sums_ref[...] = jnp.zeros_like(sums_ref)

    bias = jnp.broadcast_to(bias_ref[0], (LANES, step)).T[:, 0:1]
    gate = jnp.maximum(dot(up_ref[...], normed_t[...]) + bias, 0.0)
    activation = (gate * gate).astype(bf)
    gate_grad = (2.0 * gate * dot(down_ref[...], grad_t[...])).astype(bf)
    weights_ref[0, 0] = dot(gate_grad, normed[...]).astype(bf)
    weights_ref[0, 1] = dot(activation, grad_ref[...]).astype(bf)
    column = jnp.sum(gate_grad.astype(f32), axis=1, keepdims=True)
    first = step_at * step
    sums_ref[pl.ds(3 + first // depth, 1), pl.ds(pl.multiple_of(first % depth, step), step)] = (
        jnp.broadcast_to(column, (step, LANES)).T[0:1, :])
    normed_grad[...] += dot(gate_grad, up_ref[...], TN)
    total[...] += dot(activation, down_ref[...], TN)

    @pl.when(step_at == steps - 1)
    def _():
        parts = [jnp.zeros((8, depth), f32)] * 3
        gain = gain_ref[0:1, :]
        for at, size in pieces:
            here = pl.ds(at, size)
            state = hidden[here, :]
            cotangent = grad_ref[here, :].astype(f32)
            upstream = normed_grad[here, :]
            factor = rows_norm(state)
            unit = state * factor
            scaled = gain * upstream
            back = factor * (scaled - unit * jnp.mean(scaled * unit, axis=-1, keepdims=True))
            low = (cotangent + back).astype(bf)
            low_ref[here, :] = low
            low_t_ref[:, here] = turned(low)
            attended_grad_ref[here, :] = dot(low, project_ref[...]).astype(bf)
            out_ref[here, :] = (state + total[here, :] + down_bias_ref[0:1, :]).astype(bf)
            for k, value in enumerate((upstream * unit, low.astype(f32), cotangent)):
                parts[k] = parts[k] + fold(value)
        for k in range(3):
            sums_ref[k:k + 1, :] = jnp.sum(parts[k], axis=0, keepdims=True)


def middle(attended, layer_input, grad, full, out_bias, gain, down_bias, up_rows, down_rows, bias, nz):
    rows, depth = layer_input.shape
    units = up_rows.shape[0] // nz
    step = min(512, units)
    per = units // step
    steps = nz * per
    block = pl.BlockSpec((step, depth), lambda i: (i, 0))
    f32, bf = jnp.float32, jnp.bfloat16
    both = jax.ShapeDtypeStruct((rows, depth), bf)
    height = 3 + nz * units // depth
    return pl.pallas_call(
        functools.partial(middle_kernel, steps, step),
        out_shape=(jax.ShapeDtypeStruct((nz, 2, units, depth), bf), both, both, jax.ShapeDtypeStruct((depth, rows), bf), both,
                   jax.ShapeDtypeStruct((height + -height % 8, depth), f32)),
        grid=(steps,),
        in_specs=[VMEM] * 7 + [block, block, pl.BlockSpec((1, 1, step), lambda i: (i, 0, 0))],
        out_specs=[pl.BlockSpec((1, 2, step, depth), lambda i: (i // per, 0, i % per, 0))] + [VMEM] * 5,
        scratch_shapes=[
            pltpu.VMEM((rows, depth), f32), pltpu.VMEM((rows, depth), bf), pltpu.VMEM((depth, rows), bf),
            pltpu.VMEM((depth, rows), bf), pltpu.VMEM((rows, depth), f32), pltpu.VMEM((rows, depth), f32),
        ],
        compiler_params=pltpu.CompilerParams(vmem_limit_bytes=62 << 20),
        cost_estimate=pl.CostEstimate(flops=12 * rows * depth * nz * units, bytes_accessed=60 << 20, transcendentals=0),
    )(attended, layer_input, grad, full[3], out_bias[None], gain[None], down_bias[None], up_rows, down_rows,
      bias.reshape(steps, 1, step))


def on_device(
    layer_input, lengths, norm1_gain, qkv_weight, kernels, out_weight, out_bias,
    norm2_gain, up_weight, up_bias, down_weight, down_bias, out_grad,
):
    rows = layer_input.shape[1]
    nz, nb, nx = lax.axis_size("head"), lax.axis_size("batch"), lax.axis_size("dp")
    ny = nb // 2
    shards = max(1, LONG // rows)
    place = lax.axis_index("head")
    width = qkv_weight.shape[2]
    hidden_units = up_weight.shape[1]

    first_row = place * rows
    ends = jnp.cumsum(lengths[0])
    begins = jnp.max(jnp.where(ends <= first_row, ends, 0))
    before = ((first_row - begins) // rows).astype(jnp.int32)

    cotangent = out_grad[0]
    hops = jnp.arange(1, 9)[:, None]
    far = jnp.broadcast_to(jnp.where(before >= hops, 0.0, 1e30), (8, LANES)).astype(jnp.float32)
    small = jnp.concatenate([kernels.reshape(9, width), up_bias.reshape(-1, width)], axis=0)
    small = jnp.pad(small, ((0, -small.shape[0] % 8), (0, 0)))
    shard = jnp.concatenate([qkv_weight, out_weight.T[None]], axis=0)
    attended, mass, small, full, window, linear_q, linear_k, linear_v, up_rows, down_rows = front(
        far, norm1_gain[None], small, shard, layer_input[0], up_weight.T, down_weight, nz, ny, nx, shards)
    kern = jnp.pad(small[:, :9].transpose(1, 0, 2).reshape(9, -1), ((0, 7), (0, 0)))
    up_bias_all = small[:, 9:9 + hidden_units // width].reshape(-1)
    ff_grad, layer_output, hidden_low, low_turned, attended_grad, early = middle(
        attended, layer_input[0], cotangent, full, out_bias, norm2_gain, down_bias, up_rows, down_rows, up_bias_all, nz)
    grad_q, grad_k, grad_v, kernel_sums, up_sum, down_sum, early = attention_backward(
        far, linear_q, linear_k, linear_v, kern, attended_grad, attended, mass, ff_grad, early, ny, nx)
    qkvo_sum, totals, layer_grad = tail(
        far, norm1_gain[None], kernel_sums, (grad_q, grad_k, grad_v), window, window.T, low_turned, attended, full,
        hidden_low, layer_input[0], rows, nz, ny, nx)

    width_all = norm1_gain.shape[0]
    early = early.reshape(-1)
    up_bias_grad = lax.dynamic_slice_in_dim(early[3 * width_all:], place * hidden_units, hidden_units, 0)
    kernels_grad = lax.dynamic_slice_in_dim(totals[:9].reshape(3, 3, -1), place * width, width, 2)
    f32 = jnp.float32
    return (
        layer_output[None], layer_grad[None], totals[9] / norm1_gain, qkvo_sum[:3].astype(f32), kernels_grad,
        qkvo_sum[3].T.astype(f32), early[width_all:2 * width_all], early[:width_all], up_sum,
        up_bias_grad, down_sum, early[2 * width_all:3 * width_all],
    )


def solution(mesh):
    rows = P(("batch", "dp"), "head", None)
    return jax.shard_map(
        on_device,
        mesh=mesh,
        in_specs=(
            rows, P(("batch", "dp"), None), P(), P(None, None, "head"), P(None, None, "head"), P("head", None), P(),
            P(), P(None, "head"), P("head"), P("head", None), P(), rows,
        ),
        out_specs=(
            rows, rows, P(), P(None, None, "head"), P(None, None, "head"), P("head", None),
            P(), P(), P(None, "head"), P("head"), P("head", None), P(),
        ),
        check_vma=False,
    )
```

```python
import functools
import math

import jax
import jax.numpy as jnp
from jax import lax
from jax.experimental import pallas as pl
from jax.experimental.pallas import tpu as pltpu
from jax.sharding import PartitionSpec as P

LONG = 2048
EPSILON = 1e-06
ALL = ("head", "batch", "dp")

MESH = pl.DeviceIdType.MESH
VMEM = pl.BlockSpec(memory_space=pltpu.VMEM)


class Copy:
    def __init__(self, source, target, device, send_sem, recv_sem):
        self.parts = source, target, device, send_sem, recv_sem

    def make(self):
        source, target, device, send_sem, recv_sem = self.parts
        return pltpu.make_async_remote_copy(
            src_ref=source(), dst_ref=target(), send_sem=send_sem(), recv_sem=recv_sem(), device_id=device(), device_id_type=MESH)

    def start(self):
        self.make().start()

    def wait_recv(self):
        self.make().wait_recv()

    def wait_send(self):
        self.make().wait_send()


class Copies:
    def __init__(self, send_sems, recv_sems):
        self.send_sems, self.recv_sems, self.made = send_sems, recv_sems, []

    def plan(self, source, target, device):
        n = len(self.made)
        copy = Copy(source, target, device, lambda: self.send_sems.at[n], lambda: self.recv_sems.at[n])
        self.made.append(copy)
        return copy

    def finish(self):
        for copy in self.made:
            copy.wait_send()


def start(copies):
    for copy in copies:
        copy.start()


def arrive(copies):
    for copy in copies:
        copy.wait_recv()


class Place:
    def __init__(self, nz, ny, nx):
        self.nz, self.ny, self.nx = nz, ny, nx
        self.z, batch, self.x = lax.axis_index("head"), lax.axis_index("batch"), lax.axis_index("dp")
        self.y, self.c = batch // 2, batch % 2

    def along_z(self, step):
        return lambda: {"head": (self.z + step) % self.nz}

    def along_y(self, step):
        return lambda: {"batch": (self.y + step) % self.ny * 2 + self.c}

    def along_x(self, step):
        return lambda: {"dp": (self.x + step) % self.nx}

    def other_core(self):
        return {"batch": self.y * 2 + 1 - self.c}

    def meet(self):
        partners = [self.along_z(s) for s in range(1, self.nz)]
        partners += [self.along_y(s) for s in range(1, self.ny)] + [self.along_x(s) for s in range(1, self.nx)]
        partners.append(self.other_core)
        barrier = pltpu.get_barrier_semaphore()
        for partner in partners:
            pl.semaphore_signal(barrier, inc=1, device_id=partner(), device_id_type=MESH)
        pl.semaphore_wait(barrier, len(partners))

    def band(self, rows, dy, core=0):
        size = self.nx * rows
        core = self.c if core == 0 else 1 - self.c
        return pl.ds(pl.multiple_of(((self.y - dy) % self.ny * 2 + core) * size, size), size)

    def piece(self, rows, dy, dx):
        if dx is None:
            return self.band(rows, dy)
        at = ((self.y - dy) % self.ny * 2 + self.c) * self.nx + (self.x - dx) % self.nx
        return pl.ds(pl.multiple_of(at * rows, rows), rows)


def spread(place, copies, spots):
    ny, nx = place.ny, place.nx

    def plan(spot, dy, dx, device):
        part = lambda: spot(dy, dx)
        return copies.plan(part, part, device)

    over_x = [[plan(spot, 0, 0, place.along_x(s)) for s in range(1, nx)] for spot in spots]
    over_y = [[plan(spot, 0, 0, place.along_y(t)) for t in range(1, ny)] for spot in spots]
    corner_y = [plan(spots[0], 0, s, place.along_y(t)) for s in range(1, nx) for t in range(1, ny)]
    corner_x = [plan(spots[1], t, 0, place.along_x(s)) for s in range(1, nx) for t in range(1, ny)]
    cores = [plan(spot, dy, None, place.other_core) for spot in spots for dy in range(ny)]

    def out():
        for k in (0, 1):
            start(over_x[k])
            start(over_y[k])

    def turn():
        arrive(over_x[0])
        start(corner_y)
        arrive(over_y[1])
        start(corner_x)
        arrive(over_x[1])
        arrive(over_y[0])

    def cross():
        arrive(corner_y)
        arrive(corner_x)
        start(cores)

    return [out, turn, cross, lambda: arrive(cores)]


def spread_count(ny, nx):
    return 2 * ((nx - 1) + (ny - 1) + (nx - 1) * (ny - 1) + ny)


def gather_tasks(place, copies, shards, fulls):
    nz = place.nz

    def part(k, step):
        return lambda: fulls[k]((place.z - step) % nz, 0, 0)

    rings = [
        [copies.plan(part(k, step) if step else shards[k], part(k, step), place.along_z(1)) for k in range(2)]
        for step in range(nz - 1)
    ]

    def task(step):
        spots = [lambda dy, dx, k=k: fulls[k]((place.z - 1 - step) % nz, dy, dx) for k in range(2)]
        out, *others = spread(place, copies, spots)

        def arrival():
            arrive(rings[step])
            if step < nz - 2:
                start(rings[step + 1])
            out()

        return [arrival] + others

    return lambda: start(rings[0]), [task(step) for step in range(nz - 1)]


def gather_count(nz, ny, nx):
    return (nz - 1) * (2 + spread_count(ny, nx))


def run_staggered(tasks):
    phases = [(at + n, n, phase) for n, task in enumerate(tasks) for at, phase in enumerate(task)]
    for _, _, phase in sorted(phases, key=lambda entry: entry[:2]):
        phase()


class Timetable:
    def __init__(self, per_step, steps):
        self.per_step, self.steps, self.at = per_step, steps, {}

    def add(self, task, times):
        for time, phase in zip(times, task, strict=True):
            self.at.setdefault(time, []).append(phase)

    def tick(self, slot):
        for time in range(slot, self.per_step * self.steps, self.per_step):
            if time in self.at:
                @pl.when(pl.program_id(0) == time // self.per_step)
                def _():
                    for phase in self.at[time]:
                        phase()

    def finish(self):
        for time in sorted(self.at):
            if time >= self.per_step * self.steps:
                for phase in self.at[time]:
                    phase()


class Reduction:
    def __init__(self, place, copies, grad_ref, out_ref, buffers, own_ref, own_sems):
        self.place, self.copies, self.grad, self.out = place, copies, grad_ref, out_ref
        self.own_ref, self.own_sems = own_ref, own_sems
        self.core, self.y1, self.x1, self.x2, self.y2, self.z_send, self.z_buf = buffers
        self.members, self.height, self.width = grad_ref.shape[1:]
        self.half = self.members // 2
        self.rows = self.height // (place.ny * 2 * place.nx)
        self.sums = []

    @staticmethod
    def scratch(nz, ny, nx, members, height, width):
        half, rows, bf = members // 2, height // (ny * 2 * nx), jnp.bfloat16
        band = nx * rows
        return [
            pltpu.VMEM((nz, ny, members, band, width), bf),
            pltpu.VMEM((nz, ny - 1, half, band, width), bf),
            pltpu.VMEM((nz, nx - 1, ny, half, rows, width), bf),
            pltpu.VMEM((nz, nx - 1, half, rows, width), bf),
            pltpu.VMEM((nz, ny - 1, half, rows, width), bf),
            pltpu.VMEM((nz, members, rows, width), bf),
            pltpu.VMEM((nz - 1, members, rows, width), bf),
        ]

    @staticmethod
    def count(nz, ny, nx):
        return nz * (ny + 2 * (ny - 1) + 2 * (nx - 1)) + nz - 1 + spread_count(ny, nx)

    def source(self, t, dy):
        return self.grad.at[(self.place.z + 1 + t) % self.place.nz, :, self.place.band(self.rows, dy, 1), :]

    def staged(self, t):
        block = (self.place.z + 1 + t) % self.place.nz
        return [
            pltpu.make_async_copy(self.grad.at[block, :, self.place.band(self.rows, dy), :], self.own_ref.at[t, dy], self.own_sems.at[t, dy])
            for dy in range(self.place.ny)
        ]

    def prepare(self, t):
        start(self.staged(t))

    def prepared(self, t):
        for copy in self.staged(t):
            copy.wait()

    def own(self, t, dy, m):
        return self.own_ref[t, dy, m]

    def chunk(self, t):
        place, copies, half, rows = self.place, self.copies, self.half, self.rows
        ny, nx, nz = place.ny, place.nx, place.nz
        core, x1, y1, x2, y2, f32, bf = self.core, self.x1, self.y1, self.x2, self.y2, jnp.float32, jnp.bfloat16

        def xrows(step):
            return pl.ds(pl.multiple_of((place.x + step) % nx * rows, rows), rows)

        sent = [
            copies.plan(
                lambda dy=dy: self.source(t, dy),
                lambda dy=dy: core.at[t, dy], place.other_core)
            for dy in range(ny)
        ]
        over_y = [
            copies.plan(lambda s=s: core.at[t, ny - s, 0:half], lambda s=s: y1.at[t, s - 1], place.along_y(s))
            for s in range(1, ny)
        ]
        over_x = [
            copies.plan(lambda s=s: core.at[t, :, half:, xrows(s), :], lambda s=s: x1.at[t, s - 1], place.along_x(s))
            for s in range(1, nx)
        ]
        then_x = [
            copies.plan(lambda s=s: core.at[t, 0, 0:half, xrows(s), :], lambda s=s: x2.at[t, s - 1], place.along_x(s))
            for s in range(1, nx)
        ]
        then_y = [
            copies.plan(lambda s=s: core.at[t, ny - s, half:, xrows(0), :], lambda s=s: y2.at[t, s - 1], place.along_y(s))
            for s in range(1, ny)
        ]
        along = [copies.plan(lambda: self.z_send.at[t], lambda: self.z_buf.at[t], place.along_z(1 + t))] if t < nz - 1 else []
        self.sums += along

        def first():
            start(sent)
            self.prepare(t)

        def both_cores():
            arrive(sent)
            self.prepared(t)
            for dy in range(ny):
                for m in range(self.members):
                    core[t, dy, m] = (core[t, dy, m].astype(f32) + self.own(t, dy, m).astype(f32)).astype(bf)
            start(over_y)
            start(over_x)

        def turn():
            arrive(over_y)
            for m in range(half):
                total = core[t, 0, m].astype(f32)
                for s in range(ny - 1):
                    total = total + y1[t, s, m].astype(f32)
                core[t, 0, m] = total.astype(bf)
            start(then_x)
            arrive(over_x)
            for dy in range(ny):
                for m in range(half):
                    total = core[t, dy, half + m, xrows(0), :].astype(f32)
                    for s in range(nx - 1):
                        total = total + x1[t, s, dy, m].astype(f32)
                    core[t, dy, half + m, xrows(0), :] = total.astype(bf)
            start(then_y)

        def send_on():
            arrive(then_x)
            arrive(then_y)
            for m in range(self.members):
                total = core[t, 0, m, xrows(0), :].astype(f32)
                buf, n = (x2, nx - 1) if m < half else (y2, ny - 1)
                for s in range(n):
                    total = total + buf[t, s, m % half].astype(f32)
                self.z_send[t, m] = total.astype(bf)
            start(along)

        return [first, both_cores, turn, send_on]

    def ending(self):
        place, nz = self.place, self.place.nz
        spots = [
            lambda dy, dx, lo=lo, hi=hi: self.out.at[lo:hi, place.piece(self.rows, dy, dx), :]
            for lo, hi in ((0, self.half), (self.half, self.members))
        ]
        out, *others = spread(place, self.copies, spots)

        def total():
            arrive(self.sums)
            for m in range(self.members):
                total = self.z_send[nz - 1, m].astype(jnp.float32)
                for t in range(nz - 1):
                    total = total + self.z_buf[t, m].astype(jnp.float32)
                self.out[m, place.piece(self.rows, 0, 0), :] = total.astype(jnp.bfloat16)
            out()

        return [total] + others


def small_sum(place, copies, small_ref, out_ref, s_acc, s_buf):
    nz, ny, nx = place.nz, place.ny, place.nx
    stages = ([place.other_core], [place.along_x(s) for s in range(1, nx)],
              [place.along_y(s) for s in range(1, ny)], [place.along_z(s) for s in range(1, nz)])
    firsts = [0, 1, nx, nx + ny - 1]
    sent = [
        [copies.plan(lambda k=k: s_acc.at[k], lambda n=firsts[k] + i: s_buf.at[n], partner) for i, partner in enumerate(partners)]
        for k, partners in enumerate(stages)
    ]

    def add(k):
        arrive(sent[k])
        total = s_acc[k]
        for i in range(len(sent[k])):
            total = total + s_buf[firsts[k] + i]
        return total

    def first():
        if small_ref is not None:
            s_acc[0] = small_ref[...]
        start(sent[0])

    def middle(k):
        s_acc[k + 1] = add(k)
        start(sent[k + 1])

    def last():
        out_ref[...] = add(3)

    return [first] + [functools.partial(middle, k) for k in range(3)] + [last]


def small_scratch(nz, ny, nx, shape):
    return [pltpu.VMEM((4,) + shape, jnp.float32), pltpu.VMEM((nx + ny + nz - 2,) + shape, jnp.float32)]


HS = 64
LANES = 128
EDGE = 128
TAP = 16
LOG2E = math.log2(math.e)
NT = (((1,), (1,)), ((), ()))
NN = (((1,), (0,)), ((), ()))
TN = (((0,), (0,)), ((), ()))


def dot(a, b, dims=NN):
    return lax.dot_general(a, b, dims, preferred_element_type=jnp.float32)


def spans(first, last, step):
    return [(at, min(step, last - at)) for at in range(first, last, step)]


def earlier(ref, start, size):
    if start == 0:
        rows = jnp.concatenate([jnp.zeros((TAP, LANES), jnp.float32), ref[pl.ds(0, size), :].astype(jnp.float32)], axis=0)
    else:
        rows = ref[pl.ds(start - TAP, size + TAP), :].astype(jnp.float32)
    return [pltpu.roll(rows, i, 0)[TAP:] if i else rows[TAP:] for i in range(3)]


def convolve(linear_ref, kern_ref, member, target_ref, skip, step=256):
    total = linear_ref.shape[0]
    for start, size in spans(skip, total, step):
        taps = earlier(linear_ref, start, size)
        value = sum(kern_ref[3 * member + i:3 * member + i + 1, :] * taps[i] for i in range(3))
        target_ref[pl.ds(start - skip, size), :] = value.astype(jnp.bfloat16)


def convolve_back(grad_ref, linear_ref, kern_ref, member, target_ref, sums_ref, step=256):
    total = linear_ref.shape[0]
    parts = [jnp.zeros((8, LANES), jnp.float32)] * 3
    for start, size in spans(0, total, step):
        rows = grad_ref[pl.ds(start, size + 8), :]
        linear = linear_ref[pl.ds(start, size), :].astype(jnp.float32)
        value = None
        for i in range(3):
            later = pltpu.roll(rows, size + 8 - i, 0)[:size] if i else rows[:size]
            term = kern_ref[3 * member + i:3 * member + i + 1, :] * later
            value = term if value is None else value + term
            parts[i] += jnp.sum((later * linear).reshape(size // 8, 8, LANES), axis=0)
        target_ref[pl.ds(start, size), :] = value.astype(jnp.bfloat16)
    for i in range(3):
        sums_ref[3 * member + i:3 * member + i + 1, :] = jnp.sum(parts[i], axis=0, keepdims=True)


def parts_of(rows, shards, at, size, step):
    own = (shards - 1) * rows
    pieces = []
    for hop in range(shards - 1, 0, -1):
        pieces += [(start, n, hop) for start, n in spans(own - hop * rows, own - (hop - 1) * rows, step)]
    pieces += [(start, n, 0) for start, n in spans(own, own + at, step)]
    return pieces + [(own + at, size, None)]


def column(n):
    return pl.BlockSpec((n, LANES), lambda i: (0, i))


ANY = pl.BlockSpec(memory_space=pl.ANY)
WHOLE = pl.BlockSpec((8, LANES), lambda i: (0, 0))


def backward_kernel(
    nz, ny, nx, steps, bq, kc, plan, far_ref, lq_ref, lk_ref, lv_ref, kern_ref, g_ref, o_ref, mass_ref, grad_ref, small_ref,
    gq_ref, gk_ref, gv_ref, sums_ref, up_ref, down_ref, small_out_ref,
    q_ref, k_ref, v_ref, kt_ref, dq_ref, dk_ref, dv_ref, *scratch,
):
    rows, window = q_ref.shape[0], k_ref.shape[0]
    shards = window // rows
    edge = lq_ref.shape[0] - rows
    lane = lax.broadcasted_iota(jnp.int32, (bq, LANES), 1) < HS
    scale = 1.0 / math.sqrt(HS)

    *buffers, s_acc, s_buf, sum_ref, own_ref, send_sems, recv_sems, own_sems = scratch
    place = Place(nz, ny, nx)
    copies = Copies(send_sems, recv_sems)

    @pl.when(pl.program_id(0) == 0)
    def _():
        place.meet()

    whole = Reduction(place, copies, grad_ref, sum_ref, buffers, own_ref, own_sems)
    table = Timetable(rows // bq, steps)
    chunk_plan, small_plan, ending_plan = plan
    for t, ticks in enumerate(chunk_plan):
        table.add(whole.chunk(t), ticks)
    table.add(small_sum(place, copies, small_ref, small_out_ref, s_acc, s_buf), small_plan)
    table.add(whole.ending(), ending_plan)

    convolve(lq_ref, kern_ref, 0, q_ref, edge)
    convolve(lk_ref, kern_ref, 1, k_ref, 0)
    convolve(lv_ref, kern_ref, 2, v_ref, 0)
    dk_ref[...] = jnp.zeros_like(dk_ref)
    dv_ref[...] = jnp.zeros_like(dv_ref)
    if edge:
        dq_ref[pl.ds(0, edge), :] = jnp.zeros((edge, LANES), jnp.float32)
    dq_ref[pl.ds(edge + rows, 8), :] = jnp.zeros((8, LANES), jnp.float32)
    kt_ref[...] = k_ref[...].astype(jnp.float32).T.astype(jnp.bfloat16)

    def block(at):
        query = q_ref[pl.ds(at, bq), :] * jnp.bfloat16(scale)
        grad = g_ref[pl.ds(at, bq), :]
        zero = jnp.zeros_like(query)
        queries = (jnp.where(lane, query, zero), jnp.where(lane, zero, query))
        grads = (jnp.where(lane, grad, zero), jnp.where(lane, zero, grad))
        product = (grad.astype(jnp.float32) * o_ref[pl.ds(at, bq), :].astype(jnp.float32)).T
        query_grads = [jnp.zeros((HS, bq), jnp.float32)] * 2
        deltas = [jnp.sum(product[h * HS:(h + 1) * HS], axis=0, keepdims=True) for h in range(2)]
        masses = [mass_ref[0, h:h + 1, pl.ds(at, bq)] * LOG2E for h in range(2)]
        for start, size, hop in parts_of(rows, shards, at, bq, kc):
            key = k_ref[pl.ds(start, size), :]
            value = v_ref[pl.ds(start, size), :]
            key_part = value_part = None
            for h in range(2):
                s = dot(key, queries[h], NT)
                if hop is None:
                    row = lax.broadcasted_iota(jnp.int32, (size, bq), 1)
                    col = lax.broadcasted_iota(jnp.int32, (size, bq), 0)
                    s = jnp.where(col <= row, s, -1e30)
                mass = masses[h] + far_ref[hop - 1:hop, 0:1] if hop else masses[h]
                p = jnp.exp2(s * LOG2E - mass)
                dp = dot(value, grads[h], NT)
                ds = (p * (dp - deltas[h])).astype(jnp.bfloat16)
                a = dot(p.astype(jnp.bfloat16), grads[h])
                b = dot(ds, queries[h])
                value_part = a if value_part is None else value_part + a
                key_part = b if key_part is None else key_part + b
                query_grads[h] += dot(kt_ref[h * HS:(h + 1) * HS, pl.ds(start, size)], ds)
            dk_ref[pl.ds(start, size), :] += key_part
            dv_ref[pl.ds(start, size), :] += value_part
        dq_ref[pl.ds(edge + at, bq), :] = jnp.concatenate(query_grads, axis=0).T * scale

    for slot, at in enumerate(range(0, rows, bq)):
        table.tick(slot)
        block(at)

    sums_ref[...] = jnp.zeros_like(sums_ref)
    convolve_back(dq_ref, lq_ref, kern_ref, 0, gq_ref, sums_ref)
    convolve_back(dk_ref, lk_ref, kern_ref, 1, gk_ref, sums_ref)
    convolve_back(dv_ref, lv_ref, kern_ref, 2, gv_ref, sums_ref)

    @pl.when(pl.program_id(0) == steps - 1)
    def _():
        table.finish()
        for at, size in spans(0, sum_ref.shape[1], 256):
            up_ref[:, pl.ds(at, size)] = sum_ref[0, pl.ds(at, size), :].astype(jnp.float32).T
            down_ref[pl.ds(at, size), :] = sum_ref[1, pl.ds(at, size), :].astype(jnp.float32)
        copies.finish()


def attention_backward(far, late, linear_k, linear_v, kern, grads, outs, mass, ff_grad, small, ny, nx):
    rows = grads.shape[0]
    edged, width = late.shape
    window = linear_k.shape[0]
    pairs = width // LANES
    bq = min(256, rows)
    bf = jnp.bfloat16
    nz, members, height, columns = ff_grad.shape
    count = Reduction.count(nz, ny, nx) + nx + ny + nz - 2
    ticks = pairs * (rows // bq)
    gap = max(1, 5 * ticks // 32)
    chunks = [(gap * t, gap * t + 2, gap * t + 7, gap * t + 10) for t in range(nz)]
    end = max(chunks[-1][-1] + 1, ticks - 8)
    plan = (chunks, range(2, 12, 2), (end, end + 4, end + 6, end + 7))
    return pl.pallas_call(
        functools.partial(backward_kernel, nz, ny, nx, pairs, bq, 1024, plan),
        out_shape=(jax.ShapeDtypeStruct((edged, width), bf), jax.ShapeDtypeStruct((window, width), bf),
                   jax.ShapeDtypeStruct((window, width), bf), jax.ShapeDtypeStruct((16, width), jnp.float32),
                   jax.ShapeDtypeStruct((columns, height), jnp.float32), jax.ShapeDtypeStruct((height, columns), jnp.float32),
                   jax.ShapeDtypeStruct(small.shape, jnp.float32)),
        grid=(pairs,),
        in_specs=[WHOLE, column(edged), column(window), column(window), column(16), column(rows), column(rows),
                  pl.BlockSpec((1, 8, rows), lambda i: (i, 0, 0)), ANY, VMEM],
        out_specs=[column(edged), column(window), column(window), column(16), VMEM, VMEM, VMEM],
        scratch_shapes=[
            pltpu.VMEM((rows, LANES), bf), pltpu.VMEM((window, LANES), bf), pltpu.VMEM((window, LANES), bf),
            pltpu.VMEM((LANES, window), bf), pltpu.VMEM((edged + 8, LANES), jnp.float32),
            pltpu.VMEM((window + 8, LANES), jnp.float32), pltpu.VMEM((window + 8, LANES), jnp.float32),
        ] + Reduction.scratch(nz, ny, nx, members, height, columns) + small_scratch(nz, ny, nx, small.shape) + [
            pltpu.VMEM((members, height, columns), bf),
            pltpu.VMEM((nz, ny, members, nx * (height // (ny * 2 * nx)), columns), bf),
            pltpu.SemaphoreType.DMA((count,)), pltpu.SemaphoreType.DMA((count,)), pltpu.SemaphoreType.DMA((nz, ny)),
        ],
        compiler_params=pltpu.CompilerParams(collective_id=2, has_side_effects=True, vmem_limit_bytes=60 << 20),
    )(far, late, linear_k, linear_v, kern, grads, outs, mass, ff_grad, small)


def taps_of(rows, size):
    return [pltpu.roll(rows, i, 0)[TAP:TAP + size] if i else rows[TAP:TAP + size] for i in range(3)]


def front_kernel(
    nz, ny, nx, shards, bq, kc, far_ref, gain_ref, small_ref, qkv_ref, project_ref, input_ref, up_in_ref, down_ref,
    out_ref, mass_ref, small_out_ref, full_out, window_out, turned_out, lq_out, lk_out, lv_out, up_out, down_out,
    up_ref, full, window, turned, lq, lk, lv, small_all, q_ref, k_ref, v_ref, s0_ref, s1_ref, acc_ref, total_ref, peak_ref,
    send_sems, recv_sems, out_sems,
):
    rows, depth = input_ref.shape
    window_rows = window.shape[0]
    own = window_rows - rows
    edge = lq.shape[0] - rows
    members, width = 4, qkv_ref.shape[2]
    per = width // LANES
    half = members // 2
    share = depth // (ny * 2 * nx)
    units = down_ref.shape[0]
    part = units // (ny * 2 * nx)
    step_at = pl.program_id(0)
    f32, bf = jnp.float32, jnp.bfloat16
    scale = 1.0 / math.sqrt(HS)
    lane = lax.broadcasted_iota(jnp.int32, (bq, LANES), 1) < HS

    place = Place(nz, ny, nx)
    copies = Copies(send_sems, recv_sems)

    def columns(block, size=width, first=0):
        return pl.ds(pl.multiple_of(block * width + first, LANES), size)

    begin, tasks = gather_tasks(
        place, copies,
        [lambda lo=lo, hi=hi: full.at[lo:hi, place.piece(share, 0, 0), columns(place.z)] for lo, hi in ((0, half), (half, members))],
        [lambda block, dy, dx, lo=lo, hi=hi: full.at[lo:hi, place.piece(share, dy, dx), columns(block)]
         for lo, hi in ((0, half), (half, members))])
    smalls = [copies.plan(lambda: small_ref, lambda: small_all.at[place.z], place.along_z(s)) for s in range(1, nz)]

    def rows_to(hop, at, size):
        return copies.plan(
            lambda: window.at[pl.ds(own + at, size), :], lambda: window.at[pl.ds(own - hop * rows + at, size), :],
            place.along_z(hop))

    near = [rows_to(1, rows - edge, edge)] if shards > 1 else []
    distant = []
    for hop in range(1, shards):
        distant += [rows_to(hop, at, size) for at, size in spans(0, rows - (edge if hop == 1 else 0), 256)]

    def spot(ref):
        return lambda block, dy, dx: ref.at[pl.ds(pl.multiple_of(block * units, units), units), :].at[place.piece(part, dy, dx), :]

    ff_begin, ff_tasks = gather_tasks(
        place, copies, [lambda ref=ref: ref.at[place.piece(part, 0, 0), :] for ref in (up_ref, down_ref)],
        [spot(up_out), spot(down_out)])

    def local(n, source, target):
        return pltpu.make_async_copy(source, target, out_sems.at[n])

    def stores(which):
        mine = pl.ds(pl.multiple_of(place.z * units, units), units)
        return {
            "units": lambda: [local(0, up_ref, up_out.at[mine, :]), local(1, down_ref, down_out.at[mine, :])],
            "full": lambda: [local(2, full, full_out)],
            "window": lambda: [local(3, window, window_out)],
            "turned": lambda: [local(7, turned, turned_out)],
            "linear": lambda: [local(4, lq, lq_out), local(5, lk, lk_out), local(6, lv, lv_out)],
        }[which]()

    def keep_valid(hop, first, size):
        for at, n in spans(first, first + size, 256):
            at_rows = pl.ds(own - hop * rows + at, n)
            window[at_rows, :] = jnp.where(far_ref[hop - 1:hop, 0:1] > 0, jnp.zeros((n, depth), bf), window[at_rows, :])

    @pl.when(step_at == 0)
    def _():
        for at, size in spans(0, rows, 256):
            values = input_ref[at:at + size, :].astype(f32)
            factor = lax.rsqrt(jnp.mean(values * values, axis=-1, keepdims=True) + EPSILON)
            window[pl.ds(own + at, size), :] = (values * factor * gain_ref[0:1, :]).astype(bf)
        small_all[place.z] = small_ref[...]
        for m in range(3):
            full[m, :, columns(place.z)] = qkv_ref[m]
        full[3, :, columns(place.z)] = project_ref[...].astype(f32).T.astype(bf)
        place.meet()
        start(near)
        begin()
        start(smalls)
        arrive(near)
        if shards > 1:
            keep_valid(1, rows - edge, edge)

    def all_rows():
        arrive(distant)
        for hop in range(1, shards):
            keep_valid(hop, 0, rows - (edge if hop == 1 else 0))
        start(stores("window"))

    slots = per + 1
    table = Timetable(slots, 2 * nz)
    for s, (arrival, turn, cross, done) in enumerate(tasks):
        table.add([arrival, turn], (slots * s if s else 1, slots * s + (1 if s else per)))
    for s, (arrival, turn, cross, done) in enumerate(tasks):
        table.add([cross, done], (slots * (s + 1), slots * (s + 1)))
    for s in range(nz - 1):
        waiting = distant[s:s + 1] if s < nz - 2 else distant[s:]
        table.add([lambda waiting=waiting: start(waiting)], [slots * s if s else 1])
    table.add([lambda: arrive(smalls)], [slots])
    table.add([lambda: start(stores("full")), all_rows], [slots * (nz - 1), slots * nz])
    def turn_up(at, size):
        return lambda: up_ref.__setitem__((slice(at, at + size), slice(None)), up_in_ref[:, at:at + size].astype(f32).T.astype(bf))

    for n, (at, size) in enumerate(spans(0, units, 256)):
        table.add([turn_up(at, size)], [slots + n])
    table.add([lambda: start(stores("units")), ff_begin], [slots * nz - 1, slots * nz - 1])
    for s, task in enumerate(ff_tasks):
        first = slots * nz + 3 * (s + 1) - 1
        table.add(task, (first, first + 3, first + 5, first + 6))

    def turn_rows(at, size):
        return lambda: turned.__setitem__((slice(None), slice(at, at + size)), window[at:at + size, :].astype(f32).T.astype(bf))

    for n, (at, size) in enumerate(spans(0, window_rows, 256)):
        table.add([turn_rows(at, size)], [slots * nz + 1 + n % (slots * nz - 1)])

    relative = step_at % nz
    block = (place.z - relative) % nz

    def filtered(source, member, target, first, size, source_first, p):
        lanes = columns(block, LANES, p * LANES)
        for at, n in spans(first, first + size, 256):
            inside = at - source_first
            if inside == 0:
                rows_in = source[pl.ds(0, n), lanes].astype(f32)
                rows_in = jnp.concatenate([jnp.zeros((TAP, LANES), f32), rows_in], axis=0)
            else:
                rows_in = source[pl.ds(inside - TAP, n + TAP), lanes].astype(f32)
            taps = taps_of(rows_in, n)
            value = sum(small_all[block, 3 * member + i:3 * member + i + 1, p * LANES:(p + 1) * LANES] * taps[i] for i in range(3))
            target(at, n, value.astype(bf))

    def into(ref, shift=0):
        def put(at, n, value):
            ref[pl.ds(at - shift, n), :] = value
        return put

    def queries_of(at):
        query = q_ref[pl.ds(at, bq), :] * jnp.bfloat16(scale)
        zero = jnp.zeros_like(query)
        return jnp.where(lane, query, zero), jnp.where(lane, zero, query)

    def scores(queries, parts, shift):
        peaks = [{}, {}]
        for start_at, size, hop in parts:
            key = k_ref[pl.ds(start_at, size), :]
            for h, store in enumerate((s0_ref, s1_ref)):
                s = dot(queries[h], key, NT)
                if hop is None:
                    row = lax.broadcasted_iota(jnp.int32, (bq, size), 0)
                    col = lax.broadcasted_iota(jnp.int32, (bq, size), 1)
                    s = jnp.where(col <= row, s, -1e30)
                store[:, pl.ds(start_at - shift, size)] = s
                top = jnp.max(s, axis=1, keepdims=True)
                group = hop or 0
                peaks[h][group] = jnp.maximum(peaks[h][group], top) if group in peaks[h] else top
        return peaks

    def weighted(parts, shift, bases):
        sums = [None, None]
        for start_at, size, hop in parts:
            value = v_ref[pl.ds(start_at, size), :]
            wide = lax.broadcasted_iota(jnp.int32, (size, LANES), 1) < HS
            one = jnp.ones_like(value)
            values = (jnp.where(wide, value, one), jnp.where(wide, one, value))
            for h, store in enumerate((s0_ref, s1_ref)):
                p = jnp.exp2(store[:, pl.ds(start_at - shift, size)] * LOG2E - bases[h][hop or 0]).astype(bf)
                o = dot(p, values[h])
                sums[h] = o if sums[h] is None else sums[h] + o
        return jnp.where(lane, sums[0], sums[1]), pltpu.roll(jnp.where(lane, sums[1], sums[0]), HS, 1)

    def finish_rows(p, at, acc, total, peak):
        out_ref[pl.ds(at, bq), columns(block, LANES, p * LANES)] = (acc / total).astype(bf)
        mass = (peak + jnp.log(total)).T
        mass_ref[block * per + p, 0:1, pl.ds(at, bq)] = mass[0:1]
        mass_ref[block * per + p, 1:2, pl.ds(at, bq)] = mass[HS:HS + 1]

    def linear(target, member, first, last, target_first):
        for at, n in spans(first, last, 256):
            value = dot(window[pl.ds(at, n), :], full[member, :, columns(block)])
            target[pl.ds(at - target_first, n), columns(block)] = value.astype(bf)

    table.tick(0)

    @pl.when(step_at < nz)
    def _():
        linear(lq, 0, own - edge, window_rows, own - edge)
        linear(lk, 1, own - edge, window_rows, 0)
        linear(lv, 2, own - edge, window_rows, 0)

    @pl.when(step_at >= nz)
    def _():
        if shards > 1:
            linear(lk, 1, 0, own - edge, 0)
            linear(lv, 2, 0, own - edge, 0)

    for p in range(per):
        state = relative * per + p

        @pl.when(step_at < nz)
        def _():
            filtered(lq, 0, into(q_ref, own), own, rows, own - edge, p)
            filtered(lk, 1, into(k_ref), own, rows, 0, p)
            filtered(lv, 2, into(v_ref), own, rows, 0, p)
            for at in range(0, rows, bq):
                parts = [(start_at, n, 0) for start_at, n in spans(own, own + at, kc)] + [(own + at, bq, None)]
                peaks = scores(queries_of(at), parts, own)
                acc, total = weighted(parts, own, [{0: peaks[h][0] * LOG2E} for h in range(2)])
                here = pl.ds(at, bq)
                peak = jnp.where(lane, peaks[0][0], peaks[1][0])
                if shards > 1:
                    acc_ref[state, here, :] = acc
                    total_ref[state, here, :] = total
                    peak_ref[state, here, :] = peak
                else:
                    finish_rows(p, at, acc, total, peak)

        if shards > 1:
            @pl.when(step_at >= nz)
            def _():
                filtered(lq, 0, into(q_ref, own), own, rows, own - edge, p)
                filtered(lk, 1, into(k_ref), 0, own, 0, p)
                filtered(lv, 2, into(v_ref), 0, own, 0, p)
                for at in range(0, rows, bq):
                    here = pl.ds(at, bq)
                    parts = []
                    for hop in range(shards - 1, 0, -1):
                        parts += [(s, n, hop) for s, n in spans(own - hop * rows, own - (hop - 1) * rows, kc)]
                    peaks = scores(queries_of(at), parts, 0)
                    old = peak_ref[state, here, :]
                    tops, bases = [], []
                    for h in range(2):
                        top = old[:, h * HS:h * HS + 1]
                        for hop in range(1, shards):
                            top = jnp.maximum(top, peaks[h][hop] - far_ref[hop - 1:hop, 0:1])
                        tops.append(top)
                        bases.append({hop: top * LOG2E + far_ref[hop - 1:hop, 0:1] for hop in range(1, shards)})
                    acc, total = weighted(parts, 0, bases)
                    peak = jnp.where(lane, tops[0], tops[1])
                    fade = jnp.exp2((old - peak) * LOG2E)
                    finish_rows(p, at, acc_ref[state, here, :] * fade + acc, total_ref[state, here, :] * fade + total, peak)

        table.tick(p + 1)

    @pl.when(step_at == 2 * nz - 1)
    def _():
        start(stores("turned"))
        start(stores("linear"))
        small_out_ref[...] = small_all[...]
        table.finish()
        for which in ("units", "full", "window", "turned", "linear"):
            for copy in stores(which):
                copy.wait()
        copies.finish()


def front(far, gain, small, qkv, project, layer_input, up, down, nz, ny, nx, shards):
    rows, depth = layer_input.shape
    members, width = 4, qkv.shape[2]
    window_rows = shards * rows
    edge = EDGE if shards > 1 else 0
    pairs = depth // LANES
    units = down.shape[0]
    bq = min(512, rows)
    f32, bf = jnp.float32, jnp.bfloat16
    sent = sum(len(spans(0, rows - (edge if hop == 1 else 0), 256)) for hop in range(1, shards)) + (1 if shards > 1 else 0)
    count = 2 * gather_count(nz, ny, nx) + nz - 1 + sent
    store = pltpu.VMEM((bq, max(rows, window_rows - rows)), f32)
    state = pltpu.VMEM((pairs, rows, LANES), f32)
    return pl.pallas_call(
        functools.partial(front_kernel, nz, ny, nx, shards, bq, 512),
        out_shape=(
            jax.ShapeDtypeStruct((rows, depth), bf), jax.ShapeDtypeStruct((pairs, 8, rows), f32),
            jax.ShapeDtypeStruct((nz,) + small.shape, f32), jax.ShapeDtypeStruct((members, depth, depth), bf),
            jax.ShapeDtypeStruct((window_rows, depth), bf), jax.ShapeDtypeStruct((depth, window_rows), bf),
            jax.ShapeDtypeStruct((rows + edge, depth), bf),
            jax.ShapeDtypeStruct((window_rows, depth), bf), jax.ShapeDtypeStruct((window_rows, depth), bf),
            jax.ShapeDtypeStruct((nz * units, depth), bf), jax.ShapeDtypeStruct((nz * units, depth), bf),
        ),
        grid=(2 * nz,),
        in_specs=[VMEM] * 8,
        out_specs=[VMEM] * 3 + [ANY] * 8,
        scratch_shapes=[
            pltpu.VMEM((units, depth), bf), pltpu.VMEM((members, depth, depth), bf), pltpu.VMEM((window_rows, depth), bf),
            pltpu.VMEM((depth, window_rows), bf), pltpu.VMEM((rows + edge, depth), bf), pltpu.VMEM((window_rows, depth), bf),
            pltpu.VMEM((window_rows, depth), bf),
            pltpu.VMEM((nz,) + small.shape, f32),
            pltpu.VMEM((rows, LANES), bf), pltpu.VMEM((window_rows, LANES), bf), pltpu.VMEM((window_rows, LANES), bf),
            store, store, state, state, state,
            pltpu.SemaphoreType.DMA((count,)), pltpu.SemaphoreType.DMA((count,)), pltpu.SemaphoreType.DMA((8,)),
        ],
        compiler_params=pltpu.CompilerParams(collective_id=0, has_side_effects=True, vmem_limit_bytes=63 << 20),
        cost_estimate=pl.CostEstimate(flops=30 << 30, bytes_accessed=60 << 20, transcendentals=0),
    )(far, gain, small, qkv, project, layer_input, up, down)


class TailReduction(Reduction):
    def __init__(self, place, copies, lefts, rights, send_ref, out_ref, buffers, shape):
        self.place, self.copies, self.out = place, copies, out_ref
        self.core, self.y1, self.x1, self.x2, self.y2, self.z_send, self.z_buf = buffers
        self.lefts, self.rights, self.send = lefts, rights, send_ref
        self.members, self.height, self.width = shape
        self.half = self.members // 2
        self.rows = self.height // (place.ny * 2 * place.nx)
        self.sums = []

    def product(self, t, dy, m, core):
        block = (self.place.z + 1 + t) % self.place.nz
        columns = pl.ds(pl.multiple_of(block * self.width, self.width), self.width)
        left, first = self.lefts[m]
        return dot(left[self.place.band(self.rows, dy, core), first:], self.rights[m][:, columns])

    def source(self, t, dy):
        return self.send.at[t, dy]

    def prepare(self, t):
        pass

    def prepared(self, t):
        pass

    def own(self, t, dy, m):
        return self.product(t, dy, m, 0)

    def fill(self, t):
        for dy in range(self.place.ny):
            for m in range(self.members):
                self.send[t, dy, m] = self.product(t, dy, m, 1).astype(jnp.bfloat16)


def tail_kernel(
    nz, ny, nx, rows, shards, far_ref, gain_ref, sums_ref, gq_in, gk_in, gv_in, window_in, turned_in, low_turned_in,
    attended_in, weight_in, low_in, input_in, out_ref, small_out_ref, grad_out_ref, *scratch,
):
    (gq, gk, gv, window, turned, low_turned, attended, weight, low, own_input, partial, far_send, far_came, send,
     *buffers, s_acc, s_buf, load_sems, send_sems, recv_sems) = scratch
    place = Place(nz, ny, nx)
    copies = Copies(send_sems, recv_sems)
    edge = gq.shape[0] - rows
    window_rows = window.shape[0]
    f32, bf = jnp.float32, jnp.bfloat16
    loads = {}
    for n, (source, target) in enumerate((
        (gk_in, gk), (weight_in.at[1:3], weight.at[1:3]), (gv_in, gv), (window_in, window), (gq_in, gq),
        (weight_in.at[0:1], weight.at[0:1]), (turned_in, turned), (low_turned_in, low_turned), (attended_in, attended),
        (low_in, low), (input_in, own_input),
    )):
        loads[n] = pltpu.make_async_copy(source, target, load_sems.at[n])
        loads[n].start()

    step = min(256, rows)
    whole = TailReduction(
        place, copies, [(turned, window_rows - rows - edge), (turned, 0), (turned, 0), (low_turned, 0)],
        [gq, gk, gv, attended], send, out_ref, buffers, out_ref.shape)
    chunks = [whole.chunk(t) for t in range(nz)]
    ending = whole.ending()
    small = small_sum(place, copies, None, small_out_ref, s_acc, s_buf)
    backs = {
        (hop, at): copies.plan(
            lambda hop=hop, at=at: far_send.at[hop - 1, at:at + step, :], lambda hop=hop, at=at: far_came.at[hop - 1, at:at + step, :],
            place.along_z(-hop))
        for hop in range(1, shards) for at in range(0, rows, step)
    }
    place.meet()

    gains = [jnp.zeros((8, window.shape[1]), f32)]

    def normed_rows(at):
        part = dot(gk[at:at + step, :], weight[1], NT) + dot(gv[at:at + step, :], weight[2], NT)
        first = at - (window_rows - rows - edge)
        if first >= 0:
            part = part + dot(gq[first:first + step, :], weight[0], NT)
        elif first + step > 0:
            query = dot(gq[0:first + step, :], weight[0], NT)
            part = part + jnp.concatenate([jnp.zeros((-first, part.shape[1]), f32), query], axis=0)
        product = part * window[at:at + step, :].astype(f32)
        gains[0] = gains[0] + jnp.sum(product.reshape(step // 8, 8, -1), axis=0)
        return part

    for n in range(6):
        loads[n].wait()
    for hop in range(shards - 1, 0, -1):
        keep = jnp.where(far_ref[hop - 1:hop, 0:1] > 0, 0.0, 1.0)
        for at in range(0, rows, step):
            part = normed_rows(window_rows - (hop + 1) * rows + at) * keep
            far_send[hop - 1, at:at + step, :] = part.astype(bf)
            backs[hop, at].start()

    def own_rows(at):
        partial[at:at + step, :] = normed_rows(window_rows - rows + at).astype(bf)

    def begin(t):
        whole.fill(t)
        chunks[t][0]()

    for n in range(6, 9):
        loads[n].wait()
    owned = list(range(0, rows, step))
    begin(0)
    for t in range(nz + 2):
        if t + 1 < nz:
            begin(t + 1)
        if t < nz:
            chunks[t][1]()
        if owned:
            own_rows(owned.pop(0))
        if 0 <= t - 1 < nz:
            chunks[t - 1][2]()
        if 0 <= t - 2 < nz:
            chunks[t - 2][3]()
    while owned:
        own_rows(owned.pop(0))
    s_acc[0] = sums_ref[...]
    s_acc[0, 9:10, :] = jnp.sum(gains[0], axis=0, keepdims=True)
    small[0]()
    ending[0]()
    small[1]()
    ending[1]()
    small[2]()
    ending[2]()
    small[3]()
    loads[9].wait()
    loads[10].wait()
    for copy in backs.values():
        copy.wait_recv()
    gain = gain_ref[0:1, :]
    for at in range(0, rows, step):
        values = own_input[at:at + step, :].astype(f32)
        upstream = partial[at:at + step, :].astype(f32)
        for hop in range(1, shards):
            upstream = upstream + far_came[hop - 1, at:at + step, :].astype(f32)
        factor = lax.rsqrt(jnp.mean(values * values, axis=-1, keepdims=True) + EPSILON)
        unit = values * factor
        scaled = gain * upstream
        back = factor * (scaled - unit * jnp.mean(scaled * unit, axis=-1, keepdims=True))
        grad_out_ref[at:at + step, :] = (low[at:at + step, :].astype(f32) + back).astype(bf)
    ending[3]()
    small[4]()
    copies.finish()


def tail(far, gain, sums, grads, window, turned, low_turned, attended, weight, low, own_input, rows, nz, ny, nx):
    grad_q, grad_k, grad_v = grads
    window_rows, depth = window.shape
    shards = window_rows // rows
    width = depth // nz
    members, bf = 4, jnp.bfloat16
    band = nx * (depth // (ny * 2 * nx))
    step = min(256, rows)
    count = Reduction.count(nz, ny, nx) + nx + ny + nz - 2 + (shards - 1) * (rows // step)
    buffers = [pltpu.VMEM(t.shape, bf) for t in (grad_q, grad_k, grad_v, window, turned, low_turned, attended)]
    hops = max(1, shards - 1)
    return pl.pallas_call(
        functools.partial(tail_kernel, nz, ny, nx, rows, shards),
        out_shape=(jax.ShapeDtypeStruct((members, depth, width), bf), jax.ShapeDtypeStruct(sums.shape, jnp.float32),
                   jax.ShapeDtypeStruct((rows, depth), bf)),
        in_specs=[VMEM, VMEM, VMEM] + [ANY] * 10,
        out_specs=(VMEM, VMEM, VMEM),
        scratch_shapes=buffers + [
            pltpu.VMEM((3, depth, depth), bf), pltpu.VMEM((rows, depth), bf), pltpu.VMEM((rows, depth), bf),
            pltpu.VMEM((rows, depth), bf), pltpu.VMEM((hops, rows, depth), bf), pltpu.VMEM((hops, rows, depth), bf),
            pltpu.VMEM((nz, ny, members, band, width), bf),
        ] + Reduction.scratch(nz, ny, nx, members, depth, width) + small_scratch(nz, ny, nx, sums.shape) + [
            pltpu.SemaphoreType.DMA((11,)), pltpu.SemaphoreType.DMA((count,)), pltpu.SemaphoreType.DMA((count,)),
        ],
        compiler_params=pltpu.CompilerParams(collective_id=3, has_side_effects=True, vmem_limit_bytes=62 << 20),
        cost_estimate=pl.CostEstimate(flops=24 << 30, bytes_accessed=60 << 20, transcendentals=0),
    )(far, gain, sums, grad_q, grad_k, grad_v, window, turned, low_turned, attended, weight, low, own_input)


def rows_norm(values):
    return lax.rsqrt(jnp.mean(values * values, axis=-1, keepdims=True) + EPSILON)


def turned(values):
    return values.astype(jnp.float32).T.astype(jnp.bfloat16)


def fold(values):
    return jnp.sum(values.reshape(values.shape[0] // 8, 8, values.shape[1]), axis=0)


def middle_kernel(
    steps, step, attended_ref, input_ref, grad_ref, full_ref, out_bias_ref, gain_ref, down_bias_ref, up_ref, down_ref, bias_ref,
    weights_ref, out_ref, low_ref, low_t_ref, attended_grad_ref, sums_ref,
    hidden, normed, normed_t, grad_t, normed_grad, total, project_ref, load_sem,
):
    rows, depth = input_ref.shape
    f32, bf = jnp.float32, jnp.bfloat16
    step_at = pl.program_id(0)
    pieces = spans(0, rows, 256)

    @pl.when(step_at == 0)
    def _():
        load = pltpu.make_async_copy(full_ref.at[3], project_ref, load_sem)
        load.start()
        for at, size in pieces:
            grad_t[:, pl.ds(at, size)] = turned(grad_ref[pl.ds(at, size), :])
        load.wait()
        for at, size in pieces:
            here = pl.ds(at, size)
            state = input_ref[here, :].astype(f32) + dot(attended_ref[here, :], project_ref[...], NT) + out_bias_ref[0:1, :]
            hidden[here, :] = state
            value = state * rows_norm(state) * gain_ref[0:1, :]
            normed[here, :] = value.astype(bf)
            normed_t[:, here] = value.T.astype(bf)
        normed_grad[...] = jnp.zeros_like(normed_grad)
        total[...] = jnp.zeros_like(total)
        sums_ref[...] = jnp.zeros_like(sums_ref)

    bias = jnp.broadcast_to(bias_ref[0], (LANES, step)).T[:, 0:1]
    gate = jnp.maximum(dot(up_ref[...], normed_t[...]) + bias, 0.0)
    activation = (gate * gate).astype(bf)
    gate_grad = (2.0 * gate * dot(down_ref[...], grad_t[...])).astype(bf)
    weights_ref[0, 0] = dot(gate_grad, normed[...]).astype(bf)
    weights_ref[0, 1] = dot(activation, grad_ref[...]).astype(bf)
    column = jnp.sum(gate_grad.astype(f32), axis=1, keepdims=True)
    first = step_at * step
    sums_ref[pl.ds(3 + first // depth, 1), pl.ds(pl.multiple_of(first % depth, step), step)] = (
        jnp.broadcast_to(column, (step, LANES)).T[0:1, :])
    normed_grad[...] += dot(gate_grad, up_ref[...], TN)
    total[...] += dot(activation, down_ref[...], TN)

    @pl.when(step_at == steps - 1)
    def _():
        parts = [jnp.zeros((8, depth), f32)] * 3
        gain = gain_ref[0:1, :]
        for at, size in pieces:
            here = pl.ds(at, size)
            state = hidden[here, :]
            cotangent = grad_ref[here, :].astype(f32)
            upstream = normed_grad[here, :]
            factor = rows_norm(state)
            unit = state * factor
            scaled = gain * upstream
            back = factor * (scaled - unit * jnp.mean(scaled * unit, axis=-1, keepdims=True))
            low = (cotangent + back).astype(bf)
            low_ref[here, :] = low
            low_t_ref[:, here] = turned(low)
            attended_grad_ref[here, :] = dot(low, project_ref[...]).astype(bf)
            out_ref[here, :] = (state + total[here, :] + down_bias_ref[0:1, :]).astype(bf)
            for k, value in enumerate((upstream * unit, low.astype(f32), cotangent)):
                parts[k] = parts[k] + fold(value)
        for k in range(3):
            sums_ref[k:k + 1, :] = jnp.sum(parts[k], axis=0, keepdims=True)


def middle(attended, layer_input, grad, full, out_bias, gain, down_bias, up_rows, down_rows, bias, nz):
    rows, depth = layer_input.shape
    units = up_rows.shape[0] // nz
    step = min(512, units)
    per = units // step
    steps = nz * per
    block = pl.BlockSpec((step, depth), lambda i: (i, 0))
    f32, bf = jnp.float32, jnp.bfloat16
    both = jax.ShapeDtypeStruct((rows, depth), bf)
    height = 3 + nz * units // depth
    return pl.pallas_call(
        functools.partial(middle_kernel, steps, step),
        out_shape=(jax.ShapeDtypeStruct((nz, 2, units, depth), bf), both, both, jax.ShapeDtypeStruct((depth, rows), bf), both,
                   jax.ShapeDtypeStruct((height + -height % 8, depth), f32)),
        grid=(steps,),
        in_specs=[VMEM] * 3 + [ANY] + [VMEM] * 3 + [block, block, pl.BlockSpec((1, 1, step), lambda i: (i, 0, 0))],
        out_specs=[pl.BlockSpec((1, 2, step, depth), lambda i: (i // per, 0, i % per, 0))] + [VMEM] * 5,
        scratch_shapes=[
            pltpu.VMEM((rows, depth), f32), pltpu.VMEM((rows, depth), bf), pltpu.VMEM((depth, rows), bf),
            pltpu.VMEM((depth, rows), bf), pltpu.VMEM((rows, depth), f32), pltpu.VMEM((rows, depth), f32),
            pltpu.VMEM((depth, depth), bf), pltpu.SemaphoreType.DMA,
        ],
        compiler_params=pltpu.CompilerParams(vmem_limit_bytes=62 << 20),
        cost_estimate=pl.CostEstimate(flops=12 * rows * depth * nz * units, bytes_accessed=60 << 20, transcendentals=0),
    )(attended, layer_input, grad, full, out_bias[None], gain[None], down_bias[None], up_rows, down_rows,
      bias.reshape(steps, 1, step))


def on_device(
    layer_input, lengths, norm1_gain, qkv_weight, kernels, out_weight, out_bias,
    norm2_gain, up_weight, up_bias, down_weight, down_bias, out_grad,
):
    rows = layer_input.shape[1]
    nz, nb, nx = lax.axis_size("head"), lax.axis_size("batch"), lax.axis_size("dp")
    ny = nb // 2
    shards = max(1, LONG // rows)
    place = lax.axis_index("head")
    width = qkv_weight.shape[2]
    hidden_units = up_weight.shape[1]

    first_row = place * rows
    ends = jnp.cumsum(lengths[0])
    begins = jnp.max(jnp.where(ends <= first_row, ends, 0))
    before = ((first_row - begins) // rows).astype(jnp.int32)

    cotangent = out_grad[0]
    hops = jnp.arange(1, 9)[:, None]
    far = jnp.broadcast_to(jnp.where(before >= hops, 0.0, 1e30), (8, LANES)).astype(jnp.float32)
    small = jnp.concatenate([kernels.reshape(9, width), up_bias.reshape(-1, width)], axis=0)
    small = jnp.pad(small, ((0, -small.shape[0] % 8), (0, 0)))
    attended, mass, small, full, window, turned, linear_q, linear_k, linear_v, up_rows, down_rows = front(
        far, norm1_gain[None], small, qkv_weight, out_weight, layer_input[0], up_weight, down_weight, nz, ny, nx, shards)
    kern = jnp.pad(small[:, :9].transpose(1, 0, 2).reshape(9, -1), ((0, 7), (0, 0)))
    up_bias_all = small[:, 9:9 + hidden_units // width].reshape(-1)
    ff_grad, layer_output, hidden_low, low_turned, attended_grad, early = middle(
        attended, layer_input[0], cotangent, full, out_bias, norm2_gain, down_bias, up_rows, down_rows, up_bias_all, nz)
    grad_q, grad_k, grad_v, kernel_sums, up_sum, down_sum, early = attention_backward(
        far, linear_q, linear_k, linear_v, kern, attended_grad, attended, mass, ff_grad, early, ny, nx)
    qkvo_sum, totals, layer_grad = tail(
        far, norm1_gain[None], kernel_sums, (grad_q, grad_k, grad_v), window, turned, low_turned, attended, full,
        hidden_low, layer_input[0], rows, nz, ny, nx)

    width_all = norm1_gain.shape[0]
    early = early.reshape(-1)
    up_bias_grad = lax.dynamic_slice_in_dim(early[3 * width_all:], place * hidden_units, hidden_units, 0)
    kernels_grad = lax.dynamic_slice_in_dim(totals[:9].reshape(3, 3, -1), place * width, width, 2)
    f32 = jnp.float32
    return (
        layer_output[None], layer_grad[None], totals[9] / norm1_gain, qkvo_sum[:3].astype(f32), kernels_grad,
        qkvo_sum[3].T.astype(f32), early[width_all:2 * width_all], early[:width_all], up_sum,
        up_bias_grad, down_sum, early[2 * width_all:3 * width_all],
    )


def solution(mesh):
    rows = P(("batch", "dp"), "head", None)
    return jax.shard_map(
        on_device,
        mesh=mesh,
        in_specs=(
            rows, P(("batch", "dp"), None), P(), P(None, None, "head"), P(None, None, "head"), P("head", None), P(),
            P(), P(None, "head"), P("head"), P("head", None), P(), rows,
        ),
        out_specs=(
            rows, rows, P(), P(None, None, "head"), P(None, None, "head"), P("head", None),
            P(), P(), P(None, "head"), P("head"), P("head", None), P(),
        ),
        check_vma=False,
    )
```

```python
import functools
import math

import jax
import jax.numpy as jnp
from jax import lax
from jax.experimental import pallas as pl
from jax.experimental.pallas import tpu as pltpu
from jax.sharding import PartitionSpec as P

LONG = 2048
EPSILON = 1e-06
ALL = ("head", "batch", "dp")

MESH = pl.DeviceIdType.MESH
VMEM = pl.BlockSpec(memory_space=pltpu.VMEM)


class Copy:
    def __init__(self, source, target, device, send_sem, recv_sem):
        self.parts = source, target, device, send_sem, recv_sem

    def make(self):
        source, target, device, send_sem, recv_sem = self.parts
        return pltpu.make_async_remote_copy(
            src_ref=source(), dst_ref=target(), send_sem=send_sem(), recv_sem=recv_sem(), device_id=device(), device_id_type=MESH)

    def start(self):
        self.make().start()

    def wait_recv(self):
        self.make().wait_recv()

    def wait_send(self):
        self.make().wait_send()


class Copies:
    def __init__(self, send_sems, recv_sems):
        self.send_sems, self.recv_sems, self.made = send_sems, recv_sems, []

    def plan(self, source, target, device):
        n = len(self.made)
        copy = Copy(source, target, device, lambda: self.send_sems.at[n], lambda: self.recv_sems.at[n])
        self.made.append(copy)
        return copy

    def finish(self):
        for copy in self.made:
            copy.wait_send()


def start(copies):
    for copy in copies:
        copy.start()


def arrive(copies):
    for copy in copies:
        copy.wait_recv()


class Place:
    def __init__(self, nz, ny, nx):
        self.nz, self.ny, self.nx = nz, ny, nx
        self.z, batch, self.x = lax.axis_index("head"), lax.axis_index("batch"), lax.axis_index("dp")
        self.y, self.c = batch // 2, batch % 2

    def along_z(self, step):
        return lambda: {"head": (self.z + step) % self.nz}

    def along_y(self, step):
        return lambda: {"batch": (self.y + step) % self.ny * 2 + self.c}

    def along_x(self, step):
        return lambda: {"dp": (self.x + step) % self.nx}

    def other_core(self):
        return {"batch": self.y * 2 + 1 - self.c}

    def meet(self):
        partners = [self.along_z(s) for s in range(1, self.nz)]
        partners += [self.along_y(s) for s in range(1, self.ny)] + [self.along_x(s) for s in range(1, self.nx)]
        partners.append(self.other_core)
        barrier = pltpu.get_barrier_semaphore()
        for partner in partners:
            pl.semaphore_signal(barrier, inc=1, device_id=partner(), device_id_type=MESH)
        pl.semaphore_wait(barrier, len(partners))

    def band(self, rows, dy, core=0):
        size = self.nx * rows
        core = self.c if core == 0 else 1 - self.c
        return pl.ds(pl.multiple_of(((self.y - dy) % self.ny * 2 + core) * size, size), size)

    def piece(self, rows, dy, dx):
        if dx is None:
            return self.band(rows, dy)
        at = ((self.y - dy) % self.ny * 2 + self.c) * self.nx + (self.x - dx) % self.nx
        return pl.ds(pl.multiple_of(at * rows, rows), rows)


def spread(place, copies, spots):
    ny, nx = place.ny, place.nx

    def plan(spot, dy, dx, device):
        part = lambda: spot(dy, dx)
        return copies.plan(part, part, device)

    over_x = [[plan(spot, 0, 0, place.along_x(s)) for s in range(1, nx)] for spot in spots]
    over_y = [[plan(spot, 0, 0, place.along_y(t)) for t in range(1, ny)] for spot in spots]
    corner_y = [plan(spots[0], 0, s, place.along_y(t)) for s in range(1, nx) for t in range(1, ny)]
    corner_x = [plan(spots[1], t, 0, place.along_x(s)) for s in range(1, nx) for t in range(1, ny)]
    cores = [plan(spot, dy, None, place.other_core) for spot in spots for dy in range(ny)]

    def out():
        for k in (0, 1):
            start(over_x[k])
            start(over_y[k])

    def turn():
        arrive(over_x[0])
        start(corner_y)
        arrive(over_y[1])
        start(corner_x)
        arrive(over_x[1])
        arrive(over_y[0])

    def cross():
        arrive(corner_y)
        arrive(corner_x)
        start(cores)

    return [out, turn, cross, lambda: arrive(cores)]


def spread_count(ny, nx):
    return 2 * ((nx - 1) + (ny - 1) + (nx - 1) * (ny - 1) + ny)


def gather_tasks(place, copies, shards, fulls):
    nz = place.nz

    def part(k, step):
        return lambda: fulls[k]((place.z - step) % nz, 0, 0)

    rings = [
        [copies.plan(part(k, step) if step else shards[k], part(k, step), place.along_z(1)) for k in range(2)]
        for step in range(nz - 1)
    ]

    def task(step):
        spots = [lambda dy, dx, k=k: fulls[k]((place.z - 1 - step) % nz, dy, dx) for k in range(2)]
        out, *others = spread(place, copies, spots)

        def arrival():
            arrive(rings[step])
            if step < nz - 2:
                start(rings[step + 1])
            out()

        return [arrival] + others

    return lambda: start(rings[0]), [task(step) for step in range(nz - 1)]


def gather_count(nz, ny, nx):
    return (nz - 1) * (2 + spread_count(ny, nx))


def run_staggered(tasks):
    phases = [(at + n, n, phase) for n, task in enumerate(tasks) for at, phase in enumerate(task)]
    for _, _, phase in sorted(phases, key=lambda entry: entry[:2]):
        phase()


class Timetable:
    def __init__(self, per_step, steps):
        self.per_step, self.steps, self.at = per_step, steps, {}

    def add(self, task, times):
        for time, phase in zip(times, task, strict=True):
            self.at.setdefault(time, []).append(phase)

    def tick(self, slot):
        for time in range(slot, self.per_step * self.steps, self.per_step):
            if time in self.at:
                @pl.when(pl.program_id(0) == time // self.per_step)
                def _():
                    for phase in self.at[time]:
                        phase()

    def finish(self):
        for time in sorted(self.at):
            if time >= self.per_step * self.steps:
                for phase in self.at[time]:
                    phase()


class Reduction:
    def __init__(self, place, copies, grad_ref, out_ref, buffers, own_ref, own_sems):
        self.place, self.copies, self.grad, self.out = place, copies, grad_ref, out_ref
        self.own_ref, self.own_sems = own_ref, own_sems
        self.core, self.y1, self.x1, self.x2, self.y2, self.z_send, self.z_buf = buffers
        self.members, self.height, self.width = grad_ref.shape[1:]
        self.half = self.members // 2
        self.rows = self.height // (place.ny * 2 * place.nx)
        self.sums = []

    @staticmethod
    def scratch(nz, ny, nx, members, height, width):
        half, rows, bf = members // 2, height // (ny * 2 * nx), jnp.bfloat16
        band = nx * rows
        return [
            pltpu.VMEM((nz, ny, members, band, width), bf),
            pltpu.VMEM((nz, ny - 1, half, band, width), bf),
            pltpu.VMEM((nz, nx - 1, ny, half, rows, width), bf),
            pltpu.VMEM((nz, nx - 1, half, rows, width), bf),
            pltpu.VMEM((nz, ny - 1, half, rows, width), bf),
            pltpu.VMEM((nz, members, rows, width), bf),
            pltpu.VMEM((nz - 1, members, rows, width), bf),
        ]

    @staticmethod
    def count(nz, ny, nx):
        return nz * (ny + 2 * (ny - 1) + 2 * (nx - 1)) + nz - 1 + spread_count(ny, nx)

    def source(self, t, dy):
        return self.grad.at[(self.place.z + 1 + t) % self.place.nz, :, self.place.band(self.rows, dy, 1), :]

    def staged(self, t):
        block = (self.place.z + 1 + t) % self.place.nz
        return [
            pltpu.make_async_copy(self.grad.at[block, :, self.place.band(self.rows, dy), :], self.own_ref.at[t, dy], self.own_sems.at[t, dy])
            for dy in range(self.place.ny)
        ]

    def prepare(self, t):
        start(self.staged(t))

    def prepared(self, t):
        for copy in self.staged(t):
            copy.wait()

    def own(self, t, dy, m):
        return self.own_ref[t, dy, m]

    def chunk(self, t):
        place, copies, half, rows = self.place, self.copies, self.half, self.rows
        ny, nx, nz = place.ny, place.nx, place.nz
        core, x1, y1, x2, y2, f32, bf = self.core, self.x1, self.y1, self.x2, self.y2, jnp.float32, jnp.bfloat16

        def xrows(step):
            return pl.ds(pl.multiple_of((place.x + step) % nx * rows, rows), rows)

        sent = [
            copies.plan(
                lambda dy=dy: self.source(t, dy),
                lambda dy=dy: core.at[t, dy], place.other_core)
            for dy in range(ny)
        ]
        over_y = [
            copies.plan(lambda s=s: core.at[t, ny - s, 0:half], lambda s=s: y1.at[t, s - 1], place.along_y(s))
            for s in range(1, ny)
        ]
        over_x = [
            copies.plan(lambda s=s: core.at[t, :, half:, xrows(s), :], lambda s=s: x1.at[t, s - 1], place.along_x(s))
            for s in range(1, nx)
        ]
        then_x = [
            copies.plan(lambda s=s: core.at[t, 0, 0:half, xrows(s), :], lambda s=s: x2.at[t, s - 1], place.along_x(s))
            for s in range(1, nx)
        ]
        then_y = [
            copies.plan(lambda s=s: core.at[t, ny - s, half:, xrows(0), :], lambda s=s: y2.at[t, s - 1], place.along_y(s))
            for s in range(1, ny)
        ]
        along = [copies.plan(lambda: self.z_send.at[t], lambda: self.z_buf.at[t], place.along_z(1 + t))] if t < nz - 1 else []
        self.sums += along

        def first():
            start(sent)
            self.prepare(t)

        def both_cores():
            arrive(sent)
            self.prepared(t)
            for dy in range(ny):
                for m in range(self.members):
                    core[t, dy, m] = (core[t, dy, m].astype(f32) + self.own(t, dy, m).astype(f32)).astype(bf)
            start(over_y)
            start(over_x)

        def turn():
            arrive(over_y)
            for m in range(half):
                total = core[t, 0, m].astype(f32)
                for s in range(ny - 1):
                    total = total + y1[t, s, m].astype(f32)
                core[t, 0, m] = total.astype(bf)
            start(then_x)
            arrive(over_x)
            for dy in range(ny):
                for m in range(half):
                    total = core[t, dy, half + m, xrows(0), :].astype(f32)
                    for s in range(nx - 1):
                        total = total + x1[t, s, dy, m].astype(f32)
                    core[t, dy, half + m, xrows(0), :] = total.astype(bf)
            start(then_y)

        def send_on():
            arrive(then_x)
            arrive(then_y)
            for m in range(self.members):
                total = core[t, 0, m, xrows(0), :].astype(f32)
                buf, n = (x2, nx - 1) if m < half else (y2, ny - 1)
                for s in range(n):
                    total = total + buf[t, s, m % half].astype(f32)
                self.z_send[t, m] = total.astype(bf)
            start(along)

        return [first, both_cores, turn, send_on]

    def ending(self):
        place, nz = self.place, self.place.nz
        spots = [
            lambda dy, dx, lo=lo, hi=hi: self.out.at[lo:hi, place.piece(self.rows, dy, dx), :]
            for lo, hi in ((0, self.half), (self.half, self.members))
        ]
        out, *others = spread(place, self.copies, spots)

        def total():
            arrive(self.sums)
            for m in range(self.members):
                total = self.z_send[nz - 1, m].astype(jnp.float32)
                for t in range(nz - 1):
                    total = total + self.z_buf[t, m].astype(jnp.float32)
                self.out[m, place.piece(self.rows, 0, 0), :] = total.astype(jnp.bfloat16)
            out()

        return [total] + others


def small_sum(place, copies, small_ref, out_ref, s_acc, s_buf):
    nz, ny, nx = place.nz, place.ny, place.nx
    stages = ([place.other_core], [place.along_x(s) for s in range(1, nx)],
              [place.along_y(s) for s in range(1, ny)], [place.along_z(s) for s in range(1, nz)])
    firsts = [0, 1, nx, nx + ny - 1]
    sent = [
        [copies.plan(lambda k=k: s_acc.at[k], lambda n=firsts[k] + i: s_buf.at[n], partner) for i, partner in enumerate(partners)]
        for k, partners in enumerate(stages)
    ]

    def add(k):
        arrive(sent[k])
        total = s_acc[k]
        for i in range(len(sent[k])):
            total = total + s_buf[firsts[k] + i]
        return total

    def first():
        if small_ref is not None:
            s_acc[0] = small_ref[...]
        start(sent[0])

    def middle(k):
        s_acc[k + 1] = add(k)
        start(sent[k + 1])

    def last():
        out_ref[...] = add(3)

    return [first] + [functools.partial(middle, k) for k in range(3)] + [last]


def small_scratch(nz, ny, nx, shape):
    return [pltpu.VMEM((4,) + shape, jnp.float32), pltpu.VMEM((nx + ny + nz - 2,) + shape, jnp.float32)]


HS = 64
LANES = 128
EDGE = 128
TAP = 16
LOG2E = math.log2(math.e)
NT = (((1,), (1,)), ((), ()))
NN = (((1,), (0,)), ((), ()))
TN = (((0,), (0,)), ((), ()))


def dot(a, b, dims=NN):
    return lax.dot_general(a, b, dims, preferred_element_type=jnp.float32)


def spans(first, last, step):
    return [(at, min(step, last - at)) for at in range(first, last, step)]


def earlier(ref, start, size):
    if start == 0:
        rows = jnp.concatenate([jnp.zeros((TAP, LANES), jnp.float32), ref[pl.ds(0, size), :].astype(jnp.float32)], axis=0)
    else:
        rows = ref[pl.ds(start - TAP, size + TAP), :].astype(jnp.float32)
    return [pltpu.roll(rows, i, 0)[TAP:] if i else rows[TAP:] for i in range(3)]


def convolve(linear_ref, kern_ref, member, target_ref, skip, step=256):
    total = linear_ref.shape[0]
    for start, size in spans(skip, total, step):
        taps = earlier(linear_ref, start, size)
        value = sum(kern_ref[3 * member + i:3 * member + i + 1, :] * taps[i] for i in range(3))
        target_ref[pl.ds(start - skip, size), :] = value.astype(jnp.bfloat16)


def convolve_back(grad_ref, linear_ref, kern_ref, member, target_ref, sums_ref, step=256):
    total = linear_ref.shape[0]
    parts = [jnp.zeros((8, LANES), jnp.float32)] * 3
    for start, size in spans(0, total, step):
        rows = grad_ref[pl.ds(start, size + 8), :]
        linear = linear_ref[pl.ds(start, size), :].astype(jnp.float32)
        value = None
        for i in range(3):
            later = pltpu.roll(rows, size + 8 - i, 0)[:size] if i else rows[:size]
            term = kern_ref[3 * member + i:3 * member + i + 1, :] * later
            value = term if value is None else value + term
            parts[i] += jnp.sum((later * linear).reshape(size // 8, 8, LANES), axis=0)
        target_ref[pl.ds(start, size), :] = value.astype(jnp.bfloat16)
    for i in range(3):
        sums_ref[3 * member + i:3 * member + i + 1, :] = jnp.sum(parts[i], axis=0, keepdims=True)


def parts_of(rows, shards, at, size, step):
    own = (shards - 1) * rows
    pieces = []
    for hop in range(shards - 1, 0, -1):
        pieces += [(start, n, hop) for start, n in spans(own - hop * rows, own - (hop - 1) * rows, step)]
    pieces += [(start, n, 0) for start, n in spans(own, own + at, step)]
    return pieces + [(own + at, size, None)]


def column(n):
    return pl.BlockSpec((n, LANES), lambda i: (0, i))


ANY = pl.BlockSpec(memory_space=pl.ANY)
WHOLE = pl.BlockSpec((8, LANES), lambda i: (0, 0))


def backward_kernel(
    nz, ny, nx, steps, bq, kc, plan, far_ref, lq_ref, lk_ref, lv_ref, kern_ref, g_ref, o_ref, mass_ref, grad_ref, small_ref,
    gq_ref, gk_ref, gv_ref, sums_ref, up_ref, down_ref, small_out_ref,
    q_ref, k_ref, v_ref, kt_ref, dq_ref, dk_ref, dv_ref, *scratch,
):
    rows, window = q_ref.shape[0], k_ref.shape[0]
    shards = window // rows
    edge = lq_ref.shape[0] - rows
    lane = lax.broadcasted_iota(jnp.int32, (bq, LANES), 1) < HS
    scale = 1.0 / math.sqrt(HS)

    *buffers, s_acc, s_buf, sum_ref, own_ref, send_sems, recv_sems, own_sems = scratch
    place = Place(nz, ny, nx)
    copies = Copies(send_sems, recv_sems)

    @pl.when(pl.program_id(0) == 0)
    def _():
        place.meet()

    whole = Reduction(place, copies, grad_ref, sum_ref, buffers, own_ref, own_sems)
    table = Timetable(rows // bq, steps)
    chunk_plan, small_plan, ending_plan = plan
    for t, ticks in enumerate(chunk_plan):
        table.add(whole.chunk(t), ticks)
    table.add(small_sum(place, copies, small_ref, small_out_ref, s_acc, s_buf), small_plan)
    table.add(whole.ending(), ending_plan)

    convolve(lq_ref, kern_ref, 0, q_ref, edge)
    convolve(lk_ref, kern_ref, 1, k_ref, 0)
    convolve(lv_ref, kern_ref, 2, v_ref, 0)
    dk_ref[...] = jnp.zeros_like(dk_ref)
    dv_ref[...] = jnp.zeros_like(dv_ref)
    if edge:
        dq_ref[pl.ds(0, edge), :] = jnp.zeros((edge, LANES), jnp.float32)
    dq_ref[pl.ds(edge + rows, 8), :] = jnp.zeros((8, LANES), jnp.float32)
    kt_ref[...] = k_ref[...].astype(jnp.float32).T.astype(jnp.bfloat16)

    def block(at):
        query = q_ref[pl.ds(at, bq), :] * jnp.bfloat16(scale)
        grad = g_ref[pl.ds(at, bq), :]
        zero = jnp.zeros_like(query)
        queries = (jnp.where(lane, query, zero), jnp.where(lane, zero, query))
        grads = (jnp.where(lane, grad, zero), jnp.where(lane, zero, grad))
        product = (grad.astype(jnp.float32) * o_ref[pl.ds(at, bq), :].astype(jnp.float32)).T
        query_grads = [jnp.zeros((HS, bq), jnp.float32)] * 2
        deltas = [jnp.sum(product[h * HS:(h + 1) * HS], axis=0, keepdims=True) for h in range(2)]
        masses = [mass_ref[0, h:h + 1, pl.ds(at, bq)] * LOG2E for h in range(2)]
        for start, size, hop in parts_of(rows, shards, at, bq, kc):
            key = k_ref[pl.ds(start, size), :]
            value = v_ref[pl.ds(start, size), :]
            key_part = value_part = None
            for h in range(2):
                s = dot(key, queries[h], NT)
                if hop is None:
                    row = lax.broadcasted_iota(jnp.int32, (size, bq), 1)
                    col = lax.broadcasted_iota(jnp.int32, (size, bq), 0)
                    s = jnp.where(col <= row, s, -1e30)
                mass = masses[h] + far_ref[hop - 1:hop, 0:1] if hop else masses[h]
                p = jnp.exp2(s * LOG2E - mass)
                dp = dot(value, grads[h], NT)
                ds = (p * (dp - deltas[h])).astype(jnp.bfloat16)
                a = dot(p.astype(jnp.bfloat16), grads[h])
                b = dot(ds, queries[h])
                value_part = a if value_part is None else value_part + a
                key_part = b if key_part is None else key_part + b
                query_grads[h] += dot(kt_ref[h * HS:(h + 1) * HS, pl.ds(start, size)], ds)
            dk_ref[pl.ds(start, size), :] += key_part
            dv_ref[pl.ds(start, size), :] += value_part
        dq_ref[pl.ds(edge + at, bq), :] = jnp.concatenate(query_grads, axis=0).T * scale

    for slot, at in enumerate(range(0, rows, bq)):
        table.tick(slot)
        block(at)

    sums_ref[...] = jnp.zeros_like(sums_ref)
    convolve_back(dq_ref, lq_ref, kern_ref, 0, gq_ref, sums_ref)
    convolve_back(dk_ref, lk_ref, kern_ref, 1, gk_ref, sums_ref)
    convolve_back(dv_ref, lv_ref, kern_ref, 2, gv_ref, sums_ref)

    @pl.when(pl.program_id(0) == steps - 1)
    def _():
        table.finish()
        for at, size in spans(0, sum_ref.shape[1], 256):
            up_ref[:, pl.ds(at, size)] = sum_ref[0, pl.ds(at, size), :].astype(jnp.float32).T.astype(up_ref.dtype)
            down_ref[pl.ds(at, size), :] = sum_ref[1, pl.ds(at, size), :]
        copies.finish()


def attention_backward(far, late, linear_k, linear_v, kern, grads, outs, mass, ff_grad, small, ny, nx):
    rows = grads.shape[0]
    edged, width = late.shape
    window = linear_k.shape[0]
    pairs = width // LANES
    bq = min(256, rows)
    bf = jnp.bfloat16
    nz, members, height, columns = ff_grad.shape
    count = Reduction.count(nz, ny, nx) + nx + ny + nz - 2
    ticks = pairs * (rows // bq)
    gap = max(1, 5 * ticks // 32)
    chunks = [(gap * t, gap * t + 2, gap * t + 7, gap * t + 10) for t in range(nz)]
    end = max(chunks[-1][-1] + 1, ticks - 8)
    plan = (chunks, range(2, 12, 2), (end, end + 4, end + 6, end + 7))
    return pl.pallas_call(
        functools.partial(backward_kernel, nz, ny, nx, pairs, bq, 1024, plan),
        out_shape=(jax.ShapeDtypeStruct((edged, width), bf), jax.ShapeDtypeStruct((window, width), bf),
                   jax.ShapeDtypeStruct((window, width), bf), jax.ShapeDtypeStruct((16, width), jnp.float32),
                   jax.ShapeDtypeStruct((columns, height), bf), jax.ShapeDtypeStruct((height, columns), bf),
                   jax.ShapeDtypeStruct(small.shape, jnp.float32)),
        grid=(pairs,),
        in_specs=[WHOLE, column(edged), column(window), column(window), column(16), column(rows), column(rows),
                  pl.BlockSpec((1, 8, rows), lambda i: (i, 0, 0)), ANY, VMEM],
        out_specs=[column(edged), column(window), column(window), column(16), VMEM, VMEM, VMEM],
        scratch_shapes=[
            pltpu.VMEM((rows, LANES), bf), pltpu.VMEM((window, LANES), bf), pltpu.VMEM((window, LANES), bf),
            pltpu.VMEM((LANES, window), bf), pltpu.VMEM((edged + 8, LANES), jnp.float32),
            pltpu.VMEM((window + 8, LANES), jnp.float32), pltpu.VMEM((window + 8, LANES), jnp.float32),
        ] + Reduction.scratch(nz, ny, nx, members, height, columns) + small_scratch(nz, ny, nx, small.shape) + [
            pltpu.VMEM((members, height, columns), bf),
            pltpu.VMEM((nz, ny, members, nx * (height // (ny * 2 * nx)), columns), bf),
            pltpu.SemaphoreType.DMA((count,)), pltpu.SemaphoreType.DMA((count,)), pltpu.SemaphoreType.DMA((nz, ny)),
        ],
        compiler_params=pltpu.CompilerParams(collective_id=2, has_side_effects=True, vmem_limit_bytes=60 << 20),
    )(far, late, linear_k, linear_v, kern, grads, outs, mass, ff_grad, small)


def taps_of(rows, size):
    return [pltpu.roll(rows, i, 0)[TAP:TAP + size] if i else rows[TAP:TAP + size] for i in range(3)]


def front_kernel(
    nz, ny, nx, shards, bq, kc, far_ref, gain_ref, small_ref, qkv_ref, project_ref, input_ref, up_in_ref, down_ref,
    out_ref, mass_ref, small_out_ref, full_out, window_out, turned_out, lq_out, lk_out, lv_out, up_out, down_out,
    up_ref, full, window, turned, lq, lk, lv, small_all, q_ref, k_ref, v_ref, s0_ref, s1_ref, acc_ref, total_ref, peak_ref,
    send_sems, recv_sems, out_sems,
):
    rows, depth = input_ref.shape
    window_rows = window.shape[0]
    own = window_rows - rows
    edge = lq.shape[0] - rows
    members, width = 4, qkv_ref.shape[2]
    per = width // LANES
    half = members // 2
    share = depth // (ny * 2 * nx)
    units = down_ref.shape[0]
    part = units // (ny * 2 * nx)
    step_at = pl.program_id(0)
    f32, bf = jnp.float32, jnp.bfloat16
    scale = 1.0 / math.sqrt(HS)
    lane = lax.broadcasted_iota(jnp.int32, (bq, LANES), 1) < HS

    place = Place(nz, ny, nx)
    copies = Copies(send_sems, recv_sems)

    def columns(block, size=width, first=0):
        return pl.ds(pl.multiple_of(block * width + first, LANES), size)

    begin, tasks = gather_tasks(
        place, copies,
        [lambda lo=lo, hi=hi: full.at[lo:hi, place.piece(share, 0, 0), columns(place.z)] for lo, hi in ((0, half), (half, members))],
        [lambda block, dy, dx, lo=lo, hi=hi: full.at[lo:hi, place.piece(share, dy, dx), columns(block)]
         for lo, hi in ((0, half), (half, members))])
    smalls = [copies.plan(lambda: small_ref, lambda: small_all.at[place.z], place.along_z(s)) for s in range(1, nz)]

    def rows_to(hop, at, size):
        return copies.plan(
            lambda: window.at[pl.ds(own + at, size), :], lambda: window.at[pl.ds(own - hop * rows + at, size), :],
            place.along_z(hop))

    near = [rows_to(1, rows - edge, edge)] if shards > 1 else []
    distant = []
    for hop in range(1, shards):
        distant += [rows_to(hop, at, size) for at, size in spans(0, rows - (edge if hop == 1 else 0), 256)]

    def spot(ref):
        return lambda block, dy, dx: ref.at[pl.ds(pl.multiple_of(block * units, units), units), :].at[place.piece(part, dy, dx), :]

    ff_begin, ff_tasks = gather_tasks(
        place, copies, [lambda ref=ref: ref.at[place.piece(part, 0, 0), :] for ref in (up_ref, down_ref)],
        [spot(up_out), spot(down_out)])

    def local(n, source, target):
        return pltpu.make_async_copy(source, target, out_sems.at[n])

    def stores(which):
        mine = pl.ds(pl.multiple_of(place.z * units, units), units)
        return {
            "units": lambda: [local(0, up_ref, up_out.at[mine, :]), local(1, down_ref, down_out.at[mine, :])],
            "full": lambda: [local(2, full, full_out)],
            "window": lambda: [local(3, window, window_out)],
            "turned": lambda: [local(7, turned, turned_out)],
            "linear": lambda: [local(4, lq, lq_out), local(5, lk, lk_out), local(6, lv, lv_out)],
        }[which]()

    def keep_valid(hop, first, size):
        for at, n in spans(first, first + size, 256):
            at_rows = pl.ds(own - hop * rows + at, n)
            window[at_rows, :] = jnp.where(far_ref[hop - 1:hop, 0:1] > 0, jnp.zeros((n, depth), bf), window[at_rows, :])

    @pl.when(step_at == 0)
    def _():
        for at, size in spans(0, rows, 256):
            values = input_ref[at:at + size, :].astype(f32)
            factor = lax.rsqrt(jnp.mean(values * values, axis=-1, keepdims=True) + EPSILON)
            window[pl.ds(own + at, size), :] = (values * factor * gain_ref[0:1, :]).astype(bf)
        small_all[place.z] = small_ref[...]
        for m in range(3):
            full[m, :, columns(place.z)] = qkv_ref[m]
        full[3, :, columns(place.z)] = project_ref[...].astype(f32).T.astype(bf)
        place.meet()
        start(near)
        begin()
        start(smalls)
        arrive(near)
        if shards > 1:
            keep_valid(1, rows - edge, edge)

    def all_rows():
        arrive(distant)
        for hop in range(1, shards):
            keep_valid(hop, 0, rows - (edge if hop == 1 else 0))
        start(stores("window"))

    slots = per + 1
    table = Timetable(slots, 2 * nz)
    for s, (arrival, turn, cross, done) in enumerate(tasks):
        table.add([arrival, turn], (slots * s if s else 1, slots * s + (1 if s else per)))
    for s, (arrival, turn, cross, done) in enumerate(tasks):
        table.add([cross, done], (slots * (s + 1), slots * (s + 1)))
    for s in range(nz - 1):
        waiting = distant[s:s + 1] if s < nz - 2 else distant[s:]
        table.add([lambda waiting=waiting: start(waiting)], [slots * s if s else 1])
    table.add([lambda: arrive(smalls)], [slots])
    table.add([lambda: start(stores("full")), all_rows], [slots * (nz - 1), slots * nz])
    def turn_up(at, size):
        return lambda: up_ref.__setitem__((slice(at, at + size), slice(None)), up_in_ref[:, at:at + size].astype(f32).T.astype(bf))

    for n, (at, size) in enumerate(spans(0, units, 256)):
        table.add([turn_up(at, size)], [slots + n])
    table.add([lambda: start(stores("units")), ff_begin], [slots * nz - 1, slots * nz - 1])
    for s, task in enumerate(ff_tasks):
        first = slots * nz + 3 * (s + 1) - 1
        table.add(task, (first, first + 3, first + 5, first + 6))

    def turn_rows(at, size):
        return lambda: turned.__setitem__((slice(None), slice(at, at + size)), window[at:at + size, :].astype(f32).T.astype(bf))

    for n, (at, size) in enumerate(spans(0, window_rows, 256)):
        table.add([turn_rows(at, size)], [slots * nz + 1 + n % (slots * nz - 1)])

    relative = step_at % nz
    block = (place.z - relative) % nz

    def filtered(source, member, target, first, size, source_first, p):
        lanes = columns(block, LANES, p * LANES)
        for at, n in spans(first, first + size, 256):
            inside = at - source_first
            if inside == 0:
                rows_in = source[pl.ds(0, n), lanes].astype(f32)
                rows_in = jnp.concatenate([jnp.zeros((TAP, LANES), f32), rows_in], axis=0)
            else:
                rows_in = source[pl.ds(inside - TAP, n + TAP), lanes].astype(f32)
            taps = taps_of(rows_in, n)
            value = sum(small_all[block, 3 * member + i:3 * member + i + 1, p * LANES:(p + 1) * LANES] * taps[i] for i in range(3))
            target(at, n, value.astype(bf))

    def into(ref, shift=0):
        def put(at, n, value):
            ref[pl.ds(at - shift, n), :] = value
        return put

    def queries_of(at):
        query = q_ref[pl.ds(at, bq), :] * jnp.bfloat16(scale)
        zero = jnp.zeros_like(query)
        return jnp.where(lane, query, zero), jnp.where(lane, zero, query)

    def scores(queries, parts, shift):
        peaks = [{}, {}]
        for start_at, size, hop in parts:
            key = k_ref[pl.ds(start_at, size), :]
            for h, store in enumerate((s0_ref, s1_ref)):
                s = dot(queries[h], key, NT)
                if hop is None:
                    row = lax.broadcasted_iota(jnp.int32, (bq, size), 0)
                    col = lax.broadcasted_iota(jnp.int32, (bq, size), 1)
                    s = jnp.where(col <= row, s, -1e30)
                store[:, pl.ds(start_at - shift, size)] = s
                top = jnp.max(s, axis=1, keepdims=True)
                group = hop or 0
                peaks[h][group] = jnp.maximum(peaks[h][group], top) if group in peaks[h] else top
        return peaks

    def weighted(parts, shift, bases):
        sums = [None, None]
        for start_at, size, hop in parts:
            value = v_ref[pl.ds(start_at, size), :]
            wide = lax.broadcasted_iota(jnp.int32, (size, LANES), 1) < HS
            one = jnp.ones_like(value)
            values = (jnp.where(wide, value, one), jnp.where(wide, one, value))
            for h, store in enumerate((s0_ref, s1_ref)):
                p = jnp.exp2(store[:, pl.ds(start_at - shift, size)] * LOG2E - bases[h][hop or 0]).astype(bf)
                o = dot(p, values[h])
                sums[h] = o if sums[h] is None else sums[h] + o
        return jnp.where(lane, sums[0], sums[1]), pltpu.roll(jnp.where(lane, sums[1], sums[0]), HS, 1)

    def finish_rows(p, at, acc, total, peak):
        out_ref[pl.ds(at, bq), columns(block, LANES, p * LANES)] = (acc / total).astype(bf)
        mass = (peak + jnp.log(total)).T
        mass_ref[block * per + p, 0:1, pl.ds(at, bq)] = mass[0:1]
        mass_ref[block * per + p, 1:2, pl.ds(at, bq)] = mass[HS:HS + 1]

    def linear(target, member, first, last, target_first):
        for at, n in spans(first, last, 256):
            value = dot(window[pl.ds(at, n), :], full[member, :, columns(block)])
            target[pl.ds(at - target_first, n), columns(block)] = value.astype(bf)

    table.tick(0)

    @pl.when(step_at < nz)
    def _():
        linear(lq, 0, own - edge, window_rows, own - edge)
        linear(lk, 1, own - edge, window_rows, 0)
        linear(lv, 2, own - edge, window_rows, 0)

    @pl.when(step_at >= nz)
    def _():
        if shards > 1:
            linear(lk, 1, 0, own - edge, 0)
            linear(lv, 2, 0, own - edge, 0)

    for p in range(per):
        state = relative * per + p

        @pl.when(step_at < nz)
        def _():
            filtered(lq, 0, into(q_ref, own), own, rows, own - edge, p)
            filtered(lk, 1, into(k_ref), own, rows, 0, p)
            filtered(lv, 2, into(v_ref), own, rows, 0, p)
            for at in range(0, rows, bq):
                parts = [(start_at, n, 0) for start_at, n in spans(own, own + at, kc)] + [(own + at, bq, None)]
                peaks = scores(queries_of(at), parts, own)
                acc, total = weighted(parts, own, [{0: peaks[h][0] * LOG2E} for h in range(2)])
                here = pl.ds(at, bq)
                peak = jnp.where(lane, peaks[0][0], peaks[1][0])
                if shards > 1:
                    acc_ref[state, here, :] = acc
                    total_ref[state, here, :] = total
                    peak_ref[state, here, :] = peak
                else:
                    finish_rows(p, at, acc, total, peak)

        if shards > 1:
            @pl.when(step_at >= nz)
            def _():
                filtered(lq, 0, into(q_ref, own), own, rows, own - edge, p)
                filtered(lk, 1, into(k_ref), 0, own, 0, p)
                filtered(lv, 2, into(v_ref), 0, own, 0, p)
                for at in range(0, rows, bq):
                    here = pl.ds(at, bq)
                    parts = []
                    for hop in range(shards - 1, 0, -1):
                        parts += [(s, n, hop) for s, n in spans(own - hop * rows, own - (hop - 1) * rows, kc)]
                    peaks = scores(queries_of(at), parts, 0)
                    old = peak_ref[state, here, :]
                    tops, bases = [], []
                    for h in range(2):
                        top = old[:, h * HS:h * HS + 1]
                        for hop in range(1, shards):
                            top = jnp.maximum(top, peaks[h][hop] - far_ref[hop - 1:hop, 0:1])
                        tops.append(top)
                        bases.append({hop: top * LOG2E + far_ref[hop - 1:hop, 0:1] for hop in range(1, shards)})
                    acc, total = weighted(parts, 0, bases)
                    peak = jnp.where(lane, tops[0], tops[1])
                    fade = jnp.exp2((old - peak) * LOG2E)
                    finish_rows(p, at, acc_ref[state, here, :] * fade + acc, total_ref[state, here, :] * fade + total, peak)

        table.tick(p + 1)

    @pl.when(step_at == 2 * nz - 1)
    def _():
        start(stores("turned"))
        start(stores("linear"))
        small_out_ref[...] = small_all[...]
        table.finish()
        for which in ("units", "full", "window", "turned", "linear"):
            for copy in stores(which):
                copy.wait()
        copies.finish()


def front(far, gain, small, qkv, project, layer_input, up, down, nz, ny, nx, shards):
    rows, depth = layer_input.shape
    members, width = 4, qkv.shape[2]
    window_rows = shards * rows
    edge = EDGE if shards > 1 else 0
    pairs = depth // LANES
    units = down.shape[0]
    bq = min(512, rows)
    f32, bf = jnp.float32, jnp.bfloat16
    sent = sum(len(spans(0, rows - (edge if hop == 1 else 0), 256)) for hop in range(1, shards)) + (1 if shards > 1 else 0)
    count = 2 * gather_count(nz, ny, nx) + nz - 1 + sent
    store = pltpu.VMEM((bq, max(rows, window_rows - rows)), f32)
    state = pltpu.VMEM((pairs, rows, LANES), f32)
    return pl.pallas_call(
        functools.partial(front_kernel, nz, ny, nx, shards, bq, 512),
        out_shape=(
            jax.ShapeDtypeStruct((rows, depth), bf), jax.ShapeDtypeStruct((pairs, 8, rows), f32),
            jax.ShapeDtypeStruct((nz,) + small.shape, f32), jax.ShapeDtypeStruct((members, depth, depth), bf),
            jax.ShapeDtypeStruct((window_rows, depth), bf), jax.ShapeDtypeStruct((depth, window_rows), bf),
            jax.ShapeDtypeStruct((rows + edge, depth), bf),
            jax.ShapeDtypeStruct((window_rows, depth), bf), jax.ShapeDtypeStruct((window_rows, depth), bf),
            jax.ShapeDtypeStruct((nz * units, depth), bf), jax.ShapeDtypeStruct((nz * units, depth), bf),
        ),
        grid=(2 * nz,),
        in_specs=[VMEM] * 8,
        out_specs=[VMEM] * 3 + [ANY] * 8,
        scratch_shapes=[
            pltpu.VMEM((units, depth), bf), pltpu.VMEM((members, depth, depth), bf), pltpu.VMEM((window_rows, depth), bf),
            pltpu.VMEM((depth, window_rows), bf), pltpu.VMEM((rows + edge, depth), bf), pltpu.VMEM((window_rows, depth), bf),
            pltpu.VMEM((window_rows, depth), bf),
            pltpu.VMEM((nz,) + small.shape, f32),
            pltpu.VMEM((rows, LANES), bf), pltpu.VMEM((window_rows, LANES), bf), pltpu.VMEM((window_rows, LANES), bf),
            store, store, state, state, state,
            pltpu.SemaphoreType.DMA((count,)), pltpu.SemaphoreType.DMA((count,)), pltpu.SemaphoreType.DMA((8,)),
        ],
        compiler_params=pltpu.CompilerParams(collective_id=0, has_side_effects=True, vmem_limit_bytes=63 << 20),
        cost_estimate=pl.CostEstimate(flops=30 << 30, bytes_accessed=60 << 20, transcendentals=0),
    )(far, gain, small, qkv, project, layer_input, up, down)


class TailReduction(Reduction):
    def __init__(self, place, copies, lefts, rights, send_ref, out_ref, buffers, shape):
        self.place, self.copies, self.out = place, copies, out_ref
        self.core, self.y1, self.x1, self.x2, self.y2, self.z_send, self.z_buf = buffers
        self.lefts, self.rights, self.send = lefts, rights, send_ref
        self.members, self.height, self.width = shape
        self.half = self.members // 2
        self.rows = self.height // (place.ny * 2 * place.nx)
        self.sums = []

    def product(self, t, dy, m, core):
        block = (self.place.z + 1 + t) % self.place.nz
        columns = pl.ds(pl.multiple_of(block * self.width, self.width), self.width)
        left, first = self.lefts[m]
        return dot(left[self.place.band(self.rows, dy, core), first:], self.rights[m][:, columns])

    def source(self, t, dy):
        return self.send.at[t, dy]

    def prepare(self, t):
        pass

    def prepared(self, t):
        pass

    def own(self, t, dy, m):
        return self.product(t, dy, m, 0)

    def fill(self, t):
        for dy in range(self.place.ny):
            for m in range(self.members):
                self.send[t, dy, m] = self.product(t, dy, m, 1).astype(jnp.bfloat16)


def tail_kernel(
    nz, ny, nx, rows, shards, far_ref, gain_ref, sums_ref, gq_in, gk_in, gv_in, window_in, turned_in, low_turned_in,
    attended_in, weight_in, low_in, input_in, out_ref, small_out_ref, grad_out_ref, *scratch,
):
    (gq, gk, gv, window, turned, low_turned, attended, weight, low, own_input, partial, far_send, far_came, send,
     *buffers, s_acc, s_buf, load_sems, send_sems, recv_sems) = scratch
    place = Place(nz, ny, nx)
    copies = Copies(send_sems, recv_sems)
    edge = gq.shape[0] - rows
    window_rows = window.shape[0]
    f32, bf = jnp.float32, jnp.bfloat16
    loads = {}
    for n, (source, target) in enumerate((
        (gk_in, gk), (weight_in.at[1:3], weight.at[1:3]), (gv_in, gv), (window_in, window), (gq_in, gq),
        (weight_in.at[0:1], weight.at[0:1]), (turned_in, turned), (low_turned_in, low_turned), (attended_in, attended),
        (low_in, low), (input_in, own_input),
    )):
        loads[n] = pltpu.make_async_copy(source, target, load_sems.at[n])
        loads[n].start()

    step = min(256, rows)
    whole = TailReduction(
        place, copies, [(turned, window_rows - rows - edge), (turned, 0), (turned, 0), (low_turned, 0)],
        [gq, gk, gv, attended], send, out_ref, buffers, out_ref.shape)
    chunks = [whole.chunk(t) for t in range(nz)]
    ending = whole.ending()
    small = small_sum(place, copies, None, small_out_ref, s_acc, s_buf)
    backs = {
        (hop, at): copies.plan(
            lambda hop=hop, at=at: far_send.at[hop - 1, at:at + step, :], lambda hop=hop, at=at: far_came.at[hop - 1, at:at + step, :],
            place.along_z(-hop))
        for hop in range(1, shards) for at in range(0, rows, step)
    }
    place.meet()

    gains = [jnp.zeros((8, window.shape[1]), f32)]

    def normed_rows(at):
        part = dot(gk[at:at + step, :], weight[1], NT) + dot(gv[at:at + step, :], weight[2], NT)
        first = at - (window_rows - rows - edge)
        if first >= 0:
            part = part + dot(gq[first:first + step, :], weight[0], NT)
        elif first + step > 0:
            query = dot(gq[0:first + step, :], weight[0], NT)
            part = part + jnp.concatenate([jnp.zeros((-first, part.shape[1]), f32), query], axis=0)
        product = part * window[at:at + step, :].astype(f32)
        gains[0] = gains[0] + jnp.sum(product.reshape(step // 8, 8, -1), axis=0)
        return part

    for n in range(6):
        loads[n].wait()
    for hop in range(shards - 1, 0, -1):
        keep = jnp.where(far_ref[hop - 1:hop, 0:1] > 0, 0.0, 1.0)
        for at in range(0, rows, step):
            part = normed_rows(window_rows - (hop + 1) * rows + at) * keep
            far_send[hop - 1, at:at + step, :] = part.astype(bf)
            backs[hop, at].start()

    def own_rows(at):
        partial[at:at + step, :] = normed_rows(window_rows - rows + at).astype(bf)

    def begin(t):
        whole.fill(t)
        chunks[t][0]()

    for n in range(6, 9):
        loads[n].wait()
    owned = list(range(0, rows, step))
    begin(0)
    for t in range(nz + 2):
        if t + 1 < nz:
            begin(t + 1)
        if t < nz:
            chunks[t][1]()
        if owned:
            own_rows(owned.pop(0))
        if 0 <= t - 1 < nz:
            chunks[t - 1][2]()
        if 0 <= t - 2 < nz:
            chunks[t - 2][3]()
    while owned:
        own_rows(owned.pop(0))
    s_acc[0] = sums_ref[...]
    s_acc[0, 9:10, :] = jnp.sum(gains[0], axis=0, keepdims=True)
    small[0]()
    ending[0]()
    small[1]()
    ending[1]()
    small[2]()
    ending[2]()
    small[3]()
    loads[9].wait()
    loads[10].wait()
    for copy in backs.values():
        copy.wait_recv()
    gain = gain_ref[0:1, :]
    for at in range(0, rows, step):
        values = own_input[at:at + step, :].astype(f32)
        upstream = partial[at:at + step, :].astype(f32)
        for hop in range(1, shards):
            upstream = upstream + far_came[hop - 1, at:at + step, :].astype(f32)
        factor = lax.rsqrt(jnp.mean(values * values, axis=-1, keepdims=True) + EPSILON)
        unit = values * factor
        scaled = gain * upstream
        back = factor * (scaled - unit * jnp.mean(scaled * unit, axis=-1, keepdims=True))
        grad_out_ref[at:at + step, :] = (low[at:at + step, :].astype(f32) + back).astype(bf)
    ending[3]()
    small[4]()
    copies.finish()


def tail(far, gain, sums, grads, window, turned, low_turned, attended, weight, low, own_input, rows, nz, ny, nx):
    grad_q, grad_k, grad_v = grads
    window_rows, depth = window.shape
    shards = window_rows // rows
    width = depth // nz
    members, bf = 4, jnp.bfloat16
    band = nx * (depth // (ny * 2 * nx))
    step = min(256, rows)
    count = Reduction.count(nz, ny, nx) + nx + ny + nz - 2 + (shards - 1) * (rows // step)
    buffers = [pltpu.VMEM(t.shape, bf) for t in (grad_q, grad_k, grad_v, window, turned, low_turned, attended)]
    hops = max(1, shards - 1)
    return pl.pallas_call(
        functools.partial(tail_kernel, nz, ny, nx, rows, shards),
        out_shape=(jax.ShapeDtypeStruct((members, depth, width), bf), jax.ShapeDtypeStruct(sums.shape, jnp.float32),
                   jax.ShapeDtypeStruct((rows, depth), bf)),
        in_specs=[VMEM, VMEM, VMEM] + [ANY] * 10,
        out_specs=(VMEM, VMEM, VMEM),
        scratch_shapes=buffers + [
            pltpu.VMEM((3, depth, depth), bf), pltpu.VMEM((rows, depth), bf), pltpu.VMEM((rows, depth), bf),
            pltpu.VMEM((rows, depth), bf), pltpu.VMEM((hops, rows, depth), bf), pltpu.VMEM((hops, rows, depth), bf),
            pltpu.VMEM((nz, ny, members, band, width), bf),
        ] + Reduction.scratch(nz, ny, nx, members, depth, width) + small_scratch(nz, ny, nx, sums.shape) + [
            pltpu.SemaphoreType.DMA((11,)), pltpu.SemaphoreType.DMA((count,)), pltpu.SemaphoreType.DMA((count,)),
        ],
        compiler_params=pltpu.CompilerParams(collective_id=3, has_side_effects=True, vmem_limit_bytes=62 << 20),
        cost_estimate=pl.CostEstimate(flops=24 << 30, bytes_accessed=60 << 20, transcendentals=0),
    )(far, gain, sums, grad_q, grad_k, grad_v, window, turned, low_turned, attended, weight, low, own_input)


def rows_norm(values):
    return lax.rsqrt(jnp.mean(values * values, axis=-1, keepdims=True) + EPSILON)


def turned(values):
    return values.astype(jnp.float32).T.astype(jnp.bfloat16)


def fold(values):
    return jnp.sum(values.reshape(values.shape[0] // 8, 8, values.shape[1]), axis=0)


def middle_kernel(
    steps, step, attended_ref, input_ref, grad_ref, full_ref, out_bias_ref, gain_ref, down_bias_ref, up_ref, down_ref, bias_ref,
    weights_ref, out_ref, low_ref, low_t_ref, attended_grad_ref, sums_ref,
    hidden, normed, normed_t, grad_t, normed_grad, total, project_ref, load_sem,
):
    rows, depth = input_ref.shape
    f32, bf = jnp.float32, jnp.bfloat16
    step_at = pl.program_id(0)
    pieces = spans(0, rows, 256)

    @pl.when(step_at == 0)
    def _():
        load = pltpu.make_async_copy(full_ref.at[3], project_ref, load_sem)
        load.start()
        for at, size in pieces:
            grad_t[:, pl.ds(at, size)] = turned(grad_ref[pl.ds(at, size), :])
        load.wait()
        for at, size in pieces:
            here = pl.ds(at, size)
            state = input_ref[here, :].astype(f32) + dot(attended_ref[here, :], project_ref[...], NT) + out_bias_ref[0:1, :]
            hidden[here, :] = state
            value = state * rows_norm(state) * gain_ref[0:1, :]
            normed[here, :] = value.astype(bf)
            normed_t[:, here] = value.T.astype(bf)
        normed_grad[...] = jnp.zeros_like(normed_grad)
        total[...] = jnp.zeros_like(total)
        sums_ref[...] = jnp.zeros_like(sums_ref)

    bias = jnp.broadcast_to(bias_ref[0], (LANES, step)).T[:, 0:1]
    gate = jnp.maximum(dot(up_ref[...], normed_t[...]) + bias, 0.0)
    activation = (gate * gate).astype(bf)
    gate_grad = (2.0 * gate * dot(down_ref[...], grad_t[...])).astype(bf)
    weights_ref[0, 0] = dot(gate_grad, normed[...]).astype(bf)
    weights_ref[0, 1] = dot(activation, grad_ref[...]).astype(bf)
    column = jnp.sum(gate_grad.astype(f32), axis=1, keepdims=True)
    first = step_at * step
    sums_ref[pl.ds(3 + first // depth, 1), pl.ds(pl.multiple_of(first % depth, step), step)] = (
        jnp.broadcast_to(column, (step, LANES)).T[0:1, :])
    normed_grad[...] += dot(gate_grad, up_ref[...], TN)
    total[...] += dot(activation, down_ref[...], TN)

    @pl.when(step_at == steps - 1)
    def _():
        parts = [jnp.zeros((8, depth), f32)] * 3
        gain = gain_ref[0:1, :]
        for at, size in pieces:
            here = pl.ds(at, size)
            state = hidden[here, :]
            cotangent = grad_ref[here, :].astype(f32)
            upstream = normed_grad[here, :]
            factor = rows_norm(state)
            unit = state * factor
            scaled = gain * upstream
            back = factor * (scaled - unit * jnp.mean(scaled * unit, axis=-1, keepdims=True))
            low = (cotangent + back).astype(bf)
            low_ref[here, :] = low
            low_t_ref[:, here] = turned(low)
            attended_grad_ref[here, :] = dot(low, project_ref[...]).astype(bf)
            out_ref[here, :] = (state + total[here, :] + down_bias_ref[0:1, :]).astype(bf)
            for k, value in enumerate((upstream * unit, low.astype(f32), cotangent)):
                parts[k] = parts[k] + fold(value)
        for k in range(3):
            sums_ref[k:k + 1, :] = jnp.sum(parts[k], axis=0, keepdims=True)


def middle(attended, layer_input, grad, full, out_bias, gain, down_bias, up_rows, down_rows, bias, nz):
    rows, depth = layer_input.shape
    units = up_rows.shape[0] // nz
    step = min(512, units)
    per = units // step
    steps = nz * per
    block = pl.BlockSpec((step, depth), lambda i: (i, 0))
    f32, bf = jnp.float32, jnp.bfloat16
    both = jax.ShapeDtypeStruct((rows, depth), bf)
    height = 3 + nz * units // depth
    return pl.pallas_call(
        functools.partial(middle_kernel, steps, step),
        out_shape=(jax.ShapeDtypeStruct((nz, 2, units, depth), bf), both, both, jax.ShapeDtypeStruct((depth, rows), bf), both,
                   jax.ShapeDtypeStruct((height + -height % 8, depth), f32)),
        grid=(steps,),
        in_specs=[VMEM] * 3 + [ANY] + [VMEM] * 3 + [block, block, pl.BlockSpec((1, 1, step), lambda i: (i, 0, 0))],
        out_specs=[pl.BlockSpec((1, 2, step, depth), lambda i: (i // per, 0, i % per, 0))] + [VMEM] * 5,
        scratch_shapes=[
            pltpu.VMEM((rows, depth), f32), pltpu.VMEM((rows, depth), bf), pltpu.VMEM((depth, rows), bf),
            pltpu.VMEM((depth, rows), bf), pltpu.VMEM((rows, depth), f32), pltpu.VMEM((rows, depth), f32),
            pltpu.VMEM((depth, depth), bf), pltpu.SemaphoreType.DMA,
        ],
        compiler_params=pltpu.CompilerParams(vmem_limit_bytes=62 << 20),
        cost_estimate=pl.CostEstimate(flops=12 * rows * depth * nz * units, bytes_accessed=60 << 20, transcendentals=0),
    )(attended, layer_input, grad, full, out_bias[None], gain[None], down_bias[None], up_rows, down_rows,
      bias.reshape(steps, 1, step))


def on_device(
    layer_input, lengths, norm1_gain, qkv_weight, kernels, out_weight, out_bias,
    norm2_gain, up_weight, up_bias, down_weight, down_bias, out_grad,
):
    rows = layer_input.shape[1]
    nz, nb, nx = lax.axis_size("head"), lax.axis_size("batch"), lax.axis_size("dp")
    ny = nb // 2
    shards = max(1, LONG // rows)
    place = lax.axis_index("head")
    width = qkv_weight.shape[2]
    hidden_units = up_weight.shape[1]

    first_row = place * rows
    ends = jnp.cumsum(lengths[0])
    begins = jnp.max(jnp.where(ends <= first_row, ends, 0))
    before = ((first_row - begins) // rows).astype(jnp.int32)

    cotangent = out_grad[0]
    hops = jnp.arange(1, 9)[:, None]
    far = jnp.broadcast_to(jnp.where(before >= hops, 0.0, 1e30), (8, LANES)).astype(jnp.float32)
    small = jnp.concatenate([kernels.reshape(9, width), up_bias.reshape(-1, width)], axis=0)
    small = jnp.pad(small, ((0, -small.shape[0] % 8), (0, 0)))
    attended, mass, small, full, window, turned, linear_q, linear_k, linear_v, up_rows, down_rows = front(
        far, norm1_gain[None], small, qkv_weight, out_weight, layer_input[0], up_weight, down_weight, nz, ny, nx, shards)
    kern = jnp.pad(small[:, :9].transpose(1, 0, 2).reshape(9, -1), ((0, 7), (0, 0)))
    up_bias_all = small[:, 9:9 + hidden_units // width].reshape(-1)
    ff_grad, layer_output, hidden_low, low_turned, attended_grad, early = middle(
        attended, layer_input[0], cotangent, full, out_bias, norm2_gain, down_bias, up_rows, down_rows, up_bias_all, nz)
    grad_q, grad_k, grad_v, kernel_sums, up_sum, down_sum, early = attention_backward(
        far, linear_q, linear_k, linear_v, kern, attended_grad, attended, mass, ff_grad, early, ny, nx)
    qkvo_sum, totals, layer_grad = tail(
        far, norm1_gain[None], kernel_sums, (grad_q, grad_k, grad_v), window, turned, low_turned, attended, full,
        hidden_low, layer_input[0], rows, nz, ny, nx)

    width_all = norm1_gain.shape[0]
    early = early.reshape(-1)
    up_bias_grad = lax.dynamic_slice_in_dim(early[3 * width_all:], place * hidden_units, hidden_units, 0)
    kernels_grad = lax.dynamic_slice_in_dim(totals[:9].reshape(3, 3, -1), place * width, width, 2)
    f32 = jnp.float32
    return (
        layer_output[None], layer_grad[None], totals[9] / norm1_gain, qkvo_sum[:3].astype(f32), kernels_grad,
        qkvo_sum[3].T.astype(f32), early[width_all:2 * width_all], early[:width_all], up_sum.astype(f32),
        up_bias_grad, down_sum.astype(f32), early[2 * width_all:3 * width_all],
    )


def solution(mesh):
    rows = P(("batch", "dp"), "head", None)
    return jax.shard_map(
        on_device,
        mesh=mesh,
        in_specs=(
            rows, P(("batch", "dp"), None), P(), P(None, None, "head"), P(None, None, "head"), P("head", None), P(),
            P(), P(None, "head"), P("head"), P("head", None), P(), rows,
        ),
        out_specs=(
            rows, rows, P(), P(None, None, "head"), P(None, None, "head"), P("head", None),
            P(), P(), P(None, "head"), P("head"), P("head", None), P(),
        ),
        check_vma=False,
    )
```
